32 devices in a mesh: band: 4 (over x, core), crop: 8 (over z, y).
Axes of the slice: x: 2, y: 2, z: 4, core: 2. Of those that a mesh axis runs over, the one named last changes fastest.
Arguments:
- patches: bfloat16 [8, 1776, 768], P('crop', 'band'), may hold values from -6 to 6
- specials: bfloat16 [8, 5, 768], P('crop'), may hold values from -6 to 6
- patch_mask: int32 [8, 1776], P('crop', 'band'), may hold values from 0 to 1, as said below
- band_rows: int32 [4], replicated, may hold values from 1 to 12, as said below
- mask_token: float32 [768], replicated, may hold values from -5 to 5
- first_gain: float32 [768], replicated, may hold values from 0.5 to 1.5
- first_shift: float32 [768], replicated, may hold values from -3 to 3
- joint_weight: bfloat16 [768, 2304], replicated, may hold values from -0.21875 to 0.21875
- query_bias: float32 [768], replicated, may hold values from -3 to 3
- value_bias: float32 [768], replicated, may hold values from -3 to 3
- out_weight: bfloat16 [768, 768], replicated, may hold values from -4 to 4
- out_bias: float32 [768], replicated, may hold values from -3 to 3
- first_scale: float32 [768], replicated, may hold values from 0.25 to 1
- second_gain: float32 [768], replicated, may hold values from 0.5 to 1.5
- second_shift: float32 [768], replicated, may hold values from -3 to 3
- up_weight: bfloat16 [768, 3072], replicated, may hold values from -0.21875 to 0.21875
- up_bias: float32 [3072], replicated, may hold values from -3 to 3
- down_weight: bfloat16 [3072, 768], replicated, may hold values from -0.109375 to 0.109375
- down_bias: float32 [768], replicated, may hold values from -3 to 3
- second_scale: float32 [768], replicated, may hold values from 0.25 to 1
- cot_patches: bfloat16 [8, 1776, 768], P('crop', 'band'), may hold values from -6 to 6
- cot_specials: bfloat16 [8, 5, 768], P('crop'), may hold values from -6 to 6
Outputs:
- out_patches: bfloat16 [8, 1776, 768], P('crop', 'band')
- out_specials: bfloat16 [8, 5, 768], P('crop')
- grad_patches: bfloat16 [8, 1776, 768], P('crop', 'band')
- grad_specials: bfloat16 [8, 5, 768], P('crop')
- mask_token_grad: float32 [768], P('crop')
- first_gain_grad: float32 [768], P('crop')
- first_shift_grad: float32 [768], P('crop')
- joint_weight_grad: float32 [768, 2304], P('crop')
- query_bias_grad: float32 [768], P('crop')
- value_bias_grad: float32 [768], P('crop')
- out_weight_grad: float32 [768, 768], P('crop')
- out_bias_grad: float32 [768], P('crop')
- first_scale_grad: float32 [768], P('crop')
- second_gain_grad: float32 [768], P('crop')
- second_shift_grad: float32 [768], P('crop')
- up_weight_grad: float32 [768, 3072], P('crop')
- up_bias_grad: float32 [3072], P('crop')
- down_weight_grad: float32 [3072, 768], P('crop')
- down_bias_grad: float32 [768], P('crop')
- second_scale_grad: float32 [768], P('crop')
The draws below stay inside these ranges and needn't reach their ends.
Inputs may be any that keep to these rules, and one draw needn't show every extreme that they name: `band_rows`: the bands' rows add up to 37, and one band holds exactly 12. `patch_mask`: masked patches form rectangular blocks.
All inputs are finite; a program needn't handle non-finite values.
Results may differ from the reference program's by a relative error of at most 0.028.
Values may be sent and summed in bfloat16 or wider, within the bound.
A program may use at most 192 MiB of HBM per device.

```python
import math
import jax
import jax.numpy as jnp
from jax import lax

D = 768
HEADS = 12
HEAD = 64
FF = 3072
GRID = 37
SPECIAL = 5
ROWS_MAX = 12
SLOTS = 444
CROPS = 8
N_BAND = 4


def draw_band_rows(key, part):
    key = jax.random.fold_in(key, 11)
    keys = jax.random.split(key, 4)
    others = N_BAND - 1
    extra = GRID - ROWS_MAX - others
    chosen = jax.random.randint(keys[0], (), 0, N_BAND)
    order = jax.random.permutation(keys[1], others)
    rest = (extra // others + (order < extra % others).astype(jnp.int32)).astype(jnp.int32)
    pairing = jax.random.permutation(keys[2], others)
    giver = pairing[0]
    taker = pairing[1 % others]
    room = jnp.minimum(rest[giver], ROWS_MAX - 2 - rest[taker])
    moved = jax.random.randint(keys[3], (), 0, room + 1)
    rest = rest.at[giver].add(-moved)
    rest = rest.at[taker].add(moved)
    positions = jnp.arange(N_BAND, dtype=jnp.int32)
    other_index = jnp.clip(positions - (positions > chosen).astype(jnp.int32), 0, others - 1)
    return jnp.where(positions == chosen, ROWS_MAX, 1 + rest[other_index]).astype(jnp.int32)


def draw_patch_mask(key, part):
    key = jax.random.fold_in(key, 23)
    height = N_BAND * ROWS_MAX
    keys = jax.random.split(key, 4)
    top = jax.random.randint(keys[0], (CROPS, 4), 0, height)
    left = jax.random.randint(keys[1], (CROPS, 4), 0, GRID)
    tall = jax.random.randint(keys[2], (CROPS, 4), 1, height // 2 + 2)
    broad = jax.random.randint(keys[3], (CROPS, 4), 1, GRID // 2 + 2)
    slot_ids = jnp.arange(N_BAND * SLOTS, dtype=jnp.int32)
    row_ids = slot_ids // GRID
    column_ids = slot_ids % GRID
    inside = (row_ids[None, None, :] >= top[..., None]) & (row_ids[None, None, :] < (top + tall)[..., None]) & (column_ids[None, None, :] >= left[..., None]) & (column_ids[None, None, :] < (left + broad)[..., None])
    return jnp.any(inside, axis=1).astype(jnp.int32)


def levels(rng, extent, cuts, smallest, high):
    level = 1.0
    for dim, parts in cuts:
        draws = jax.random.uniform(jax.random.fold_in(jax.random.fold_in(rng, 6), dim), (parts,), jnp.float32, smallest / len(cuts), high / len(cuts))
        level = level * jnp.repeat(jnp.exp(draws), extent[dim] // parts).reshape((-1,) + (1,) * (len(extent) - 1 - dim))
    return level


def gaussian(rng, shape, scale, most, pieces=(), kind=jnp.bfloat16):
    values = scale * jax.random.normal(rng, shape, jnp.float32)
    if pieces:
        values = values * levels(rng, shape, pieces, -0.22, 0.18)
    return jnp.clip(values, -most, most).astype(kind)


def setup_inputs(seed: int = 0) -> dict:
    seeds = jax.random.split(jax.random.key(seed), 23)
    patches = gaussian(seeds[0], (CROPS, N_BAND * SLOTS, D), 1.0, 6.0, ((0, 8), (1, 4)))
    specials = gaussian(seeds[1], (CROPS, SPECIAL, D), 1.0, 6.0, ((0, 8),))
    patch_mask = draw_patch_mask(jax.random.fold_in(seeds[22], 71), 0)
    band_rows = draw_band_rows(jax.random.fold_in(seeds[22], 71), 0)
    mask_token = gaussian(seeds[4], (D,), 1.0, 5.0, (), jnp.float32)
    first_gain = jnp.clip(1.0 + 0.1 * jax.random.normal(seeds[5], (D,), jnp.float32), 0.5, 1.5)
    first_shift = gaussian(seeds[6], (D,), 0.5, 3.0, (), jnp.float32)
    joint_weight = gaussian(seeds[7], (D, 3 * D), D ** -0.5, 0.21875)
    query_bias = gaussian(seeds[8], (D,), 0.5, 3.0, (), jnp.float32)
    value_bias = gaussian(seeds[9], (D,), 0.5, 3.0, (), jnp.float32)
    out_weight = gaussian(seeds[10], (D, D), 2 ** -0.5, 4.0)
    out_bias = gaussian(seeds[11], (D,), 0.3, 3.0, (), jnp.float32)
    first_scale = jnp.clip(jnp.exp(jax.random.uniform(seeds[12], (D,), jnp.float32, math.log(0.25), math.log(1.0))), 0.25, 1.0)
    second_gain = jnp.clip(1.0 + 0.1 * jax.random.normal(seeds[13], (D,), jnp.float32), 0.5, 1.5)
    second_shift = gaussian(seeds[14], (D,), 0.5, 3.0, (), jnp.float32)
    up_weight = gaussian(seeds[15], (D, FF), D ** -0.5, 0.21875)
    up_bias = gaussian(seeds[16], (FF,), 0.5, 3.0, (), jnp.float32)
    down_weight = gaussian(seeds[17], (FF, D), FF ** -0.5, 0.109375)
    down_bias = gaussian(seeds[18], (D,), 0.3, 3.0, (), jnp.float32)
    second_scale = jnp.clip(jnp.exp(jax.random.uniform(seeds[19], (D,), jnp.float32, math.log(0.25), math.log(1.0))), 0.25, 1.0)
    cot_patches = gaussian(seeds[20], (CROPS, N_BAND * SLOTS, D), 1.0, 6.0, ((0, 8), (1, 4)))
    cot_specials = gaussian(seeds[21], (CROPS, SPECIAL, D), 1.0, 6.0, ((0, 8),))
    return {"patches": patches, "specials": specials, "patch_mask": patch_mask, "band_rows": band_rows, "mask_token": mask_token, "first_gain": first_gain, "first_shift": first_shift, "joint_weight": joint_weight, "query_bias": query_bias, "value_bias": value_bias, "out_weight": out_weight, "out_bias": out_bias, "first_scale": first_scale, "second_gain": second_gain, "second_shift": second_shift, "up_weight": up_weight, "up_bias": up_bias, "down_weight": down_weight, "down_bias": down_bias, "second_scale": second_scale, "cot_patches": cot_patches, "cot_specials": cot_specials}


@jax.custom_vjp
def low(v):
    return lax.optimization_barrier(v.astype(jnp.bfloat16)).astype(jnp.float32)

@jax.custom_vjp
def low_back(v):
    return v

def low_keep(v):
    return (low(v), None)

def low_pass(kept, grad):
    return (grad,)

def back_keep(v):
    return (v, None)

def back_low(kept, grad):
    return (low(grad),)
low.defvjp(low_keep, low_pass)
low_back.defvjp(back_keep, back_low)

def standardize(rows):
    centred = rows - lax.optimization_barrier(jnp.mean(rows, axis=-1, keepdims=True))
    spread = lax.optimization_barrier(jnp.mean(centred * centred, axis=-1, keepdims=True))
    return centred * lax.rsqrt(spread + 1e-06)

def crop_layer(params, patch_rows, special_rows, masked, validity):
    mask_token, first_gain, first_shift, joint_weight, query_bias, value_bias, out_weight, out_bias, first_scale, second_gain, second_shift, up_weight, up_bias, down_weight, down_bias, second_scale = params
    highest = lax.Precision.HIGHEST
    filled = jnp.where(masked[:, None] > 0, mask_token[None, :], patch_rows)
    tokens = jnp.concatenate([special_rows, filled], axis=0)
    row_count = tokens.shape[0]
    key_valid = jnp.concatenate([jnp.ones((SPECIAL,), jnp.float32), validity])
    first = low(standardize(tokens) * first_gain + first_shift)
    joint = jnp.dot(first, joint_weight, precision=highest)
    queries = low(low_back(joint[:, :D] + query_bias)).reshape(row_count, HEADS, HEAD)
    keys = low(low_back(joint[:, D:2 * D])).reshape(row_count, HEADS, HEAD)
    values = low(low_back(joint[:, 2 * D:] + value_bias)).reshape(row_count, HEADS, HEAD)
    scores = low_back(jnp.einsum('qhd,khd->hqk', queries, keys, precision=highest) * HEAD ** (-0.5))
    weights = jnp.exp(scores) * key_valid
    totals = lax.optimization_barrier(jnp.sum(weights, axis=-1))
    summed = low_back(jnp.einsum('hqk,khd->qhd', low(weights), values, precision=highest))
    attended = low((summed / jnp.transpose(totals)[:, :, None]).reshape(row_count, D))
    branch = low_back(jnp.dot(attended, out_weight, precision=highest) + out_bias)
    middle = tokens + first_scale * branch
    second = low(standardize(middle) * second_gain + second_shift)
    hidden = low_back(jnp.dot(second, up_weight, precision=highest) + up_bias)
    active = low(jax.nn.gelu(hidden, approximate=False))
    branch_two = low_back(jnp.dot(active, down_weight, precision=highest) + down_bias)
    return middle + second_scale * branch_two

def reference(patches, specials, patch_mask, band_rows, mask_token, first_gain, first_shift, joint_weight, query_bias, value_bias, out_weight, out_bias, first_scale, second_gain, second_shift, up_weight, up_bias, down_weight, down_bias, second_scale, cot_patches, cot_specials):
    slot_ids = jnp.arange(N_BAND * SLOTS, dtype=jnp.int32)
    owners = (slot_ids // SLOTS).astype(jnp.int32)
    validity = (slot_ids % SLOTS < band_rows[owners] * GRID).astype(jnp.float32)
    params = tuple((p.astype(jnp.float32) for p in (mask_token, first_gain, first_shift, joint_weight, query_bias, value_bias, out_weight, out_bias, first_scale, second_gain, second_shift, up_weight, up_bias, down_weight, down_bias, second_scale)))
    zeros = tuple((jnp.zeros_like(p) for p in params))

    def one_crop(running, inputs):
        patch_rows, special_rows, masked, cot_patch, cot_special = inputs

        def forward(weights, rows, heads_rows):
            return crop_layer(weights, rows, heads_rows, masked, validity)
        output, pull = jax.vjp(forward, params, patch_rows.astype(jnp.float32), special_rows.astype(jnp.float32))
        cotangent = jnp.concatenate([cot_special.astype(jnp.float32), cot_patch.astype(jnp.float32) * validity[:, None]], axis=0)
        weight_grads, patch_grad, special_grad = pull(cotangent)
        running = tuple((a + b for a, b in zip(running, weight_grads)))
        return (running, ((output[SPECIAL:] * validity[:, None]).astype(jnp.bfloat16), output[:SPECIAL].astype(jnp.bfloat16), patch_grad.astype(jnp.bfloat16), special_grad.astype(jnp.bfloat16)))
    totals, results = lax.scan(one_crop, zeros, (patches, specials, patch_mask, cot_patches, cot_specials))
    return (results[0], results[1], results[2], results[3], totals[0], totals[1], totals[2], totals[3], totals[4], totals[5], totals[6], totals[7], totals[8], totals[9], totals[10], totals[11], totals[12], totals[13], totals[14], totals[15])
```

```python
from functools import partial

import jax
import jax.numpy as jnp
from jax import lax
from jax.experimental import pallas as pl
from jax.experimental.pallas import tpu as pltpu
from jax.sharding import PartitionSpec as P

HEAD = 64
GRID = 37
PAIR = 2 * HEAD
BANDS = 4
F32 = jnp.float32
BF16 = jnp.bfloat16
VMEM_LIMIT = 56 << 20


def round_up(value, unit):
    return (value + unit - 1) // unit * unit


def params(semantics=None):
    return pltpu.CompilerParams(vmem_limit_bytes=VMEM_LIMIT)


def dot(a, b):
    return jnp.dot(a, b, preferred_element_type=F32)


def dot_nt(a, b):
    return lax.dot_general(a, b, (((1,), (1,)), ((), ())), preferred_element_type=F32)


def dot_tn(a, b):
    return lax.dot_general(a, b, (((0,), (0,)), ((), ())), preferred_element_type=F32)


def normalize(rows):
    centred = rows - jnp.mean(rows, axis=-1, keepdims=True)
    spread = jnp.mean(centred * centred, axis=-1, keepdims=True)
    scale = lax.rsqrt(spread + 1e-06)
    return centred * scale, scale


def normalize_back(grad, hat, scale):
    return scale * (
        grad
        - jnp.mean(grad, axis=-1, keepdims=True)
        - hat * jnp.mean(grad * hat, axis=-1, keepdims=True)
    )


def column_sum(rows):
    return jnp.sum(rows, axis=0, keepdims=True)


def whole(shape):
    return pl.BlockSpec(shape, lambda *_: (0,) * len(shape))


SMEM = pl.BlockSpec(memory_space=pltpu.SMEM)


def own_special(specials, band, slot):
    row = jnp.zeros((1, specials.shape[1]), F32)
    for special in range(specials.shape[0]):
        if special // BANDS == slot:
            row = row + jnp.where(band == special % BANDS, specials[special : special + 1], 0.0)
    return row


def place_rows(ref, patch_rows, specials, band):
    slots = patch_rows.shape[0]
    rows = ref.shape[0]
    ref[0:slots, :] = patch_rows
    extra = [own_special(specials, band, slot) for slot in range(rows - slots)]
    ref[slots:rows, :] = jnp.concatenate(extra, axis=0)


def counted_rows(info_ref, relative, rows, slots, width):
    index = lax.broadcasted_iota(jnp.int32, (rows, width), 0)
    used = index < info_ref[relative]
    special = (index >= slots) & (index < slots + info_ref[BANDS + relative])
    return used | special


def stack_pair(rows):
    lane = lax.broadcasted_iota(jnp.int32, rows.shape, 1)
    zero = jnp.zeros_like(rows)
    return jnp.concatenate(
        [jnp.where(lane < HEAD, rows, zero), jnp.where(lane >= HEAD, rows, zero)], axis=0
    )


def unstack_pair(rows):
    half = rows.shape[0] // 2
    lane = lax.broadcasted_iota(jnp.int32, (half, rows.shape[1]), 1)
    return jnp.where(lane < HEAD, rows[:half], rows[half:])


def first_kernel(info, mask, patches, specials, token, gain, shift, tokens, first):
    band = info[2 * BANDS]
    filled = jnp.where(mask[...] > 0, token[...], patches[...].astype(F32))
    place_rows(tokens, filled, specials[...].astype(F32), band)
    hat, _ = normalize(tokens[...])
    first[...] = (hat * gain[...] + shift[...]).astype(BF16)


def project_kernel(slots, info, first, weight, query_bias, value_bias, queries, keys, values):
    relative = pl.program_id(0)
    rows, width = queries.shape
    counted = counted_rows(info, relative, rows, slots, width)
    low = first[...]

    @pl.when(relative == 0)
    def _():
        queries[...] = (dot(low, weight[:, :width]) + query_bias[...]).astype(BF16)

    keys[...] = jnp.where(counted, dot(low, weight[:, width : 2 * width]), 0.0).astype(BF16)
    values[...] = jnp.where(
        counted, dot(low, weight[:, 2 * width :]) + value_bias[...], 0.0
    ).astype(BF16)


def attend_kernel(slots, info, queries, keys, values, attended, totals, weights):
    rows = queries.shape[0]
    factor = HEAD ** (-0.5)
    stacked = stack_pair((queries[...].astype(F32) * factor).astype(BF16))
    scores = dot_nt(stacked, keys[...])
    low = jnp.exp(scores).astype(BF16)
    weights[0] = low
    ones = jnp.concatenate(
        [
            counted_rows(info, r, rows, slots, PAIR).astype(F32).astype(BF16)
            for r in range(BANDS)
        ],
        axis=0,
    )
    summed = dot(low, jnp.concatenate([values[...], ones], axis=1))
    total = unstack_pair(summed[:, PAIR:])
    attended[...] = unstack_pair(summed[:, :PAIR]) / total
    totals[...] = total


def middle_kernel(
    slots,
    info,
    attended,
    tokens,
    weight,
    bias,
    first_scale,
    gain,
    shift,
    second_scale,
    cot_patches,
    cot_specials,
    branch,
    middle,
    second,
    incoming,
    down_in,
    down_bias_grad,
):
    rows = tokens.shape[0]
    band = info[2 * BANDS]
    side = dot(attended[...].astype(BF16), weight[...]) + bias[...]
    branch[...] = side
    mid = tokens[...] + first_scale[...] * side
    middle[...] = mid
    hat, _ = normalize(mid)
    second[...] = (hat * gain[...] + shift[...]).astype(BF16)
    counted = counted_rows(info, 0, slots, slots, tokens.shape[1])
    given = jnp.where(counted, cot_patches[...].astype(F32), 0.0)
    place_rows(incoming, given, cot_specials[...].astype(F32), band)
    low = (incoming[...] * second_scale[...]).astype(BF16)
    down_in[...] = low
    down_bias_grad[...] = column_sum(low.astype(F32))


def gelu_and_slope(x):
    phi = 0.5 + 0.5 * lax.erf(x * 0.7071067811865476)
    density = jnp.exp(-0.5 * x * x) * 0.3989422804014327
    return x * phi, phi + x * density


def mlp_kernel(
    second, down_in, up, up_bias, down, branch_two, second_grad, up_grad, up_bias_grad, down_grad
):
    step = pl.program_id(0)
    low = second[...]
    grad = down_in[...]
    hidden = dot(low, up[...]) + up_bias[...]
    active, slope = gelu_and_slope(hidden)
    active = active.astype(BF16)
    hidden_in = (slope * dot_nt(grad, down[...])).astype(BF16)

    @pl.when(step == 0)
    def _():
        branch_two[...] = jnp.zeros_like(branch_two)
        second_grad[...] = jnp.zeros_like(second_grad)

    branch_two[...] += dot(active, down[...])
    second_grad[...] += dot_nt(hidden_in, up[...])
    up_grad[...] = dot_tn(low, hidden_in).astype(BF16)
    down_grad[...] = dot_tn(active, grad).astype(BF16)
    up_bias_grad[...] = column_sum(hidden_in.astype(F32))


def middle_back_kernel(
    slots,
    info,
    middle,
    branch,
    branch_two,
    second_grad,
    incoming,
    attended,
    weight,
    down_bias,
    second_scale,
    gain,
    first_scale,
    out_patches,
    out_specials,
    middle_grad,
    attended_grad,
    weight_grad,
    vectors,
):
    rows = middle.shape[0]
    mid = middle[...]
    given = incoming[...]
    two = branch_two[...] + down_bias[...]
    output = mid + second_scale[...] * two
    counted = counted_rows(info, 0, slots, slots, mid.shape[1])
    out_patches[...] = jnp.where(counted, output[:slots], 0.0).astype(BF16)
    out_specials[...] = output[slots:]
    hat, scale = normalize(mid)
    grad = second_grad[...]
    back = given + normalize_back(grad * gain[...], hat, scale)
    middle_grad[...] = back
    out_in = (back * first_scale[...]).astype(BF16)
    attended_grad[...] = dot_nt(out_in, weight[...])
    weight_grad[...] = dot_tn(attended[...].astype(BF16), out_in).astype(BF16)
    vectors[...] = jnp.concatenate(
        [
            column_sum(given * two),
            column_sum(grad * hat),
            column_sum(grad),
            column_sum(back * branch[...]),
            column_sum(out_in.astype(F32)),
            jnp.zeros((3, mid.shape[1]), F32),
        ],
        axis=0,
    )


def attend_back_kernel(
    slots,
    info,
    weights,
    queries,
    keys,
    values,
    attended,
    totals,
    attended_grad,
    query_grad,
    key_grad,
    value_grad,
):
    rows = queries.shape[0]
    factor = HEAD ** (-0.5)
    stacked = stack_pair((queries[...].astype(F32) * factor).astype(BF16))
    inverse = 1.0 / totals[...]
    scaled = attended_grad[...] * inverse
    returned = stack_pair(scaled.astype(BF16))
    product = scaled * attended[...]
    slope = jnp.sum(stack_pair(product), axis=1, keepdims=True)
    stacked_t = stacked.astype(F32).T.astype(BF16)
    returned_t = returned.astype(F32).T.astype(BF16)
    total = jnp.zeros((2 * rows, PAIR), F32)
    for block in range(BANDS):
        span = slice(block * rows, (block + 1) * rows)
        counted = counted_rows(info, block, rows, slots, PAIR)
        low = weights[0, :, span]
        moved = dot_nt(returned, values[span, :])
        scores = (low.astype(F32) * (moved - slope)).astype(BF16)
        total = total + dot(scores, keys[span, :])
        key_part = dot(stacked_t, scores).T
        value_part = dot(returned_t, low).T
        key_grad[span, :] = jnp.where(counted, key_part, 0.0).astype(BF16)
        value_grad[span, :] = jnp.where(counted, value_part, 0.0).astype(BF16)
    query_grad[...] = (unstack_pair(total) * factor).astype(BF16)


def joint_grad_kernel(firsts, query_grad, key_grad, value_grad, weight, weight_grad, first_grad):
    rows = query_grad.shape[0]
    width = query_grad.shape[1]
    low = firsts[...]
    weight_grad[:, :width] = dot_tn(low[:rows], query_grad[...]).astype(BF16)
    weight_grad[:, width : 2 * width] = dot_tn(low, key_grad[...]).astype(BF16)
    weight_grad[:, 2 * width :] = dot_tn(low, value_grad[...]).astype(BF16)
    for block in range(BANDS):
        span = slice(block * rows, (block + 1) * rows)
        part = dot_nt(key_grad[span, :], weight[:, width : 2 * width])
        part = part + dot_nt(value_grad[span, :], weight[:, 2 * width :])
        if block == 0:
            part = part + dot_nt(query_grad[...], weight[:, :width])
        first_grad[span, :] = part.astype(BF16)


def first_back_kernel(
    slots,
    first_grad,
    tokens,
    middle_grad,
    mask,
    gain,
    query_grad,
    value_grad,
    grad_patches,
    grad_specials,
    vectors,
):
    grad = first_grad[...]
    hat, scale = normalize(tokens[...])
    token_grad = middle_grad[...] + normalize_back(grad * gain[...], hat, scale)
    masked = mask[...] > 0
    patch_grad = token_grad[:slots]
    grad_patches[...] = jnp.where(masked, 0.0, patch_grad).astype(BF16)
    grad_specials[...] = token_grad[slots:]
    vectors[...] = jnp.concatenate(
        [
            column_sum(jnp.where(masked, patch_grad, 0.0)),
            column_sum(grad * hat),
            column_sum(grad),
            column_sum(query_grad[...].astype(F32)),
            column_sum(value_grad[...].astype(F32)),
            jnp.zeros((3, grad.shape[1]), F32),
        ],
        axis=0,
    )


def swap(x, axis, distance):
    size = lax.axis_size(axis)
    return lax.ppermute(x, axis, [(i, i ^ distance) for i in range(size)])


def halve(x, axis, distance):
    bit = (lax.axis_index(axis) // distance) % 2
    sent = lax.dynamic_index_in_dim(x, 1 - bit, 0, keepdims=False)
    kept = lax.dynamic_index_in_dim(x, bit, 0, keepdims=False)
    got = swap(sent, axis, distance)
    return (kept.astype(F32) + got.astype(F32)).astype(BF16)


def reduce_weight(partial_sum):
    rows, columns = partial_sum.shape
    crops = lax.axis_size("crop")
    half = columns // 2
    x = jnp.stack([partial_sum[:, :half], partial_sum[:, half:]])
    x = halve(x, "band", 1)
    distance = 1
    held = x.reshape((crops, rows // crops, half))
    order = []
    while distance < crops:
        order.append(distance)
        distance *= 2
    for distance in order:
        count = held.shape[0]
        held = held.reshape((count // 2, 2) + held.shape[1:])
        held = jnp.moveaxis(held, 1, 0)
        held = halve(held, "crop", distance)
    held = held.reshape((rows // crops, half))
    other = swap(held, "band", 2)
    full = (held.astype(F32) + other.astype(F32)).astype(BF16)
    mate = swap(full, "band", 1)
    bit = lax.axis_index("band") % 2
    low = jnp.where(bit == 0, full, mate).astype(F32)
    high = jnp.where(bit == 0, mate, full).astype(F32)
    return jnp.concatenate([low, high], axis=1)


def gather_blocks(x):
    near = swap(x, "band", 1)
    far = swap(x, "band", 2)
    diagonal = swap(far, "band", 1)
    return jnp.concatenate([x, near, far, diagonal], axis=0)


def scatter_blocks(x):
    rows = x.shape[0] // BANDS
    got = swap(jnp.concatenate([x[rows : 2 * rows], x[3 * rows :]], axis=0), "band", 1)
    own = x[:rows].astype(F32) + got[:rows].astype(F32)
    far = (x[2 * rows : 3 * rows].astype(F32) + got[rows:].astype(F32)).astype(BF16)
    return own + swap(far, "band", 2).astype(F32)


def body(
    patches,
    specials,
    patch_mask,
    band_rows,
    mask_token,
    first_gain,
    first_shift,
    joint_weight,
    query_bias,
    value_bias,
    out_weight,
    out_bias,
    first_scale,
    second_gain,
    second_shift,
    up_weight,
    up_bias,
    down_weight,
    down_bias,
    second_scale,
    cot_patches,
    cot_specials,
):
    slots, width = patches.shape[1:]
    special_count = specials.shape[1]
    hidden_width = up_weight.shape[1]
    owned = -(-special_count // BANDS)
    rows = round_up(slots + owned, 16)
    pad = rows - slots
    every = BANDS * rows
    pairs = width // PAIR
    band = lax.axis_index("band")
    relatives = [band ^ r for r in range(BANDS)]
    info = jnp.stack(
        [band_rows[b] * GRID for b in relatives]
        + [(special_count - b + BANDS - 1) // BANDS for b in relatives]
        + [band]
    ).astype(jnp.int32)
    line = lambda v: v.reshape(1, -1)
    mask = patch_mask.reshape(slots, 1)
    patches, specials = patches[0], specials[0]
    cot_patches, cot_specials = cot_patches[0], cot_specials[0]
    shaped = jax.ShapeDtypeStruct

    tokens, first = pl.pallas_call(
        first_kernel,
        out_shape=[shaped((rows, width), F32), shaped((rows, width), BF16)],
        in_specs=[SMEM] + [pl.BlockSpec(memory_space=pltpu.VMEM)] * 6,
        compiler_params=params(),
        name="first",
    )(info, mask, patches, specials, line(mask_token), line(first_gain), line(first_shift))

    firsts = gather_blocks(first)

    block = pl.BlockSpec((rows, width), lambda i: (i, 0))
    queries, keys, values = pl.pallas_call(
        partial(project_kernel, slots),
        grid=(BANDS,),
        out_shape=[
            shaped((rows, width), BF16),
            shaped((every, width), BF16),
            shaped((every, width), BF16),
        ],
        in_specs=[SMEM, block, whole((width, 3 * width)), whole((1, width)), whole((1, width))],
        out_specs=[whole((rows, width)), block, block],
        compiler_params=params(),
        name="project",
    )(info, firsts, joint_weight, line(query_bias), line(value_bias))

    own_pair = pl.BlockSpec((rows, PAIR), lambda i: (0, i))
    all_pair = pl.BlockSpec((every, PAIR), lambda i: (0, i))
    kept = pl.BlockSpec((1, 2 * rows, every), lambda i: (i, 0, 0))
    attended, totals, weights = pl.pallas_call(
        partial(attend_kernel, slots),
        grid=(pairs,),
        out_shape=[
            shaped((rows, width), F32),
            shaped((rows, width), F32),
            shaped((pairs, 2 * rows, every), BF16),
        ],
        in_specs=[SMEM, own_pair, all_pair, all_pair],
        out_specs=[own_pair, own_pair, kept],
        compiler_params=params(),
        name="attend",
    )(info, queries, keys, values)

    vmem = pl.BlockSpec(memory_space=pltpu.VMEM)
    branch, middle, second, incoming, down_in, down_bias_grad = pl.pallas_call(
        partial(middle_kernel, slots),
        out_shape=[
            shaped((rows, width), F32),
            shaped((rows, width), F32),
            shaped((rows, width), BF16),
            shaped((rows, width), F32),
            shaped((rows, width), BF16),
            shaped((1, width), F32),
        ],
        in_specs=[SMEM] + [vmem] * 10,
        out_specs=[vmem] * 6,
        compiler_params=params(),
        name="middle",
    )(
        info,
        attended,
        tokens,
        out_weight,
        line(out_bias),
        line(first_scale),
        line(second_gain),
        line(second_shift),
        line(second_scale),
        cot_patches,
        cot_specials,
    )

    steps = 6
    chunk = hidden_width // steps
    branch_two, second_grad, up_grad, up_bias_grad, down_grad = pl.pallas_call(
        mlp_kernel,
        grid=(steps,),
        out_shape=[
            shaped((rows, width), F32),
            shaped((rows, width), F32),
            shaped((width, hidden_width), BF16),
            shaped((1, hidden_width), F32),
            shaped((hidden_width, width), BF16),
        ],
        in_specs=[
            whole((rows, width)),
            whole((rows, width)),
            pl.BlockSpec((width, chunk), lambda i: (0, i)),
            pl.BlockSpec((1, chunk), lambda i: (0, i)),
            pl.BlockSpec((chunk, width), lambda i: (i, 0)),
        ],
        out_specs=[
            whole((rows, width)),
            whole((rows, width)),
            pl.BlockSpec((width, chunk), lambda i: (0, i)),
            pl.BlockSpec((1, chunk), lambda i: (0, i)),
            pl.BlockSpec((chunk, width), lambda i: (i, 0)),
        ],
        compiler_params=params(),
        name="mlp",
    )(second, down_in, up_weight, line(up_bias), down_weight)

    out_patches, out_own, middle_grad, attended_grad, out_weight_grad, vectors = pl.pallas_call(
        partial(middle_back_kernel, slots),
        out_shape=[
            shaped((slots, width), BF16),
            shaped((pad, width), F32),
            shaped((rows, width), F32),
            shaped((rows, width), F32),
            shaped((width, width), BF16),
            shaped((8, width), F32),
        ],
        in_specs=[SMEM] + [vmem] * 11,
        out_specs=[vmem] * 6,
        compiler_params=params(),
        name="middle_back",
    )(
        info,
        middle,
        branch,
        branch_two,
        second_grad,
        incoming,
        attended,
        out_weight,
        line(down_bias),
        line(second_scale),
        line(second_gain),
        line(first_scale),
    )

    query_grad, key_grad, value_grad = pl.pallas_call(
        partial(attend_back_kernel, slots),
        grid=(pairs,),
        out_shape=[
            shaped((rows, width), BF16),
            shaped((every, width), BF16),
            shaped((every, width), BF16),
        ],
        in_specs=[SMEM, kept, own_pair, all_pair, all_pair, own_pair, own_pair, own_pair],
        out_specs=[own_pair, all_pair, all_pair],
        compiler_params=params(),
        name="attend_back",
    )(info, weights, queries, keys, values, attended, totals, attended_grad)

    joint_weight_grad, first_part = pl.pallas_call(
        joint_grad_kernel,
        out_shape=[shaped((width, 3 * width), BF16), shaped((every, width), BF16)],
        in_specs=[vmem] * 5,
        out_specs=[vmem] * 2,
        compiler_params=params(),
        name="joint_grad",
    )(firsts, query_grad, key_grad, value_grad, joint_weight)

    first_grad = scatter_blocks(first_part)

    grad_patches, grad_own, more_vectors = pl.pallas_call(
        partial(first_back_kernel, slots),
        out_shape=[
            shaped((slots, width), BF16),
            shaped((pad, width), F32),
            shaped((8, width), F32),
        ],
        in_specs=[vmem] * 7,
        out_specs=[vmem] * 3,
        compiler_params=params(),
        name="first_back",
    )(first_grad, tokens, middle_grad, mask, line(first_gain), query_grad, value_grad)

    both = jnp.concatenate([out_own[:owned], grad_own[:owned]], axis=1).astype(BF16)
    both = lax.all_gather(both, "band", axis=0, tiled=False)
    both = jnp.transpose(both, (1, 0, 2)).reshape(owned * BANDS, 2 * width)[:special_count]
    out_specials, grad_specials = both[None, :, :width], both[None, :, width:]

    crops = lax.axis_size("crop")
    small = jnp.concatenate(
        [vectors[:5], more_vectors[:5], down_bias_grad, up_bias_grad.reshape(-1, width)], axis=0
    )
    count = small.shape[0]
    small = jnp.transpose(small.reshape(count - hidden_width // width, crops, -1), (1, 0, 2)) if False else small
    plain = small[:11].reshape(11, crops, width // crops)
    wide = small[11:].reshape(crops, hidden_width // crops)
    packed = jnp.concatenate(
        [jnp.transpose(plain, (1, 0, 2)).reshape(crops, -1), wide], axis=1
    )
    packed = lax.psum_scatter(packed, "crop", scatter_dimension=0, tiled=False)
    packed = lax.psum(packed, "band")
    part = width // crops
    take = lambda i: packed[i * part : (i + 1) * part]

    return (
        out_patches[None],
        out_specials,
        grad_patches[None],
        grad_specials,
        take(5),
        take(6),
        take(7),
        reduce_weight(joint_weight_grad),
        take(8),
        take(9),
        reduce_weight(out_weight_grad),
        take(4),
        take(3),
        take(1),
        take(2),
        reduce_weight(up_grad),
        packed[11 * part :],
        reduce_weight(down_grad),
        take(10),
        take(0),
    )


def solution(mesh):
    split = P("crop", "band", None)
    special = P("crop", None, None)
    in_specs = (
        (split, special, P("crop", "band")) + (P(),) * 17 + (split, special)
    )
    line, matrix = P("crop"), P("crop", None)
    out_specs = (
        split,
        special,
        split,
        special,
        line,
        line,
        line,
        matrix,
        line,
        line,
        matrix,
        line,
        line,
        line,
        line,
        matrix,
        line,
        matrix,
        line,
        line,
    )
    return jax.shard_map(body, mesh=mesh, in_specs=in_specs, out_specs=out_specs, check_vma=False)
```

```python
from functools import partial

import jax
import jax.numpy as jnp
from jax import lax
from jax.experimental import pallas as pl
from jax.experimental.pallas import tpu as pltpu
from jax.sharding import PartitionSpec as P

HEAD = 64
GRID = 37
PAIR = 2 * HEAD
BANDS = 4
F32 = jnp.float32
BF16 = jnp.bfloat16
VMEM_LIMIT = 56 << 20


def round_up(value, unit):
    return (value + unit - 1) // unit * unit


def params(semantics=None):
    return pltpu.CompilerParams(vmem_limit_bytes=VMEM_LIMIT)


def dot(a, b):
    return jnp.dot(a, b, preferred_element_type=F32)


def dot_nt(a, b):
    return lax.dot_general(a, b, (((1,), (1,)), ((), ())), preferred_element_type=F32)


def dot_tn(a, b):
    return lax.dot_general(a, b, (((0,), (0,)), ((), ())), preferred_element_type=F32)


def normalize(rows):
    centred = rows - jnp.mean(rows, axis=-1, keepdims=True)
    spread = jnp.mean(centred * centred, axis=-1, keepdims=True)
    scale = lax.rsqrt(spread + 1e-06)
    return centred * scale, scale


def normalize_back(grad, hat, scale):
    return scale * (
        grad
        - jnp.mean(grad, axis=-1, keepdims=True)
        - hat * jnp.mean(grad * hat, axis=-1, keepdims=True)
    )


def column_sum(rows):
    return jnp.sum(rows, axis=0, keepdims=True)


def line(ref):
    return ref[...].reshape(1, -1)


def whole(shape):
    return pl.BlockSpec(shape, lambda *_: (0,) * len(shape))


VMEM = pl.BlockSpec(memory_space=pltpu.VMEM)
ANY = pl.BlockSpec(memory_space=pl.ANY)
SMEM = pl.BlockSpec(memory_space=pltpu.SMEM)


def own_special(specials, band, slot):
    row = jnp.zeros((1, specials.shape[1]), F32)
    for special in range(specials.shape[0]):
        if special // BANDS == slot:
            row = row + jnp.where(band == special % BANDS, specials[special : special + 1], 0.0)
    return row


def place_rows(ref, patch_rows, specials, band):
    slots = patch_rows.shape[0]
    rows = ref.shape[0]
    ref[0:slots, :] = patch_rows
    extra = [own_special(specials, band, slot) for slot in range(rows - slots)]
    ref[slots:rows, :] = jnp.concatenate(extra, axis=0)


def counted_rows(info_ref, relative, rows, slots, width):
    index = lax.broadcasted_iota(jnp.int32, (rows, width), 0)
    used = index < info_ref[relative]
    special = (index >= slots) & (index < slots + info_ref[BANDS + relative])
    return used | special


def stack_pair(rows):
    lane = lax.broadcasted_iota(jnp.int32, rows.shape, 1)
    zero = jnp.zeros_like(rows)
    return jnp.concatenate(
        [jnp.where(lane < HEAD, rows, zero), jnp.where(lane >= HEAD, rows, zero)], axis=0
    )


def unstack_pair(rows):
    half = rows.shape[0] // 2
    lane = lax.broadcasted_iota(jnp.int32, (half, rows.shape[1]), 1)
    return jnp.where(lane < HEAD, rows[:half], rows[half:])


def mask_column(mask):
    return jnp.broadcast_to(mask[...].astype(F32), (8, mask.shape[1])).T[:, :1] > 0


def first_kernel(info, mask, patches, specials, token, gain, shift, tokens, first):
    band = info[2 * BANDS]
    filled = jnp.where(mask_column(mask), line(token), patches[...].astype(F32))
    place_rows(tokens, filled, specials[...].astype(F32), band)
    hat, _ = normalize(tokens[...])
    first[...] = (hat * line(gain) + line(shift)).astype(BF16)


def project_kernel(slots, info, first, weight, query_bias, value_bias, queries, keys, values):
    relative = pl.program_id(0)
    rows, width = queries.shape
    counted = counted_rows(info, relative, rows, slots, width)
    low = first[...]

    @pl.when(relative == 0)
    def _():
        queries[...] = (dot(low, weight[:, :width]) + line(query_bias)).astype(BF16)

    keys[...] = jnp.where(counted, dot(low, weight[:, width : 2 * width]), 0.0).astype(BF16)
    values[...] = jnp.where(
        counted, dot(low, weight[:, 2 * width :]) + line(value_bias), 0.0
    ).astype(BF16)


def attend_kernel(slots, info, queries, keys, values, attended, totals, weights):
    rows = queries.shape[0]
    factor = HEAD ** (-0.5)
    stacked = stack_pair((queries[...].astype(F32) * factor).astype(BF16))
    scores = dot_nt(stacked, keys[...])
    low = jnp.exp(scores).astype(BF16)
    weights[0] = low
    ones = jnp.concatenate(
        [
            counted_rows(info, r, rows, slots, PAIR).astype(F32).astype(BF16)
            for r in range(BANDS)
        ],
        axis=0,
    )
    summed = dot(low, jnp.concatenate([values[...], ones], axis=1))
    total = unstack_pair(summed[:, PAIR:])
    attended[...] = unstack_pair(summed[:, :PAIR]) / total
    totals[...] = total


def middle_kernel(
    slots,
    info,
    attended,
    tokens,
    weight,
    bias,
    first_scale,
    gain,
    shift,
    second_scale,
    cot_patches,
    cot_specials,
    branch,
    middle,
    second,
    incoming,
    down_in,
    down_bias_grad,
):
    rows = tokens.shape[0]
    band = info[2 * BANDS]
    side = dot(attended[...].astype(BF16), weight[...]) + line(bias)
    branch[...] = side
    mid = tokens[...] + line(first_scale) * side
    middle[...] = mid
    hat, _ = normalize(mid)
    second[...] = (hat * line(gain) + line(shift)).astype(BF16)
    counted = counted_rows(info, 0, slots, slots, tokens.shape[1])
    given = jnp.where(counted, cot_patches[...].astype(F32), 0.0)
    place_rows(incoming, given, cot_specials[...].astype(F32), band)
    low = (incoming[...] * line(second_scale)).astype(BF16)
    down_in[...] = low
    down_bias_grad[...] = column_sum(low.astype(F32))


def gelu_and_slope(x):
    phi = 0.5 + 0.5 * lax.erf(x * 0.7071067811865476)
    density = jnp.exp(-0.5 * x * x) * 0.3989422804014327
    return x * phi, phi + x * density


def mlp_kernel(
    second, down_in, up, up_bias, down, branch_two, second_grad, up_grad, up_bias_grad, down_grad
):
    step = pl.program_id(0)
    low = second[...]
    grad = down_in[...]
    hidden = dot(low, up[...]) + up_bias[...]
    active, slope = gelu_and_slope(hidden)
    active = active.astype(BF16)
    hidden_in = (slope * dot_nt(grad, down[...])).astype(BF16)

    @pl.when(step == 0)
    def _():
        branch_two[...] = jnp.zeros_like(branch_two)
        second_grad[...] = jnp.zeros_like(second_grad)

    branch_two[...] += dot(active, down[...])
    second_grad[...] += dot_nt(hidden_in, up[...])
    up_grad[...] = dot_tn(low, hidden_in).astype(BF16)
    down_grad[...] = dot_tn(active, grad).astype(BF16)
    up_bias_grad[...] = column_sum(hidden_in.astype(F32))


def middle_back_kernel(
    slots,
    info,
    middle,
    branch,
    branch_two,
    second_grad,
    incoming,
    attended,
    weight,
    down_bias,
    second_scale,
    gain,
    first_scale,
    out_patches,
    out_specials,
    middle_grad,
    attended_grad,
    weight_grad,
    vectors,
):
    rows = middle.shape[0]
    mid = middle[...]
    given = incoming[...]
    two = branch_two[...] + line(down_bias)
    output = mid + line(second_scale) * two
    counted = counted_rows(info, 0, slots, slots, mid.shape[1])
    out_patches[...] = jnp.where(counted, output[:slots], 0.0).astype(BF16)
    out_specials[...] = output[slots:]
    hat, scale = normalize(mid)
    grad = second_grad[...]
    back = given + normalize_back(grad * line(gain), hat, scale)
    middle_grad[...] = back
    out_in = (back * line(first_scale)).astype(BF16)
    attended_grad[...] = dot_nt(out_in, weight[...])
    weight_grad[...] = dot_tn(attended[...].astype(BF16), out_in).astype(BF16)
    vectors[...] = jnp.concatenate(
        [
            column_sum(given * two),
            column_sum(grad * hat),
            column_sum(grad),
            column_sum(back * branch[...]),
            column_sum(out_in.astype(F32)),
            jnp.zeros((3, mid.shape[1]), F32),
        ],
        axis=0,
    )


def attend_back_kernel(
    slots,
    info,
    weights,
    queries,
    keys,
    values,
    attended,
    totals,
    attended_grad,
    query_grad,
    key_grad,
    value_grad,
):
    rows = queries.shape[0]
    factor = HEAD ** (-0.5)
    stacked = stack_pair((queries[...].astype(F32) * factor).astype(BF16))
    inverse = 1.0 / totals[...]
    scaled = attended_grad[...] * inverse
    returned = stack_pair(scaled.astype(BF16))
    product = scaled * attended[...]
    slope = jnp.sum(stack_pair(product), axis=1, keepdims=True)
    stacked_t = stacked.astype(F32).T.astype(BF16)
    returned_t = returned.astype(F32).T.astype(BF16)
    total = jnp.zeros((2 * rows, PAIR), F32)
    for block in range(BANDS):
        span = slice(block * rows, (block + 1) * rows)
        counted = counted_rows(info, block, rows, slots, PAIR)
        low = weights[0, :, span]
        moved = dot_nt(returned, values[span, :])
        scores = (low.astype(F32) * (moved - slope)).astype(BF16)
        total = total + dot(scores, keys[span, :])
        key_part = dot(stacked_t, scores).T
        value_part = dot(returned_t, low).T
        key_grad[span, :] = jnp.where(counted, key_part, 0.0).astype(BF16)
        value_grad[span, :] = jnp.where(counted, value_part, 0.0).astype(BF16)
    query_grad[...] = (unstack_pair(total) * factor).astype(BF16)


def joint_grad_kernel(firsts, query_grad, key_grad, value_grad, weight, weight_grad, first_grad):
    rows = query_grad.shape[0]
    width = query_grad.shape[1]
    low = firsts[...]
    weight_grad[:, :width] = dot_tn(low[:rows], query_grad[...]).astype(BF16)
    weight_grad[:, width : 2 * width] = dot_tn(low, key_grad[...]).astype(BF16)
    weight_grad[:, 2 * width :] = dot_tn(low, value_grad[...]).astype(BF16)
    for block in range(BANDS):
        span = slice(block * rows, (block + 1) * rows)
        part = dot_nt(key_grad[span, :], weight[:, width : 2 * width])
        part = part + dot_nt(value_grad[span, :], weight[:, 2 * width :])
        if block == 0:
            part = part + dot_nt(query_grad[...], weight[:, :width])
        first_grad[span, :] = part.astype(BF16)


def first_back_kernel(
    slots,
    first_grad,
    tokens,
    middle_grad,
    mask,
    gain,
    query_grad,
    value_grad,
    grad_patches,
    grad_specials,
    vectors,
):
    grad = first_grad[...]
    hat, scale = normalize(tokens[...])
    token_grad = middle_grad[...] + normalize_back(grad * line(gain), hat, scale)
    masked = mask_column(mask)
    patch_grad = token_grad[:slots]
    grad_patches[...] = jnp.where(masked, 0.0, patch_grad).astype(BF16)
    grad_specials[...] = token_grad[slots:]
    vectors[...] = jnp.concatenate(
        [
            column_sum(jnp.where(masked, patch_grad, 0.0)),
            column_sum(grad * hat),
            column_sum(grad),
            column_sum(query_grad[...].astype(F32)),
            column_sum(value_grad[...].astype(F32)),
            jnp.zeros((3, grad.shape[1]), F32),
        ],
        axis=0,
    )


def swap(x, axis, distance):
    size = lax.axis_size(axis)
    return lax.ppermute(x, axis, [(i, i ^ distance) for i in range(size)])


def halve(x, axis, distance):
    bit = (lax.axis_index(axis) // distance) % 2
    sent = lax.dynamic_index_in_dim(x, 1 - bit, 0, keepdims=False)
    kept = lax.dynamic_index_in_dim(x, bit, 0, keepdims=False)
    got = swap(sent, axis, distance)
    return (kept.astype(F32) + got.astype(F32)).astype(BF16)


def reduce_weight(partial_sum):
    rows, columns = partial_sum.shape
    crops = lax.axis_size("crop")
    half = columns // 2
    x = jnp.stack([partial_sum[:, :half], partial_sum[:, half:]])
    x = halve(x, "band", 1)
    distance = 1
    held = x.reshape((crops, rows // crops, half))
    order = []
    while distance < crops:
        order.append(distance)
        distance *= 2
    for distance in order:
        count = held.shape[0]
        held = held.reshape((count // 2, 2) + held.shape[1:])
        held = jnp.moveaxis(held, 1, 0)
        held = halve(held, "crop", distance)
    held = held.reshape((rows // crops, half))
    other = swap(held, "band", 2)
    full = (held.astype(F32) + other.astype(F32)).astype(BF16)
    mate = swap(full, "band", 1)
    bit = lax.axis_index("band") % 2
    low = jnp.where(bit == 0, full, mate).astype(F32)
    high = jnp.where(bit == 0, mate, full).astype(F32)
    return jnp.concatenate([low, high], axis=1)


def gather_blocks(x):
    near = swap(x, "band", 1)
    far = swap(x, "band", 2)
    diagonal = swap(far, "band", 1)
    return jnp.concatenate([x, near, far, diagonal], axis=0)


def scatter_blocks(x):
    rows = x.shape[0] // BANDS
    got = swap(jnp.concatenate([x[rows : 2 * rows], x[3 * rows :]], axis=0), "band", 1)
    own = x[:rows].astype(F32) + got[:rows].astype(F32)
    far = (x[2 * rows : 3 * rows].astype(F32) + got[rows:].astype(F32)).astype(BF16)
    return own + swap(far, "band", 2).astype(F32)


def reduce_general(
    up, down, out, joint, vectors, more, down_bias, up_bias, out_own, grad_own, special_count
):
    crops = lax.axis_size("crop")
    width = down.shape[1]
    owned = -(-special_count // BANDS)
    both = jnp.concatenate([out_own[:owned], grad_own[:owned]], axis=1).astype(BF16)
    both = lax.all_gather(both, "band", axis=0, tiled=False)
    both = jnp.transpose(both, (1, 0, 2)).reshape(owned * BANDS, 2 * width)[:special_count]
    plain = jnp.concatenate([vectors[:5], more[:5], down_bias], axis=0)
    plain = jnp.transpose(plain.reshape(11, crops, -1), (1, 0, 2)).reshape(crops, -1)
    packed = jnp.concatenate([plain, up_bias.reshape(crops, -1)], axis=1)
    packed = lax.psum_scatter(packed, "crop", scatter_dimension=0, tiled=False)
    packed = lax.psum(packed, "band")
    part = width // crops
    return (
        reduce_weight(up),
        reduce_weight(down),
        reduce_weight(out),
        reduce_weight(joint),
        [packed[i * part : (i + 1) * part] for i in range(11)],
        packed[11 * part :],
        both[None, :, :width],
        both[None, :, width:],
    )


MESH = pl.DeviceIdType.MESH
PLACES = ("core", "x", "diagonal", "y", "near", "far")


class Place:
    def __init__(self):
        band, crop = lax.axis_index("band"), lax.axis_index("crop")
        self.band = band
        self.core, self.x = lax.rem(band, 2), lax.div(band, 2)
        self.y, self.near, self.far = lax.rem(crop, 2), lax.rem(lax.div(crop, 2), 2), lax.div(crop, 4)
        core_step, x_step = 1 - 2 * self.core, 2 - 4 * self.x
        self.device = {
            "core": (band + core_step, crop),
            "x": (band + x_step, crop),
            "diagonal": (band + core_step + x_step, crop),
            "y": (band, crop + 1 - 2 * self.y),
            "near": (band, crop + 2 - 4 * self.near),
            "far": (band, crop + 4 - 8 * self.far),
        }

    def greet(self, names):
        barrier = pltpu.get_barrier_semaphore()
        for name in names:
            pl.semaphore_signal(barrier, inc=1, device_id=self.device[name], device_id_type=MESH)
        pl.semaphore_wait(barrier, len(names))


class Sender:
    def __init__(self, place, send_sems, recv_sems):
        self.place, self.send_sems, self.recv_sems = place, send_sems, recv_sems
        self.copies = {}

    def send(self, key, source, target, name):
        index = len(self.copies)
        copy = pltpu.make_async_remote_copy(
            src_ref=source,
            dst_ref=target,
            send_sem=self.send_sems.at[index],
            recv_sem=self.recv_sems.at[index],
            device_id=self.place.device[name],
            device_id_type=MESH,
        )
        copy.start()
        self.copies[key] = copy

    def arrived(self, key):
        self.copies[key].wait_recv()

    def finish(self):
        for copy in self.copies.values():
            copy.wait_send()


def chunk_list(hidden_parts):
    chunks = []
    for part in range(hidden_parts):
        chunks += [("down", part), ("up", part)]
    return chunks + [("out", 0), ("joint", 0), ("joint", 1), ("joint", 2)]


def chunk_scratch(count, rows, columns):
    unit = (rows, columns)
    return [
        pltpu.VMEM((count, 2, 2, 2, 2) + unit, BF16),
        pltpu.VMEM((count, 2, 2, 2, 2) + unit, BF16),
        pltpu.VMEM((count, 2, 2, 2) + unit, BF16),
        pltpu.VMEM((count, 2, 2) + unit, BF16),
        pltpu.VMEM((count, 2) + unit, BF16),
        pltpu.VMEM((count, 2) + unit, BF16),
    ]


class ChunkSums:
    def __init__(self, place, sender, buffers, total):
        self.place, self.sender, self.total = place, sender, total
        self.own, self.got, self.got_a, self.got_b, self.got_c, self.got_d = buffers

    def steps(self, n):
        return 7 if n % 2 == 0 else 6

    def step(self, n, stage):
        (self.even if n % 2 == 0 else self.odd)(n, stage)

    def even(self, n, stage):
        p, s, own = self.place, self.sender, self.own
        if stage == 0:
            own[n] = own[n] + self.got[n]
            s.send((n, 1), own.at[n, 1 - p.x], self.got_a.at[n], "x")
        elif stage == 1:
            s.arrived((n, 1))
            own[n, p.x] = own[n, p.x] + self.got_a[n]
            s.send((n, 2), own.at[n, p.x, :, :, 1 - p.y], self.got_b.at[n], "y")
        elif stage == 2:
            s.arrived((n, 2))
            own[n, p.x, :, :, p.y] = own[n, p.x, :, :, p.y] + self.got_b[n]
            s.send((n, 3), own.at[n, p.x, :, 1 - p.near, p.y], self.got_c.at[n], "near")
        elif stage == 3:
            s.arrived((n, 3))
            own[n, p.x, :, p.near, p.y] = own[n, p.x, :, p.near, p.y] + self.got_c[n]
            s.send((n, 4), own.at[n, p.x, 1 - p.far, p.near, p.y], self.got_d.at[n, 0], "far")
        elif stage == 4:
            s.arrived((n, 4))
            self.total[n, p.core, p.x] = own[n, p.x, p.far, p.near, p.y] + self.got_d[n, 0]
            place = self.total.at[n, p.core, p.x]
            s.send((n, 5), place, place, "x")
        elif stage == 5:
            s.arrived((n, 5))
            place = self.total.at[n, p.core]
            s.send((n, 6), place, place, "core")
        else:
            s.arrived((n, 6))

    def odd(self, n, stage):
        p, s, own = self.place, self.sender, self.own
        if stage == 0:
            own[n] = own[n] + self.got[n]
            s.send((n, 1), own.at[n, :, :, 1 - p.y], self.got_a.at[n], "y")
        elif stage == 1:
            s.arrived((n, 1))
            own[n, :, :, p.y] = own[n, :, :, p.y] + self.got_a[n]
            s.send((n, 2), own.at[n, :, 1 - p.near, p.y], self.got_b.at[n], "near")
        elif stage == 2:
            s.arrived((n, 2))
            own[n, :, p.near, p.y] = own[n, :, p.near, p.y] + self.got_b[n]
            s.send((n, 3), own.at[n, 1 - p.far, p.near, p.y], self.got_c.at[n], "far")
        elif stage == 3:
            s.arrived((n, 3))
            own[n, p.far, p.near, p.y] = own[n, p.far, p.near, p.y] + self.got_c[n]
            s.send((n, 4), own.at[n, p.far, p.near, p.y], self.got_d.at[n], "x")
        elif stage == 4:
            s.arrived((n, 4))
            self.total[n, p.core] = own[n, p.far, p.near, p.y] + self.got_d[n]
            place = self.total.at[n, p.core]
            s.send((n, 5), place, place, "core")
        else:
            s.arrived((n, 5))


class VectorSums:
    def __init__(self, place, sender, buffers, total):
        self.place, self.sender, self.total = place, sender, total
        self.own, self.got, self.got_y, self.got_near = buffers

    def step(self, stage):
        p, s, own = self.place, self.sender, self.own
        if stage == 0:
            s.send("v0", own.at[0], self.got.at[0], "core")
        elif stage == 1:
            s.arrived("v0")
            own[1] = own[0] + self.got[0]
            s.send("v1", own.at[1], self.got.at[1], "x")
        elif stage == 2:
            s.arrived("v1")
            own[2] = own[1] + self.got[1]
            s.send("v2", own.at[2, :, :, 1 - p.y], self.got_y, "y")
        elif stage == 3:
            s.arrived("v2")
            own[2, :, :, p.y] = own[2, :, :, p.y] + self.got_y[...]
            s.send("v3", own.at[2, :, 1 - p.near, p.y], self.got_near.at[0:2], "near")
        elif stage == 4:
            s.arrived("v3")
            own[2, :, p.near, p.y] = own[2, :, p.near, p.y] + self.got_near[0:2]
            s.send("v4", own.at[2, 1 - p.far, p.near, p.y], self.got_near.at[2], "far")
        else:
            s.arrived("v4")
            self.total[...] = own[2, p.far, p.near, p.y] + self.got_near[2]


def pack_vectors(own, vectors, more, down_bias, up_bias, part):
    for crop in range(8):
        span = slice(crop * part, (crop + 1) * part)
        wide = 4 * crop * part
        rows = [vectors[0:5, span], more[0:5, span], down_bias[0:1, span]]
        rows += [up_bias[0:1, wide + j * part : wide + (j + 1) * part] for j in range(4)]
        own[0, crop // 4, crop // 2 % 2, crop % 2, 0:15, 0:part] = jnp.concatenate(rows, axis=0)


def vector_scratch():
    return [
        pltpu.VMEM((3, 2, 2, 2, 16, 128), F32),
        pltpu.VMEM((2, 2, 2, 2, 16, 128), F32),
        pltpu.VMEM((2, 2, 16, 128), F32),
        pltpu.VMEM((3, 16, 128), F32),
    ]


def weight_source(refs, chunk, columns, half, x_half):
    name, part = chunk
    ref = refs[name]
    if name == "down":
        span = pl.ds(pl.multiple_of(columns * half, 128), columns)
        if x_half is None:
            return ref.at[:, :, :, part, :, :, span]
        return ref.at[:, :, :, part, x_half, :, span]
    span = pl.ds(pl.multiple_of(2 * columns * part + columns * half, 128), columns)
    if x_half is None:
        return ref.at[:, :, :, :, :, span]
    return ref.at[:, :, :, x_half, :, span]


def reduce_kernel(
    chunks,
    up,
    down,
    out,
    joint,
    vectors,
    more,
    down_bias,
    up_bias,
    out_own,
    grad_own,
    total,
    vector_total,
    specials,
    *scratch,
):
    buffers, vector_buffers = scratch[:6], scratch[6:10]
    send_sems, recv_sems, load_sems = scratch[10:]
    count = len(chunks)
    columns = total.shape[4]
    part = 2 * total.shape[3]
    place = Place()
    sender = Sender(place, send_sems, recv_sems)
    sums = ChunkSums(place, sender, buffers, total)
    vector_sums = VectorSums(place, sender, vector_buffers, vector_total)
    refs = dict(up=up, down=down, out=out, joint=joint)
    loads = []
    for n, chunk in enumerate(chunks):
        pieces = [0, 1] if n % 2 == 0 else [None]
        copies = []
        for i, piece in enumerate(pieces):
            target = sums.own.at[n] if piece is None else sums.own.at[n, piece]
            source = weight_source(refs, chunk, columns, place.core, piece)
            copy = pltpu.make_async_copy(source, target, load_sems.at[n, i])
            copy.start()
            copies.append(copy)
        loads.append(copies)
    pack_vectors(vector_sums.own, vectors, more, down_bias, up_bias, part)
    mine = jnp.concatenate([out_own[0:4], grad_own[0:4]], axis=0)
    specials[place.band] = mine
    place.greet(PLACES)
    vector_sums.step(0)
    here = specials.at[place.band]
    for name in ("core", "x", "diagonal"):
        sender.send(("special", name), here, here, name)
    for n, chunk in enumerate(chunks):
        for piece in [0, 1] if n % 2 == 0 else [None]:
            target = sums.got.at[n] if piece is None else sums.got.at[n, piece]
            source = weight_source(refs, chunk, columns, 1 - place.core, piece)
            sender.send((n, 0, piece), source, target, "core")
    events = []
    for n in range(count):
        for stage in range(sums.steps(n)):
            events.append((n // 2 + stage, stage, n))
    for stage in range(1, 6):
        events.append((stage, 0, count + stage))
    for _, stage, n in sorted(events):
        if n >= count:
            vector_sums.step(n - count)
            continue
        if stage == 0:
            for copy in loads[n]:
                copy.wait()
            for piece in [0, 1] if n % 2 == 0 else [None]:
                sender.arrived((n, 0, piece))
        sums.step(n, stage)
    for name in ("core", "x", "diagonal"):
        sender.arrived(("special", name))
    sender.finish()


def finish_kernel(
    chunks,
    special_count,
    total,
    vector_total,
    specials,
    up,
    down,
    out,
    joint,
    up_bias,
    out_specials,
    grad_specials,
    *vectors,
):
    _, _, _, rows, columns = total.shape
    refs = dict(up=up, down=down, out=out, joint=joint)
    for n, (name, part) in enumerate(chunks):
        for core in range(2):
            for x in range(2):
                row, column = x * rows, core * columns
                if name == "down":
                    row += 2 * rows * part
                else:
                    column += 2 * columns * part
                value = total[n, core, x].astype(F32)
                refs[name][row : row + rows, column : column + columns] = value
    part = vectors[0].shape[0]
    for i, vector in enumerate(vectors):
        vector[...] = vector_total[i, 0:part]
    up_bias[...] = jnp.concatenate([vector_total[i : i + 1, 0:part] for i in range(11, 15)], axis=1)[0]
    for first, target in ((0, out_specials), (4, grad_specials)):
        picked = [
            specials[s % BANDS, first + s // BANDS : first + s // BANDS + 1]
            for s in range(special_count)
        ]
        target[0] = jnp.concatenate(picked, axis=0).astype(BF16)


def reduce_all(
    up, down, out, joint, vectors, more, down_bias, up_bias, out_own, grad_own, special_count
):
    width, hidden_width = up.shape
    chunks = chunk_list(hidden_width // width)
    part = width // 8
    rows, columns = part // 2, width // 2
    count = len(chunks)
    shaped = jax.ShapeDtypeStruct
    copies = 10 * count
    total, vector_total, specials = pl.pallas_call(
        partial(reduce_kernel, chunks),
        out_shape=[
            shaped((count, 2, 2, rows, columns), BF16),
            shaped((16, 128), F32),
            shaped((BANDS, 8, width), F32),
        ],
        in_specs=[ANY] * 4 + [VMEM] * 6,
        out_specs=[VMEM] * 3,
        scratch_shapes=chunk_scratch(count, rows, columns)
        + vector_scratch()
        + [
            pltpu.SemaphoreType.DMA((copies,)),
            pltpu.SemaphoreType.DMA((copies,)),
            pltpu.SemaphoreType.DMA((count, 2)),
        ],
        compiler_params=pltpu.CompilerParams(
            vmem_limit_bytes=VMEM_LIMIT, collective_id=0, has_side_effects=True
        ),
        name="reduce_all",
    )(
        up.reshape(2, 2, 2, 2, rows, hidden_width),
        down.reshape(2, 2, 2, hidden_width // width, 2, rows, width),
        out.reshape(2, 2, 2, 2, rows, width),
        joint.reshape(2, 2, 2, 2, rows, 3 * width),
        vectors,
        more,
        down_bias,
        up_bias,
        out_own,
        grad_own,
    )
    special = shaped((1, special_count, width), BF16)
    results = pl.pallas_call(
        partial(finish_kernel, chunks, special_count),
        out_shape=[
            shaped((part, hidden_width), F32),
            shaped((hidden_width // 8, width), F32),
            shaped((part, width), F32),
            shaped((part, 3 * width), F32),
            shaped((hidden_width // 8,), F32),
            special,
            special,
        ]
        + [shaped((part,), F32)] * 11,
        in_specs=[VMEM] * 3,
        out_specs=[VMEM] * 18,
        compiler_params=params(),
        name="finish",
    )(total, vector_total, specials)
    up, down, out, joint, up_bias, out_specials, grad_specials = results[:7]
    return up, down, out, joint, results[7:], up_bias, out_specials, grad_specials


def body(
    patches,
    specials,
    patch_mask,
    band_rows,
    mask_token,
    first_gain,
    first_shift,
    joint_weight,
    query_bias,
    value_bias,
    out_weight,
    out_bias,
    first_scale,
    second_gain,
    second_shift,
    up_weight,
    up_bias,
    down_weight,
    down_bias,
    second_scale,
    cot_patches,
    cot_specials,
):
    slots, width = patches.shape[1:]
    special_count = specials.shape[1]
    hidden_width = up_weight.shape[1]
    owned = -(-special_count // BANDS)
    rows = round_up(slots + owned, 16)
    pad = rows - slots
    every = BANDS * rows
    pairs = width // PAIR
    band = lax.axis_index("band")
    relatives = [band ^ r for r in range(BANDS)]
    info = jnp.stack(
        [band_rows[b] * GRID for b in relatives]
        + [(special_count - b + BANDS - 1) // BANDS for b in relatives]
        + [band]
    ).astype(jnp.int32)
    mask = patch_mask
    patches, specials = patches[0], specials[0]
    cot_patches, cot_specials = cot_patches[0], cot_specials[0]
    shaped = jax.ShapeDtypeStruct

    tokens, first = pl.pallas_call(
        first_kernel,
        out_shape=[shaped((rows, width), F32), shaped((rows, width), BF16)],
        in_specs=[SMEM] + [VMEM] * 6,
        compiler_params=params(),
        name="first",
    )(info, mask, patches, specials, mask_token, first_gain, first_shift)

    firsts = gather_blocks(first)

    block = pl.BlockSpec((rows, width), lambda i: (i, 0))
    queries, keys, values = pl.pallas_call(
        partial(project_kernel, slots),
        grid=(BANDS,),
        out_shape=[
            shaped((rows, width), BF16),
            shaped((every, width), BF16),
            shaped((every, width), BF16),
        ],
        in_specs=[SMEM, block, whole((width, 3 * width)), VMEM, VMEM],
        out_specs=[whole((rows, width)), block, block],
        compiler_params=params(),
        name="project",
    )(info, firsts, joint_weight, query_bias, value_bias)

    own_pair = pl.BlockSpec((rows, PAIR), lambda i: (0, i))
    all_pair = pl.BlockSpec((every, PAIR), lambda i: (0, i))
    kept = pl.BlockSpec((1, 2 * rows, every), lambda i: (i, 0, 0))
    attended, totals, weights = pl.pallas_call(
        partial(attend_kernel, slots),
        grid=(pairs,),
        out_shape=[
            shaped((rows, width), F32),
            shaped((rows, width), F32),
            shaped((pairs, 2 * rows, every), BF16),
        ],
        in_specs=[SMEM, own_pair, all_pair, all_pair],
        out_specs=[own_pair, own_pair, kept],
        compiler_params=params(),
        name="attend",
    )(info, queries, keys, values)

    branch, middle, second, incoming, down_in, down_bias_grad = pl.pallas_call(
        partial(middle_kernel, slots),
        out_shape=[
            shaped((rows, width), F32),
            shaped((rows, width), F32),
            shaped((rows, width), BF16),
            shaped((rows, width), F32),
            shaped((rows, width), BF16),
            shaped((1, width), F32),
        ],
        in_specs=[SMEM] + [VMEM] * 10,
        out_specs=[VMEM] * 6,
        compiler_params=params(),
        name="middle",
    )(
        info,
        attended,
        tokens,
        out_weight,
        out_bias,
        first_scale,
        second_gain,
        second_shift,
        second_scale,
        cot_patches,
        cot_specials,
    )

    steps = 6
    chunk = hidden_width // steps
    branch_two, second_grad, up_grad, up_bias_grad, down_grad = pl.pallas_call(
        mlp_kernel,
        grid=(steps,),
        out_shape=[
            shaped((rows, width), F32),
            shaped((rows, width), F32),
            shaped((width, hidden_width), BF16),
            shaped((1, hidden_width), F32),
            shaped((hidden_width, width), BF16),
        ],
        in_specs=[
            whole((rows, width)),
            whole((rows, width)),
            pl.BlockSpec((width, chunk), lambda i: (0, i)),
            pl.BlockSpec((1, chunk), lambda i: (0, i)),
            pl.BlockSpec((chunk, width), lambda i: (i, 0)),
        ],
        out_specs=[
            whole((rows, width)),
            whole((rows, width)),
            pl.BlockSpec((width, chunk), lambda i: (0, i)),
            pl.BlockSpec((1, chunk), lambda i: (0, i)),
            pl.BlockSpec((chunk, width), lambda i: (i, 0)),
        ],
        compiler_params=params(),
        name="mlp",
    )(second, down_in, up_weight, up_bias.reshape(1, -1), down_weight)

    out_patches, out_own, middle_grad, attended_grad, out_weight_grad, vectors = pl.pallas_call(
        partial(middle_back_kernel, slots),
        out_shape=[
            shaped((slots, width), BF16),
            shaped((pad, width), F32),
            shaped((rows, width), F32),
            shaped((rows, width), F32),
            shaped((width, width), BF16),
            shaped((8, width), F32),
        ],
        in_specs=[SMEM] + [VMEM] * 11,
        out_specs=[VMEM] * 6,
        compiler_params=params(),
        name="middle_back",
    )(
        info,
        middle,
        branch,
        branch_two,
        second_grad,
        incoming,
        attended,
        out_weight,
        down_bias,
        second_scale,
        second_gain,
        first_scale,
    )

    query_grad, key_grad, value_grad = pl.pallas_call(
        partial(attend_back_kernel, slots),
        grid=(pairs,),
        out_shape=[
            shaped((rows, width), BF16),
            shaped((every, width), BF16),
            shaped((every, width), BF16),
        ],
        in_specs=[SMEM, kept, own_pair, all_pair, all_pair, own_pair, own_pair, own_pair],
        out_specs=[own_pair, all_pair, all_pair],
        compiler_params=params(),
        name="attend_back",
    )(info, weights, queries, keys, values, attended, totals, attended_grad)

    joint_weight_grad, first_part = pl.pallas_call(
        joint_grad_kernel,
        out_shape=[shaped((width, 3 * width), BF16), shaped((every, width), BF16)],
        in_specs=[VMEM] * 5,
        out_specs=[VMEM] * 2,
        compiler_params=params(),
        name="joint_grad",
    )(firsts, query_grad, key_grad, value_grad, joint_weight)

    first_grad = scatter_blocks(first_part)

    grad_patches, grad_own, more_vectors = pl.pallas_call(
        partial(first_back_kernel, slots),
        out_shape=[
            shaped((slots, width), BF16),
            shaped((pad, width), F32),
            shaped((8, width), F32),
        ],
        in_specs=[VMEM] * 7,
        out_specs=[VMEM] * 3,
        compiler_params=params(),
        name="first_back",
    )(first_grad, tokens, middle_grad, mask, first_gain, query_grad, value_grad)

    if lax.axis_size("crop") == 8:
        finished = reduce_all(
            up_grad,
            down_grad,
            out_weight_grad,
            joint_weight_grad,
            vectors,
            more_vectors,
            down_bias_grad,
            up_bias_grad,
            out_own,
            grad_own,
            special_count,
        )
    else:
        finished = reduce_general(
            up_grad,
            down_grad,
            out_weight_grad,
            joint_weight_grad,
            vectors,
            more_vectors,
            down_bias_grad,
            up_bias_grad,
            out_own,
            grad_own,
            special_count,
        )
    up, down, out, joint, rows_of, up_bias_sum, out_specials, grad_specials = finished
    return (
        out_patches[None],
        out_specials,
        grad_patches[None],
        grad_specials,
        rows_of[5],
        rows_of[6],
        rows_of[7],
        joint,
        rows_of[8],
        rows_of[9],
        out,
        rows_of[4],
        rows_of[3],
        rows_of[1],
        rows_of[2],
        up,
        up_bias_sum,
        down,
        rows_of[10],
        rows_of[0],
    )


def solution(mesh):
    split = P("crop", "band", None)
    special = P("crop", None, None)
    in_specs = (
        (split, special, P("crop", "band")) + (P(),) * 17 + (split, special)
    )
    line, matrix = P("crop"), P("crop", None)
    out_specs = (
        split,
        special,
        split,
        special,
        line,
        line,
        line,
        matrix,
        line,
        line,
        matrix,
        line,
        line,
        line,
        line,
        matrix,
        line,
        matrix,
        line,
        line,
    )
    return jax.shard_map(body, mesh=mesh, in_specs=in_specs, out_specs=out_specs, check_vma=False)
```

```python
from functools import partial

import jax
import jax.numpy as jnp
from jax import lax
from jax.experimental import pallas as pl
from jax.experimental.pallas import tpu as pltpu
from jax.sharding import PartitionSpec as P

HEAD = 64
GRID = 37
PAIR = 2 * HEAD
BANDS = 4
KEY_PART = 256
F32 = jnp.float32
BF16 = jnp.bfloat16
VMEM_LIMIT = 60 << 20


def round_up(value, unit):
    return (value + unit - 1) // unit * unit


def params(semantics=None):
    return pltpu.CompilerParams(vmem_limit_bytes=VMEM_LIMIT)


def dot(a, b):
    return jnp.dot(a, b, preferred_element_type=F32)


def dot_nt(a, b):
    return lax.dot_general(a, b, (((1,), (1,)), ((), ())), preferred_element_type=F32)


def dot_tn(a, b):
    return lax.dot_general(a, b, (((0,), (0,)), ((), ())), preferred_element_type=F32)


def normalize(rows):
    centred = rows - jnp.mean(rows, axis=-1, keepdims=True)
    spread = jnp.mean(centred * centred, axis=-1, keepdims=True)
    scale = lax.rsqrt(spread + 1e-06)
    return centred * scale, scale


def normalize_back(grad, hat, scale):
    return scale * (
        grad
        - jnp.mean(grad, axis=-1, keepdims=True)
        - hat * jnp.mean(grad * hat, axis=-1, keepdims=True)
    )


def column_sum(rows):
    return jnp.sum(rows, axis=0, keepdims=True)


def line(ref):
    return ref[...].reshape(1, -1)


def whole(shape):
    return pl.BlockSpec(shape, lambda *_: (0,) * len(shape))


VMEM = pl.BlockSpec(memory_space=pltpu.VMEM)
ANY = pl.BlockSpec(memory_space=pl.ANY)
SMEM = pl.BlockSpec(memory_space=pltpu.SMEM)


def own_special(specials, band, slot):
    row = jnp.zeros((1, specials.shape[1]), F32)
    for special in range(specials.shape[0]):
        if special // BANDS == slot:
            row = row + jnp.where(band == special % BANDS, specials[special : special + 1], 0.0)
    return row


def place_rows(ref, patch_rows, specials, band):
    slots = patch_rows.shape[0]
    rows = ref.shape[0]
    ref[0:slots, :] = patch_rows
    extra = [own_special(specials, band, slot) for slot in range(rows - slots)]
    ref[slots:rows, :] = jnp.concatenate(extra, axis=0)


def counted_rows(info_ref, relative, rows, slots, width):
    index = lax.broadcasted_iota(jnp.int32, (rows, width), 0)
    used = index < info_ref[relative]
    special = (index >= slots) & (index < slots + info_ref[BANDS + relative])
    return used | special


def stack_pair(rows):
    lane = lax.broadcasted_iota(jnp.int32, rows.shape, 1)
    zero = jnp.zeros_like(rows)
    return jnp.concatenate(
        [jnp.where(lane < HEAD, rows, zero), jnp.where(lane >= HEAD, rows, zero)], axis=0
    )


def unstack_pair(rows):
    half = rows.shape[0] // 2
    lane = lax.broadcasted_iota(jnp.int32, (half, rows.shape[1]), 1)
    return jnp.where(lane < HEAD, rows[:half], rows[half:])


def mask_column(mask):
    return jnp.broadcast_to(mask[...].astype(F32), (8, mask.shape[1])).T[:, :1] > 0


def first_kernel(slots, info, mask, patches, specials, token, gain, shift, tokens, first):
    band = info[2 * BANDS]
    filled = jnp.where(mask_column(mask), line(token), patches[...].astype(F32))
    place_rows(tokens, filled, specials[...].astype(F32), band)
    hat, _ = normalize(tokens[...])
    counted = counted_rows(info, 0, tokens.shape[0], slots, tokens.shape[1])
    first[...] = jnp.where(counted, hat * line(gain) + line(shift), 0.0).astype(BF16)


def project_kernel(slots, info, first, weight, query_bias, value_bias, queries, keys, values):
    relative = pl.program_id(0)
    rows, width = queries.shape
    counted = counted_rows(info, relative, rows, slots, width)
    low = first[...]

    @pl.when(relative == 0)
    def _():
        queries[...] = (dot(low, weight[:, :width]) + line(query_bias)).astype(BF16)

    keys[...] = dot(low, weight[:, width : 2 * width]).astype(BF16)
    values[...] = jnp.where(
        counted, dot(low, weight[:, 2 * width :]) + line(value_bias), 0.0
    ).astype(BF16)


def attend_kernel(slots, info, queries, keys, values, attended, totals, weights):
    rows = queries.shape[0]
    factor = HEAD ** (-0.5)
    stacked = stack_pair((queries[...].astype(F32) * factor).astype(BF16))
    scores = dot_nt(stacked, keys[...])
    low = jnp.exp(scores).astype(BF16)
    weights[0] = low
    ones = jnp.concatenate(
        [
            counted_rows(info, r, rows, slots, PAIR).astype(F32).astype(BF16)
            for r in range(BANDS)
        ],
        axis=0,
    )
    summed = dot(low, jnp.concatenate([values[...], ones], axis=1))
    total = unstack_pair(summed[:, PAIR:])
    attended[...] = unstack_pair(summed[:, :PAIR]) / total
    totals[...] = total


def middle_kernel(
    slots,
    info,
    attended,
    tokens,
    weight,
    bias,
    first_scale,
    gain,
    shift,
    second_scale,
    cot_patches,
    cot_specials,
    branch,
    middle,
    second,
    incoming,
    down_in,
    down_keep,
    down_send,
    down_bias_grad,
):
    rows = tokens.shape[0]
    band = info[2 * BANDS]
    side = dot(attended[...].astype(BF16), weight[...]) + line(bias)
    branch[...] = side
    mid = tokens[...] + line(first_scale) * side
    middle[...] = mid
    hat, _ = normalize(mid)
    second[...] = (hat * line(gain) + line(shift)).astype(BF16)
    counted = counted_rows(info, 0, slots, slots, tokens.shape[1])
    given = jnp.where(counted, cot_patches[...].astype(F32), 0.0)
    place_rows(incoming, given, cot_specials[...].astype(F32), band)
    low = (incoming[...] * line(second_scale)).astype(BF16)
    down_in[...] = low
    keep, send = own_half(low, band)
    down_keep[...] = keep
    down_send[...] = send
    down_bias_grad[...] = column_sum(low.astype(F32))


def own_half(rows, band):
    half = rows.shape[1] // 2
    first = lax.rem(band, 2) == 0
    low, high = rows[:, :half], rows[:, half:]
    return jnp.where(first, low, high), jnp.where(first, high, low)


def gelu_and_slope(x):
    phi = 0.5 + 0.5 * lax.erf(x * 0.7071067811865476)
    density = jnp.exp(-0.5 * x * x) * 0.3989422804014327
    return x * phi, phi + x * density


def mlp_kernel(
    info,
    second,
    down_in,
    down_keep,
    down_send,
    up,
    up_bias,
    down,
    branch_two,
    second_grad,
    up_grad_keep,
    up_grad_send,
    up_bias_grad,
    down_grad_keep,
    down_grad_send,
):
    step = pl.program_id(0)
    low = second[...]
    hidden = dot(low, up[...]) + up_bias[...]
    active, slope = gelu_and_slope(hidden)
    active = active.astype(BF16)
    hidden_in = (slope * dot_nt(down_in[...], down[...])).astype(BF16)

    @pl.when(step == 0)
    def _():
        branch_two[...] = jnp.zeros_like(branch_two)
        second_grad[...] = jnp.zeros_like(second_grad)

    branch_two[...] += dot(active, down[...])
    second_grad[...] += dot_nt(hidden_in, up[...])
    keep, send = own_half(hidden_in, info[2 * BANDS])
    up_grad_send[...] = dot_tn(low, send).astype(BF16)
    up_grad_keep[...] = dot_tn(low, keep).astype(BF16)
    down_grad_send[...] = dot_tn(active, down_send[...]).astype(BF16)
    down_grad_keep[...] = dot_tn(active, down_keep[...]).astype(BF16)
    up_bias_grad[...] = column_sum(hidden_in.astype(F32))


def middle_back_kernel(
    slots,
    info,
    middle,
    branch,
    branch_two,
    second_grad,
    incoming,
    attended,
    weight,
    down_bias,
    second_scale,
    gain,
    first_scale,
    out_patches,
    out_specials,
    middle_grad,
    attended_grad,
    out_keep,
    out_send,
    vectors,
):
    rows = middle.shape[0]
    mid = middle[...]
    given = incoming[...]
    two = branch_two[...] + line(down_bias)
    output = mid + line(second_scale) * two
    counted = counted_rows(info, 0, slots, slots, mid.shape[1])
    out_patches[...] = jnp.where(counted, output[:slots], 0.0).astype(BF16)
    out_specials[...] = output[slots:]
    hat, scale = normalize(mid)
    grad = second_grad[...]
    back = given + normalize_back(grad * line(gain), hat, scale)
    middle_grad[...] = back
    out_in = (back * line(first_scale)).astype(BF16)
    attended_grad[...] = dot_nt(out_in, weight[...])
    keep, send = own_half(out_in, info[2 * BANDS])
    low = attended[...].astype(BF16)
    out_keep[...] = dot_tn(low, keep).astype(BF16)
    out_send[...] = dot_tn(low, send).astype(BF16)
    vectors[...] = jnp.concatenate(
        [
            column_sum(given * two),
            column_sum(grad * hat),
            column_sum(grad),
            column_sum(back * branch[...]),
            column_sum(out_in.astype(F32)),
            jnp.zeros((3, mid.shape[1]), F32),
        ],
        axis=0,
    )


def attend_back_pair(weights, queries, keys, values, attended, totals, attended_grad, outs, between):
    query_grad, key_grad, value_grad = outs
    rows = queries.shape[0]
    every = keys.shape[0]
    factor = HEAD ** (-0.5)
    stacked = stack_pair((queries[...].astype(F32) * factor).astype(BF16))
    scaled = attended_grad[...] / totals[...]
    returned = stack_pair(scaled.astype(BF16))
    slope = jnp.sum(stack_pair(scaled * attended[...]), axis=1, keepdims=True)
    stacked_t = stacked.astype(F32).T.astype(BF16)
    returned_t = returned.astype(F32).T.astype(BF16)
    total = jnp.zeros((2 * rows, PAIR), F32)
    for part in range(every // KEY_PART):
        span = slice(part * KEY_PART, (part + 1) * KEY_PART)
        low = weights[0, :, span]
        moved = dot_nt(returned, values[span, :])
        scores = (low.astype(F32) * (moved - slope)).astype(BF16)
        total = total + dot(scores, keys[span, :])
        key_grad[span, :] = dot(stacked_t, scores).T.astype(BF16)
        value_grad[span, :] = dot(returned_t, low).T.astype(BF16)
        between(part)
    query_grad[...] = (unstack_pair(total) * factor).astype(BF16)


def first_part(block, rows, query_grad, key_grad, value_grad, weight):
    width = weight.shape[0]
    span = slice(block * rows, (block + 1) * rows)
    part = jnp.zeros((rows, width), F32)
    for pair in range(0, width // PAIR, 2):
        for offset, grad in ((width, key_grad), (2 * width, value_grad), (0, query_grad)):
            if offset == 0 and block > 0:
                continue
            at = slice(0, rows) if offset == 0 else span
            low = jnp.concatenate([grad[pair, at, :], grad[pair + 1, at, :]], axis=1)
            columns = slice(offset + pair * PAIR, offset + (pair + 2) * PAIR)
            part = part + dot_nt(low, weight[:, columns])
    return part


def joint_columns(firsts, grad):
    low = jnp.concatenate([grad[pair] for pair in range(grad.shape[0])], axis=1)
    return dot_tn(firsts, low).astype(BF16)


def first_back(slots, info, grad, tokens, middle_grad, mask, gain):
    rows, width = tokens.shape
    grad = jnp.where(counted_rows(info, 0, rows, slots, width), grad, 0.0)
    hat, scale = normalize(tokens[...])
    token_grad = middle_grad[...] + normalize_back(grad * line(gain), hat, scale)
    masked = mask_column(mask)
    patch_grad = token_grad[:slots]
    patches = jnp.where(masked, 0.0, patch_grad).astype(BF16)
    vectors = [
        column_sum(jnp.where(masked, patch_grad, 0.0)),
        column_sum(grad * hat),
        column_sum(grad),
    ]
    return patches, token_grad[slots:], vectors


def bias_sums(info, slots, rows, query_grad, value_grad):
    ones = [
        counted_rows(info, block, rows, slots, PAIR).astype(F32).astype(BF16)
        for block in range(BANDS)
    ]
    ones = jnp.concatenate(ones, axis=0)
    pairs = range(query_grad.shape[0])
    queries = [column_sum(query_grad[pair].astype(F32)) for pair in pairs]
    values = [dot_tn(ones, value_grad[pair])[0:1] for pair in pairs]
    both = [jnp.concatenate(queries, axis=1), jnp.concatenate(values, axis=1)]
    return jnp.concatenate(both + [jnp.zeros((6, both[0].shape[1]), F32)], axis=0)


def swap(x, axis, distance):
    size = lax.axis_size(axis)
    return lax.ppermute(x, axis, [(i, i ^ distance) for i in range(size)])


def halve(x, axis, distance):
    bit = (lax.axis_index(axis) // distance) % 2
    sent = lax.dynamic_index_in_dim(x, 1 - bit, 0, keepdims=False)
    kept = lax.dynamic_index_in_dim(x, bit, 0, keepdims=False)
    got = swap(sent, axis, distance)
    return (kept.astype(F32) + got.astype(F32)).astype(BF16)


def reduce_half(kept, got, columns):
    held = (kept.astype(F32) + got.astype(F32)).astype(BF16)
    rows, half = held.shape
    crops = lax.axis_size("crop")
    held = held.reshape((crops, rows // crops, half))
    distance = 1
    while distance < crops:
        count = held.shape[0]
        held = jnp.moveaxis(held.reshape((count // 2, 2) + held.shape[1:]), 1, 0)
        held = halve(held, "crop", distance)
        distance *= 2
    held = held.reshape((rows // crops, half))
    other = swap(held, "band", 2)
    full = (held.astype(F32) + other.astype(F32)).astype(BF16)
    mate = swap(full, "band", 1)
    bit = lax.axis_index("band") % 2
    low = jnp.where(bit == 0, full, mate).astype(F32).reshape(rows // crops, -1, columns)
    high = jnp.where(bit == 0, mate, full).astype(F32).reshape(rows // crops, -1, columns)
    return jnp.stack([low, high], axis=2).reshape(rows // crops, 2 * half)


def gather_blocks(x):
    near = swap(x, "band", 1)
    far = swap(x, "band", 2)
    diagonal = swap(far, "band", 1)
    return jnp.concatenate([x, near, far, diagonal], axis=0)


def scatter_blocks(x):
    rows = x.shape[0] // BANDS
    got = swap(jnp.concatenate([x[rows : 2 * rows], x[3 * rows :]], axis=0), "band", 1)
    own = x[:rows].astype(F32) + got[:rows].astype(F32)
    far = (x[2 * rows : 3 * rows].astype(F32) + got[rows:].astype(F32)).astype(BF16)
    return own + swap(far, "band", 2).astype(F32)


def reduce_small(vectors, more, down_bias, up_bias, out_own, grad_own, special_count):
    crops = lax.axis_size("crop")
    width = vectors.shape[1]
    owned = -(-special_count // BANDS)
    both = jnp.concatenate([out_own[:owned], grad_own[:owned]], axis=1).astype(BF16)
    both = lax.all_gather(both, "band", axis=0, tiled=False)
    both = jnp.transpose(both, (1, 0, 2)).reshape(owned * BANDS, 2 * width)[:special_count]
    plain = jnp.concatenate([vectors[:5], more[:5], down_bias], axis=0)
    plain = jnp.transpose(plain.reshape(11, crops, -1), (1, 0, 2)).reshape(crops, -1)
    packed = jnp.concatenate([plain, up_bias.reshape(crops, -1)], axis=1)
    packed = lax.psum_scatter(packed, "crop", scatter_dimension=0, tiled=False)
    packed = lax.psum(packed, "band")
    part = width // crops
    rows = [packed[i * part : (i + 1) * part] for i in range(11)]
    return rows, packed[11 * part :], both[None, :, :width], both[None, :, width:]


def attend_back_kernel(
    weights, queries, keys, values, attended, totals, attended_grad, query_grad, key_grad, value_grad
):
    outs = (query_grad.at[0], key_grad.at[0], value_grad.at[0])
    inputs = (weights, queries, keys, values, attended, totals, attended_grad)
    attend_back_pair(*inputs, outs, lambda part: None)


def joint_back_kernel(
    slots, info, firsts, query_grad, key_grad, value_grad, weight, joint_keep, joint_send, first_grad, sums
):
    rows, width = query_grad.shape[1], weight.shape[0]
    for block in range(BANDS):
        part = first_part(block, rows, query_grad, key_grad, value_grad, weight)
        first_grad[block * rows : (block + 1) * rows, :] = part.astype(BF16)
    half = width // 2
    for part, grad in enumerate((query_grad, key_grad, value_grad)):
        low = firsts[0:rows, :] if part == 0 else firsts[...]
        keep, send = own_half(joint_columns(low, grad), info[2 * BANDS])
        joint_keep[:, part * half : (part + 1) * half] = keep
        joint_send[:, part * half : (part + 1) * half] = send
    sums[...] = bias_sums(info, slots, rows, query_grad, value_grad)


def first_back_kernel(
    slots, info, first_grad, tokens, middle_grad, mask, gain, sums, patches, specials, vectors
):
    grads, special_grad, rows = first_back(
        slots, info, first_grad[...], tokens, middle_grad, mask, gain
    )
    patches[...] = grads
    specials[...] = special_grad
    vectors[...] = jnp.concatenate(rows + [sums[0:5]], axis=0)


def backward_general(given, slots, special_count):
    g = given
    rows, width = g["tokens"].shape
    every = BANDS * rows
    pairs = width // PAIR
    shaped = jax.ShapeDtypeStruct
    own_pair = pl.BlockSpec((rows, PAIR), lambda i: (0, i))
    all_pair = pl.BlockSpec((every, PAIR), lambda i: (0, i))
    grads = pl.pallas_call(
        attend_back_kernel,
        grid=(pairs,),
        out_shape=[
            shaped((pairs, rows, PAIR), BF16),
            shaped((pairs, every, PAIR), BF16),
            shaped((pairs, every, PAIR), BF16),
        ],
        in_specs=[
            pl.BlockSpec((1, 2 * rows, every), lambda i: (i, 0, 0)),
            own_pair,
            all_pair,
            all_pair,
            own_pair,
            own_pair,
            own_pair,
        ],
        out_specs=[
            pl.BlockSpec((1, rows, PAIR), lambda i: (i, 0, 0)),
            pl.BlockSpec((1, every, PAIR), lambda i: (i, 0, 0)),
            pl.BlockSpec((1, every, PAIR), lambda i: (i, 0, 0)),
        ],
        compiler_params=params(),
        name="attend_back",
    )(
        g["weights"],
        g["queries"],
        g["keys"],
        g["values"],
        g["attended"],
        g["totals"],
        g["attended_grad"],
    )
    half = width // 2
    joint_keep, joint_send, parts, sums = pl.pallas_call(
        partial(joint_back_kernel, slots),
        out_shape=[
            shaped((width, 3 * half), BF16),
            shaped((width, 3 * half), BF16),
            shaped((every, width), BF16),
            shaped((8, width), F32),
        ],
        in_specs=[SMEM] + [VMEM] * 5,
        out_specs=[VMEM] * 4,
        compiler_params=params(),
        name="joint_back",
    )(g["info"], g["firsts"], *grads, g["joint_weight"])
    grad_patches, grad_own, more = pl.pallas_call(
        partial(first_back_kernel, slots),
        out_shape=[
            shaped((slots, width), BF16),
            shaped((rows - slots, width), F32),
            shaped((8, width), F32),
        ],
        in_specs=[SMEM] + [VMEM] * 6,
        out_specs=[VMEM] * 3,
        compiler_params=params(),
        name="first_back",
    )(
        g["info"],
        scatter_blocks(parts),
        g["tokens"],
        g["middle_grad"],
        g["mask"],
        g["first_gain"],
        sums,
    )
    small = reduce_small(
        g["vectors"],
        more,
        g["down_bias_grad"],
        g["up_bias_grad"],
        g["out_own"],
        grad_own,
        special_count,
    )
    matrices = (
        reduce_half(g["up_keep"], g["up_got"], half),
        reduce_half(g["down_keep"], g["down_got"], half),
        reduce_half(g["out_keep"], swap(g["out_send"], "band", 1), half),
        reduce_half(joint_keep, swap(joint_send, "band", 1), half),
    )
    return (grad_patches,) + matrices + small


MESH = pl.DeviceIdType.MESH
CROPS = 8
X_FIRST = (0, 2, 4, 6, 10)
NEIGHBOURS = ("core", "x", "diagonal")
PLACES = NEIGHBOURS + tuple(range(1, CROPS))


class Place:
    def __init__(self):
        band, crop = lax.axis_index("band"), lax.axis_index("crop")
        self.band = band
        self.core, self.x = lax.rem(band, 2), lax.div(band, 2)
        self.y, self.near, self.far = lax.rem(crop, 2), lax.rem(lax.div(crop, 2), 2), lax.div(crop, 4)
        core_step, x_step = 1 - 2 * self.core, 2 - 4 * self.x
        self.device = {
            "core": (band + core_step, crop),
            "x": (band + x_step, crop),
            "diagonal": (band + core_step + x_step, crop),
            "y": (band, crop + 1 - 2 * self.y),
            "near": (band, crop + 2 - 4 * self.near),
            "far": (band, crop + 4 - 8 * self.far),
        }
        self.crop = crop
        for step in range(1, CROPS):
            self.device[step] = (band, lax.rem(crop + step, CROPS))

    def greet(self, names):
        barrier = pltpu.get_barrier_semaphore()
        for name in names:
            pl.semaphore_signal(barrier, inc=1, device_id=self.device[name], device_id_type=MESH)
        pl.semaphore_wait(barrier, len(names))


class Sender:
    def __init__(self, place, send_sems, recv_sems):
        self.place, self.send_sems, self.recv_sems = place, send_sems, recv_sems
        self.routes = {}

    def add(self, key, source, target, name):
        self.routes[key] = (len(self.routes), source, target, name)

    def copy(self, key):
        index, source, target, name = self.routes[key]
        return pltpu.make_async_remote_copy(
            src_ref=source,
            dst_ref=target,
            send_sem=self.send_sems.at[index],
            recv_sem=self.recv_sems.at[index],
            device_id=self.place.device[name],
            device_id_type=MESH,
        )

    def send(self, key):
        self.copy(key).start()

    def arrived(self, key):
        self.copy(key).wait_recv()

    def finish(self):
        for key in self.routes:
            self.copy(key).wait_send()


def chunk_list(hidden_parts):
    chunks = []
    for part in range(hidden_parts):
        chunks += [("down", part), ("up", part)]
    return chunks + [("out", 0), ("joint", 0), ("joint", 1), ("joint", 2)]


def chunk_scratch(count, rows, columns):
    unit = (rows, columns)
    return [
        pltpu.VMEM((count, 2, 2, 2, 2) + unit, BF16),
        pltpu.VMEM((count, 2, 2, 2) + unit, BF16),
        pltpu.VMEM((count, 2, 2) + unit, BF16),
        pltpu.VMEM((count, 2) + unit, BF16),
        pltpu.VMEM((count, 2) + unit, BF16),
    ]


class ChunkSums:
    def __init__(self, place, sender, buffers, total, count):
        p, self.sender = place, sender
        own, got_a, got_b, got_c, got_d = buffers
        self.table = {}
        for n in range(count):
            if x_first(n):
                half = total.at[n, p.core, p.x]
                rows = [
                    (None, None, own.at[n, 1 - p.x], got_a.at[n], "x"),
                    (own.at[n, p.x], got_a.at[n], own.at[n, p.x, :, :, 1 - p.y], got_b.at[n], "y"),
                    (
                        own.at[n, p.x, :, :, p.y],
                        got_b.at[n],
                        own.at[n, p.x, :, 1 - p.near, p.y],
                        got_c.at[n],
                        "near",
                    ),
                    (
                        own.at[n, p.x, :, p.near, p.y],
                        got_c.at[n],
                        own.at[n, p.x, 1 - p.far, p.near, p.y],
                        got_d.at[n, 0],
                        "far",
                    ),
                    (own.at[n, p.x, p.far, p.near, p.y], got_d.at[n, 0], half, half, "x"),
                    (None, None, total.at[n, p.core], total.at[n, p.core], "core"),
                ]
                last = half
            else:
                half = total.at[n, p.core]
                rows = [
                    (None, None, own.at[n, :, :, 1 - p.y], got_a.at[n], "y"),
                    (
                        own.at[n, :, :, p.y],
                        got_a.at[n],
                        own.at[n, :, 1 - p.near, p.y],
                        got_b.at[n],
                        "near",
                    ),
                    (
                        own.at[n, :, p.near, p.y],
                        got_b.at[n],
                        own.at[n, 1 - p.far, p.near, p.y],
                        got_c.at[n],
                        "far",
                    ),
                    (
                        own.at[n, p.far, p.near, p.y],
                        got_c.at[n],
                        own.at[n, p.far, p.near, p.y],
                        got_d.at[n],
                        "x",
                    ),
                    (own.at[n, p.far, p.near, p.y], got_d.at[n], half, half, "core"),
                ]
                last = half
            self.table[n] = rows
            for stage, (_, _, source, target, name) in enumerate(rows):
                sender.add((n, stage + 1), source, target, name)
            self.table[n, "last"] = last

    def steps(self, n):
        return len(self.table[n]) + 1

    def step(self, n, stage):
        if stage > 0:
            self.sender.arrived((n, stage))
        if stage == len(self.table[n]):
            return
        into, got, source, target, _ = self.table[n][stage]
        if into is not None:
            place = self.table[n, "last"] if source is target else into
            place[...] = into[...] + got[...]
        self.sender.send((n, stage + 1))


class VectorSums:
    def __init__(self, place, sender, buffers, total):
        self.place, self.sender, self.total = place, sender, total
        self.own, self.got, self.parts = buffers
        for step in range(1, CROPS):
            source = self.own.at[lax.rem(place.crop + step, CROPS)]
            sender.add(("vector", step), source, self.got.at[place.crop], step)
        here = self.parts.at[place.band]
        for name in NEIGHBOURS:
            sender.add(("parts", name), here, here, name)

    def spread(self):
        for step in range(1, CROPS):
            self.sender.send(("vector", step))

    def share(self):
        p = self.place
        self.got[p.crop] = self.own[p.crop]
        for step in range(1, CROPS):
            self.sender.arrived(("vector", step))
        self.parts[p.band] = jnp.sum(self.got[...], axis=0)
        for name in NEIGHBOURS:
            self.sender.send(("parts", name))

    def close(self):
        for name in NEIGHBOURS:
            self.sender.arrived(("parts", name))
        self.total[...] = jnp.sum(self.parts[...], axis=0)


def pack_vectors(own, rows, up_bias, part):
    for crop in range(CROPS):
        span = slice(crop * part, (crop + 1) * part)
        wide = 4 * crop * part
        wider = [up_bias[0:1, wide + j * part : wide + (j + 1) * part] for j in range(4)]
        own[crop, 0:15, 0:part] = jnp.concatenate([rows[:, span]] + wider, axis=0)


def vector_scratch():
    return [
        pltpu.VMEM((CROPS, 16, 128), F32),
        pltpu.VMEM((CROPS, 16, 128), F32),
        pltpu.VMEM((BANDS, 16, 128), F32),
    ]


def x_first(n):
    return n in X_FIRST


def halves_of(n):
    return (0, 1) if x_first(n) else (None,)


def part_of(ref, name, part, columns, x_half):
    at = slice(None) if x_half is None else x_half
    if name == "down":
        return ref.at[:, :, :, part, at]
    return ref.at[:, :, :, at, :, pl.ds(part * columns, columns)]


def piece(ref, x_half):
    return ref if x_half is None else ref.at[x_half]


PACE = 8.0
LAGS = (0.0, 13.0, 17.0, 20.5, 23.0, 25.5, 28.0)
SLOT = 0.65


def backward_kernel(
    chunks,
    slots,
    pairs,
    info,
    weights,
    queries,
    keys,
    values,
    attended,
    totals,
    attended_grad,
    mask,
    gain,
    vectors,
    down_bias,
    up_bias,
    out_own,
    up_keep,
    up_got,
    down_keep,
    down_got,
    out_keep,
    out_send,
    firsts_in,
    weight_in,
    tokens_in,
    middle_grad_in,
    grad_patches,
    total_out,
    vector_total,
    specials_out,
    *scratch,
):
    buffers, vector_buffers = scratch[:5], scratch[5:8]
    (
        total,
        out_got,
        joint_got,
        joint_sent,
        loaded,
        query_grad,
        key_grad,
        value_grad,
        firsts,
        weight,
        tokens,
        middle_grad,
        parts,
        got_parts,
        got_far,
        specials,
        send_sems,
        recv_sems,
        load_sems,
        whole_sems,
    ) = scratch[8:]
    step = pl.program_id(0)
    count = len(chunks)
    columns = total.shape[4]
    rows, width = tokens.shape
    place = Place()
    sender = Sender(place, send_sems, recv_sems)
    sums = ChunkSums(place, sender, buffers, total, count)
    vector_sums = VectorSums(place, sender, vector_buffers, vector_total)
    own = buffers[0]
    keeps = dict(up=up_keep, down=down_keep, out=out_keep)
    gots = dict(up=up_got, down=down_got)

    def own_loads(n):
        name, part = chunks[n]
        return [
            pltpu.make_async_copy(
                part_of(keeps[name], name, part, columns, h), piece(own.at[n], h), load_sems.at[n, 0, i]
            )
            for i, h in enumerate(halves_of(n))
        ]

    def got_loads(n):
        name, part = chunks[n]
        return [
            pltpu.make_async_copy(
                part_of(gots[name], name, part, columns, h), piece(loaded.at[n % 2], h), load_sems.at[n, 1, i]
            )
            for i, h in enumerate(halves_of(n))
        ]

    def whole_loads():
        pairs_of = ((weight_in, weight), (firsts_in, firsts), (tokens_in, tokens), (middle_grad_in, middle_grad))
        return [
            pltpu.make_async_copy(a, b, whole_sems.at[i]) for i, (a, b) in enumerate(pairs_of)
        ]

    early = [n for n, (name, _) in enumerate(chunks) if name != "joint"]
    mlp = [n for n in early if chunks[n][0] != "out"]
    out_chunk = early[-1]
    late = [n for n, (name, _) in enumerate(chunks) if name == "joint"]

    for h in halves_of(out_chunk):
        source = part_of(out_send, "out", 0, columns, h)
        sender.add((out_chunk, 0, h), source, piece(out_got, h), "core")
    for n in late:
        sender.add((n, 0), joint_sent.at[n - late[0]], joint_got.at[n - late[0]], "core")
    for index in range(2):
        sender.add(("first", index), parts.at[index], got_parts.at[index], "core")
    sender.add("far", parts.at[2], got_far, "x")
    for name in NEIGHBOURS:
        sender.add(("special", name), specials.at[place.band], specials.at[place.band], name)

    def begin():
        for n in early:
            for copy in own_loads(n):
                copy.start()
        for n in mlp[:2]:
            for copy in got_loads(n):
                copy.start()
        place.greet(PLACES)
        for h in halves_of(out_chunk):
            sender.send((out_chunk, 0, h))

    def early_stage(n, stage):
        if stage == 0:
            for copy in own_loads(n):
                copy.wait()
            if n in mlp:
                for copy in got_loads(n):
                    copy.wait()
                own[n] = own[n] + loaded[n % 2]
                if n + 2 in mlp:
                    for copy in got_loads(n + 2):
                        copy.start()
            else:
                for h in halves_of(n):
                    sender.arrived((n, 0, h))
                own[n] = own[n] + out_got[...]
        sums.step(n, stage)

    def late_stage(n, stage):
        if stage == 0:
            sender.arrived((n, 0))
            own[n] = own[n] + joint_got[n - late[0]]
        sums.step(n, stage)

    events = []
    for n in early:
        for stage in range(sums.steps(n)):
            events.append((PACE * (n // 2) + LAGS[stage] + 0.3 * (n % 2), stage, n))
    events.sort()

    @pl.when(step == 0)
    def _():
        begin()

    slots_per_pair = BANDS * rows // KEY_PART
    plan = {}
    rest = list(events)
    for index in range(pairs * slots_per_pair):
        due = [e for e in rest if e[0] <= SLOT * (index + 1)]
        rest = rest[len(due) :]
        if due:
            plan[index] = due

    def slot(part):
        for pair in range(pairs):
            index = pair * slots_per_pair + part
            if index not in plan:
                continue

            @pl.when(step == pair)
            def _():
                for _, stage, n in plan[index]:
                    early_stage(n, stage)

    @pl.when(step < pairs)
    def _():
        pair = jnp.minimum(step, pairs - 1)
        outs = (query_grad.at[pair], key_grad.at[pair], value_grad.at[pair])
        inputs = (weights, queries, keys, values, attended, totals, attended_grad)
        attend_back_pair(*inputs, outs, slot)

    @pl.when(step == 1)
    def _():
        for copy in whole_loads():
            copy.start()

    @pl.when(step == pairs)
    def _():
        waiting = list(rest)

        def catch_up(time):
            while waiting and waiting[0][0] <= time:
                _, stage, n = waiting.pop(0)
                early_stage(n, stage)

        now = SLOT * pairs * slots_per_pair
        for copy in whole_loads():
            copy.wait()
        grads = (query_grad, key_grad, value_grad)
        for index, block in enumerate((1, 3)):
            parts[index] = first_part(block, rows, *grads, weight).astype(BF16)
            sender.send(("first", index))
            now += 1.2
            catch_up(now)
        parts[2] = first_part(2, rows, *grads, weight).astype(BF16)
        sender.arrived(("first", 1))
        parts[2] = parts[2] + got_parts[1]
        sender.send("far")
        now += 1.2
        catch_up(now)
        for n in (late[1], late[2], late[0]):
            part = chunks[n][1]
            low = firsts[0:rows, :] if part == 0 else firsts[...]
            keep, send = own_half(joint_columns(low, grads[part]), place.band)
            shape = (2, 2, 2, 2, width // CROPS // 2, columns)
            keep, send = keep.reshape(shape), send.reshape(shape)
            for h in halves_of(n):
                picked = send if h is None else send[:, :, :, h]
                kept = keep if h is None else keep[:, :, :, h]
                if h is None:
                    joint_sent[n - late[0]] = picked
                    own[n] = kept
                else:
                    joint_sent[n - late[0], h] = picked
                    own[n, h] = kept
            sender.send((n, 0))
            now += 2.5
            catch_up(now)
        first_grad = first_part(0, rows, *grads, weight)
        biases = bias_sums(info, slots, rows, query_grad, value_grad)
        for n in (late[1], late[2], late[0]):
            late_stage(n, 0)
        now += 2.5
        catch_up(now)
        start = now
        for n in late:
            for stage in range(1, sums.steps(n)):
                lag = start + 6.0 + 3.0 * stage + (3.0 if n == late[2] else 0.0)
                waiting.append((lag, stage, n))
        waiting.sort()

        def finish_until(time):
            while waiting and waiting[0][0] <= time:
                _, stage, n = waiting.pop(0)
                (late_stage if n in late else early_stage)(n, stage)

        finish_until(start + FIRST_LAG)
        sender.arrived(("first", 0))
        sender.arrived("far")
        first_grad = first_grad + got_parts[0].astype(F32) + got_far[...].astype(F32)
        patches, special_grad, rows_of = first_back(
            slots, info, first_grad, tokens, middle_grad, mask, gain
        )
        grad_patches[...] = patches
        specials[place.band] = jnp.concatenate([out_own[0:4], special_grad[0:4]], axis=0)
        for name in NEIGHBOURS:
            sender.send(("special", name))
        packed = jnp.concatenate([vectors[0:5]] + rows_of + [biases[0:2], down_bias[...]], axis=0)
        pack_vectors(vector_sums.own, packed, up_bias, width // CROPS)
        vector_sums.spread()
        finish_until(start + FIRST_LAG + 8.0)
        vector_sums.share()
        finish_until(start + FIRST_LAG + 12.0)
        vector_sums.close()
        finish_until(1e9)
        for name in NEIGHBOURS:
            sender.arrived(("special", name))
        specials_out[...] = specials[...]
        sender.finish()
        copy = pltpu.make_async_copy(total, total_out, whole_sems.at[4])
        copy.start()
        copy.wait()


FIRST_LAG = 8.0


def finish_kernel(
    chunks,
    special_count,
    total,
    vector_total,
    specials,
    up,
    down,
    out,
    joint,
    up_bias,
    out_specials,
    grad_specials,
    *vectors,
):
    _, _, _, rows, columns = total.shape
    refs = dict(up=up, down=down, out=out, joint=joint)
    for n, (name, part) in enumerate(chunks):
        for core in range(2):
            for x in range(2):
                row, column = x * rows, core * columns
                if name == "down":
                    row += 2 * rows * part
                else:
                    column += 2 * columns * part
                value = total[n, core, x].astype(F32)
                refs[name][row : row + rows, column : column + columns] = value
    part = vectors[0].shape[0]
    for i, vector in enumerate(vectors):
        vector[...] = vector_total[i, 0:part]
    up_bias[...] = jnp.concatenate([vector_total[i : i + 1, 0:part] for i in range(11, 15)], axis=1)[0]
    for first, target in ((0, out_specials), (4, grad_specials)):
        picked = [
            specials[s % BANDS, first + s // BANDS : first + s // BANDS + 1]
            for s in range(special_count)
        ]
        target[0] = jnp.concatenate(picked, axis=0).astype(BF16)


def backward_fused(given, slots, special_count):
    g = given
    rows, width = g["tokens"].shape
    hidden_width = g["up_bias_grad"].shape[1]
    every = BANDS * rows
    pairs = width // PAIR
    chunks = chunk_list(hidden_width // width)
    count = len(chunks)
    part = width // CROPS
    unit_rows, columns = part // 2, width // 2
    unit = (2, 2, 2, 2, unit_rows, columns)
    hidden_parts = hidden_width // width
    shaped = jax.ShapeDtypeStruct
    last = pairs - 1
    own_pair = pl.BlockSpec((rows, PAIR), lambda i: (0, jnp.minimum(i, last)))
    all_pair = pl.BlockSpec((every, PAIR), lambda i: (0, jnp.minimum(i, last)))
    kept = pl.BlockSpec((1, 2 * rows, every), lambda i: (jnp.minimum(i, last), 0, 0))
    up_shape = (2, 2, 2, 2, unit_rows, hidden_parts * columns)
    down_shape = (2, 2, 2, hidden_parts, 2, unit_rows, columns)
    grad_patches, total, vector_total, specials = pl.pallas_call(
        partial(backward_kernel, chunks, slots, pairs),
        grid=(pairs + 1,),
        out_shape=[
            shaped((slots, width), BF16),
            shaped((count, 2, 2, unit_rows, columns), BF16),
            shaped((16, 128), F32),
            shaped((BANDS, 8, width), F32),
        ],
        in_specs=[SMEM, kept, own_pair, all_pair, all_pair, own_pair, own_pair, own_pair]
        + [VMEM] * 6
        + [ANY] * 10,
        out_specs=[VMEM, ANY, VMEM, VMEM],
        scratch_shapes=chunk_scratch(count, unit_rows, columns)
        + vector_scratch()
        + [
            pltpu.VMEM((count, 2, 2, unit_rows, columns), BF16),
            pltpu.VMEM(unit, BF16),
            pltpu.VMEM((3,) + unit, BF16),
            pltpu.VMEM((3,) + unit, BF16),
            pltpu.VMEM((2,) + unit, BF16),
            pltpu.VMEM((pairs, rows, PAIR), BF16),
            pltpu.VMEM((pairs, every, PAIR), BF16),
            pltpu.VMEM((pairs, every, PAIR), BF16),
            pltpu.VMEM((every, width), BF16),
            pltpu.VMEM((width, 3 * width), BF16),
            pltpu.VMEM((rows, width), F32),
            pltpu.VMEM((rows, width), F32),
            pltpu.VMEM((3, rows, width), BF16),
            pltpu.VMEM((2, rows, width), BF16),
            pltpu.VMEM((rows, width), BF16),
            pltpu.VMEM((BANDS, 8, width), F32),
            pltpu.SemaphoreType.DMA((10 * count,)),
            pltpu.SemaphoreType.DMA((10 * count,)),
            pltpu.SemaphoreType.DMA((count, 2, 2)),
            pltpu.SemaphoreType.DMA((5,)),
        ],
        compiler_params=pltpu.CompilerParams(
            vmem_limit_bytes=VMEM_LIMIT, collective_id=0, has_side_effects=True
        ),
        name="backward",
    )(
        g["info"],
        g["weights"],
        g["queries"],
        g["keys"],
        g["values"],
        g["attended"],
        g["totals"],
        g["attended_grad"],
        g["mask"],
        g["first_gain"],
        g["vectors"],
        g["down_bias_grad"],
        g["up_bias_grad"],
        g["out_own"],
        g["up_keep"].reshape(up_shape),
        g["up_got"].reshape(up_shape),
        g["down_keep"].reshape(down_shape),
        g["down_got"].reshape(down_shape),
        g["out_keep"].reshape(unit),
        g["out_send"].reshape(unit),
        g["firsts"],
        g["joint_weight"],
        g["tokens"],
        g["middle_grad"],
    )
    special = shaped((1, special_count, width), BF16)
    results = pl.pallas_call(
        partial(finish_kernel, chunks, special_count),
        out_shape=[
            shaped((part, hidden_width), F32),
            shaped((hidden_width // CROPS, width), F32),
            shaped((part, width), F32),
            shaped((part, 3 * width), F32),
            shaped((hidden_width // CROPS,), F32),
            special,
            special,
        ]
        + [shaped((part,), F32)] * 11,
        in_specs=[VMEM] * 3,
        out_specs=[VMEM] * 18,
        compiler_params=params(),
        name="finish",
    )(total, vector_total, specials)
    up, down, out, joint, up_bias, out_specials, grad_specials = results[:7]
    return grad_patches, up, down, out, joint, results[7:], up_bias, out_specials, grad_specials


def body(
    patches,
    specials,
    patch_mask,
    band_rows,
    mask_token,
    first_gain,
    first_shift,
    joint_weight,
    query_bias,
    value_bias,
    out_weight,
    out_bias,
    first_scale,
    second_gain,
    second_shift,
    up_weight,
    up_bias,
    down_weight,
    down_bias,
    second_scale,
    cot_patches,
    cot_specials,
):
    slots, width = patches.shape[1:]
    special_count = specials.shape[1]
    hidden_width = up_weight.shape[1]
    owned = -(-special_count // BANDS)
    rows = round_up(slots + owned, 16)
    pad = rows - slots
    every = BANDS * rows
    pairs = width // PAIR
    band = lax.axis_index("band")
    relatives = [band ^ r for r in range(BANDS)]
    info = jnp.stack(
        [band_rows[b] * GRID for b in relatives]
        + [(special_count - b + BANDS - 1) // BANDS for b in relatives]
        + [band]
    ).astype(jnp.int32)
    mask = patch_mask
    patches, specials = patches[0], specials[0]
    cot_patches, cot_specials = cot_patches[0], cot_specials[0]
    shaped = jax.ShapeDtypeStruct

    tokens, first = pl.pallas_call(
        partial(first_kernel, slots),
        out_shape=[shaped((rows, width), F32), shaped((rows, width), BF16)],
        in_specs=[SMEM] + [VMEM] * 6,
        compiler_params=params(),
        name="first",
    )(info, mask, patches, specials, mask_token, first_gain, first_shift)

    firsts = gather_blocks(first)

    block = pl.BlockSpec((rows, width), lambda i: (i, 0))
    queries, keys, values = pl.pallas_call(
        partial(project_kernel, slots),
        grid=(BANDS,),
        out_shape=[
            shaped((rows, width), BF16),
            shaped((every, width), BF16),
            shaped((every, width), BF16),
        ],
        in_specs=[SMEM, block, whole((width, 3 * width)), VMEM, VMEM],
        out_specs=[whole((rows, width)), block, block],
        compiler_params=params(),
        name="project",
    )(info, firsts, joint_weight, query_bias, value_bias)

    own_pair = pl.BlockSpec((rows, PAIR), lambda i: (0, i))
    all_pair = pl.BlockSpec((every, PAIR), lambda i: (0, i))
    kept = pl.BlockSpec((1, 2 * rows, every), lambda i: (i, 0, 0))
    attended, totals, weights = pl.pallas_call(
        partial(attend_kernel, slots),
        grid=(pairs,),
        out_shape=[
            shaped((rows, width), F32),
            shaped((rows, width), F32),
            shaped((pairs, 2 * rows, every), BF16),
        ],
        in_specs=[SMEM, own_pair, all_pair, all_pair],
        out_specs=[own_pair, own_pair, kept],
        compiler_params=params(),
        name="attend",
    )(info, queries, keys, values)

    branch, middle, second, incoming, down_in, down_keep, down_send, down_bias_grad = pl.pallas_call(
        partial(middle_kernel, slots),
        out_shape=[
            shaped((rows, width), F32),
            shaped((rows, width), F32),
            shaped((rows, width), BF16),
            shaped((rows, width), F32),
            shaped((rows, width), BF16),
            shaped((rows, width // 2), BF16),
            shaped((rows, width // 2), BF16),
            shaped((1, width), F32),
        ],
        in_specs=[SMEM] + [VMEM] * 10,
        out_specs=[VMEM] * 8,
        compiler_params=params(),
        name="middle",
    )(
        info,
        attended,
        tokens,
        out_weight,
        out_bias,
        first_scale,
        second_gain,
        second_shift,
        second_scale,
        cot_patches,
        cot_specials,
    )

    steps = hidden_width // width
    half = width // 2
    (
        branch_two,
        second_grad,
        up_keep,
        up_send,
        up_bias_grad,
        down_grad_keep,
        down_grad_send,
    ) = pl.pallas_call(
        mlp_kernel,
        grid=(steps,),
        out_shape=[
            shaped((rows, width), F32),
            shaped((rows, width), F32),
            shaped((width, hidden_width // 2), BF16),
            shaped((width, hidden_width // 2), BF16),
            shaped((1, hidden_width), F32),
            shaped((hidden_width, half), BF16),
            shaped((hidden_width, half), BF16),
        ],
        in_specs=[
            SMEM,
            whole((rows, width)),
            whole((rows, width)),
            whole((rows, half)),
            whole((rows, half)),
            pl.BlockSpec((width, width), lambda i: (0, i)),
            pl.BlockSpec((1, width), lambda i: (0, i)),
            pl.BlockSpec((width, width), lambda i: (i, 0)),
        ],
        out_specs=[
            whole((rows, width)),
            whole((rows, width)),
            pl.BlockSpec((width, half), lambda i: (0, i)),
            pl.BlockSpec((width, half), lambda i: (0, i)),
            pl.BlockSpec((1, width), lambda i: (0, i)),
            pl.BlockSpec((width, half), lambda i: (i, 0)),
            pl.BlockSpec((width, half), lambda i: (i, 0)),
        ],
        compiler_params=params(),
        name="mlp",
    )(info, second, down_in, down_keep, down_send, up_weight, up_bias.reshape(1, -1), down_weight)
    up_got = swap(up_send, "band", 1)
    down_got = swap(down_grad_send, "band", 1)

    out_patches, out_own, middle_grad, attended_grad, out_keep, out_send, vectors = pl.pallas_call(
        partial(middle_back_kernel, slots),
        out_shape=[
            shaped((slots, width), BF16),
            shaped((pad, width), F32),
            shaped((rows, width), F32),
            shaped((rows, width), F32),
            shaped((width, half), BF16),
            shaped((width, half), BF16),
            shaped((8, width), F32),
        ],
        in_specs=[SMEM] + [VMEM] * 11,
        out_specs=[VMEM] * 7,
        compiler_params=params(),
        name="middle_back",
    )(
        info,
        middle,
        branch,
        branch_two,
        second_grad,
        incoming,
        attended,
        out_weight,
        down_bias,
        second_scale,
        second_gain,
        first_scale,
    )

    given = dict(
        info=info,
        weights=weights,
        queries=queries,
        keys=keys,
        values=values,
        attended=attended,
        totals=totals,
        attended_grad=attended_grad,
        mask=mask,
        first_gain=first_gain,
        vectors=vectors,
        down_bias_grad=down_bias_grad,
        up_bias_grad=up_bias_grad,
        out_own=out_own,
        up_keep=up_keep,
        up_got=up_got,
        down_keep=down_grad_keep,
        down_got=down_got,
        out_keep=out_keep,
        out_send=out_send,
        firsts=firsts,
        joint_weight=joint_weight,
        tokens=tokens,
        middle_grad=middle_grad,
    )
    backward = backward_fused if lax.axis_size("crop") == CROPS else backward_general
    (
        grad_patches,
        up,
        down,
        out,
        joint,
        rows_of,
        up_bias_sum,
        out_specials,
        grad_specials,
    ) = backward(given, slots, special_count)
    return (
        out_patches[None],
        out_specials,
        grad_patches[None],
        grad_specials,
        rows_of[5],
        rows_of[6],
        rows_of[7],
        joint,
        rows_of[8],
        rows_of[9],
        out,
        rows_of[4],
        rows_of[3],
        rows_of[1],
        rows_of[2],
        up,
        up_bias_sum,
        down,
        rows_of[10],
        rows_of[0],
    )


def solution(mesh):
    split = P("crop", "band", None)
    special = P("crop", None, None)
    in_specs = (
        (split, special, P("crop", "band")) + (P(),) * 17 + (split, special)
    )
    line, matrix = P("crop"), P("crop", None)
    out_specs = (
        split,
        special,
        split,
        special,
        line,
        line,
        line,
        matrix,
        line,
        line,
        matrix,
        line,
        line,
        line,
        line,
        matrix,
        line,
        matrix,
        line,
        line,
    )
    return jax.shard_map(body, mesh=mesh, in_specs=in_specs, out_specs=out_specs, check_vma=False)
```

```python
from functools import partial

import jax
import jax.numpy as jnp
from jax import lax
from jax.experimental import pallas as pl
from jax.experimental.pallas import tpu as pltpu
from jax.sharding import PartitionSpec as P

HEAD = 64
GRID = 37
PAIR = 2 * HEAD
BANDS = 4
KEY_PART = 256
F32 = jnp.float32
BF16 = jnp.bfloat16
VMEM_LIMIT = 60 << 20


def round_up(value, unit):
    return (value + unit - 1) // unit * unit


def params(semantics=None):
    return pltpu.CompilerParams(vmem_limit_bytes=VMEM_LIMIT)


def dot(a, b):
    return jnp.dot(a, b, preferred_element_type=F32)


def dot_nt(a, b):
    return lax.dot_general(a, b, (((1,), (1,)), ((), ())), preferred_element_type=F32)


def dot_tn(a, b):
    return lax.dot_general(a, b, (((0,), (0,)), ((), ())), preferred_element_type=F32)


def normalize(rows):
    centred = rows - jnp.mean(rows, axis=-1, keepdims=True)
    spread = jnp.mean(centred * centred, axis=-1, keepdims=True)
    scale = lax.rsqrt(spread + 1e-06)
    return centred * scale, scale


def normalize_back(grad, hat, scale):
    return scale * (
        grad
        - jnp.mean(grad, axis=-1, keepdims=True)
        - hat * jnp.mean(grad * hat, axis=-1, keepdims=True)
    )


def column_sum(rows):
    return jnp.sum(rows, axis=0, keepdims=True)


def line(ref):
    return ref[...].reshape(1, -1)


def whole(shape):
    return pl.BlockSpec(shape, lambda *_: (0,) * len(shape))


VMEM = pl.BlockSpec(memory_space=pltpu.VMEM)
ANY = pl.BlockSpec(memory_space=pl.ANY)
SMEM = pl.BlockSpec(memory_space=pltpu.SMEM)


def own_special(specials, band, slot):
    row = jnp.zeros((1, specials.shape[1]), F32)
    for special in range(specials.shape[0]):
        if special // BANDS == slot:
            row = row + jnp.where(band == special % BANDS, specials[special : special + 1], 0.0)
    return row


def place_rows(ref, patch_rows, specials, band):
    slots = patch_rows.shape[0]
    rows = ref.shape[0]
    ref[0:slots, :] = patch_rows
    extra = [own_special(specials, band, slot) for slot in range(rows - slots)]
    ref[slots:rows, :] = jnp.concatenate(extra, axis=0)


def counted_rows(info_ref, relative, rows, slots, width):
    index = lax.broadcasted_iota(jnp.int32, (rows, width), 0)
    used = index < info_ref[relative]
    special = (index >= slots) & (index < slots + info_ref[BANDS + relative])
    return used | special


def stack_pair(rows):
    lane = lax.broadcasted_iota(jnp.int32, rows.shape, 1)
    zero = jnp.zeros_like(rows)
    return jnp.concatenate(
        [jnp.where(lane < HEAD, rows, zero), jnp.where(lane >= HEAD, rows, zero)], axis=0
    )


def unstack_pair(rows):
    half = rows.shape[0] // 2
    lane = lax.broadcasted_iota(jnp.int32, (half, rows.shape[1]), 1)
    return jnp.where(lane < HEAD, rows[:half], rows[half:])


def mask_column(mask):
    return jnp.broadcast_to(mask[...].astype(F32), (8, mask.shape[1])).T[:, :1] > 0


def first_kernel(slots, info, mask, patches, specials, token, gain, shift, tokens, first):
    band = info[2 * BANDS]
    filled = jnp.where(mask_column(mask), line(token), patches[...].astype(F32))
    place_rows(tokens, filled, specials[...].astype(F32), band)
    hat, _ = normalize(tokens[...])
    counted = counted_rows(info, 0, tokens.shape[0], slots, tokens.shape[1])
    first[...] = jnp.where(counted, hat * line(gain) + line(shift), 0.0).astype(BF16)


def split_pairs(ref, rows, value):
    for pair in range(ref.shape[0]):
        ref[pair, rows, :] = value[:, pair * PAIR : (pair + 1) * PAIR].astype(BF16)


def project_keys(low, weight, value_bias, counted, keys, values, rows):
    width = weight.shape[0]
    split_pairs(keys, rows, dot(low, weight[:, width : 2 * width]))
    value = dot(low, weight[:, 2 * width :]) + line(value_bias)
    split_pairs(values, rows, jnp.where(counted, value, 0.0))


def attend_pair(queries, keys, values, ones):
    factor = HEAD ** (-0.5)
    stacked = stack_pair((queries.astype(F32) * factor).astype(BF16))
    low = jnp.exp(dot_nt(stacked, keys)).astype(BF16)
    summed = dot(low, jnp.concatenate([values, ones], axis=1))
    return low, unstack_pair(summed[:, :PAIR]), unstack_pair(summed[:, PAIR:])


def project_kernel(slots, info, first, weight, query_bias, value_bias, queries, keys, values):
    relative = pl.program_id(0)
    rows, width = first.shape
    counted = counted_rows(info, relative, rows, slots, width)
    low = first[...]

    @pl.when(relative == 0)
    def _():
        split_pairs(queries, slice(None), dot(low, weight[:, :width]) + line(query_bias))

    project_keys(low, weight, value_bias, counted, keys, values, slice(None))


def attend_kernel(
    slots, info, queries, keys, values, firsts, attended, totals, weights, firsts_t
):
    rows = queries.shape[1]
    ones = [
        counted_rows(info, r, rows, slots, PAIR).astype(F32).astype(BF16) for r in range(BANDS)
    ]
    low, summed, total = attend_pair(
        queries[0], keys[0], values[0], jnp.concatenate(ones, axis=0)
    )
    weights[0] = low
    firsts_t[...] = firsts[...].astype(F32).T.astype(BF16)
    attended[...] = summed / total
    totals[...] = total


def forward_kernel(
    slots,
    pairs,
    info,
    mask,
    patches,
    specials,
    token,
    gain,
    shift,
    query_bias,
    value_bias,
    weight_in,
    tokens_out,
    queries_out,
    keys_out,
    values_out,
    attended,
    totals,
    weights,
    firsts_t,
    tokens,
    firsts,
    queries,
    keys,
    values,
    ones,
    sums,
    counts,
    weight,
    send_sems,
    recv_sems,
    sems,
):
    step = pl.program_id(0)
    rows, width = tokens.shape
    half_rows = 2 * rows
    place = Place()
    sender = Sender(place, send_sems, recv_sems)
    sender.add("near", firsts.at[0], firsts.at[1], "core")
    sender.add("far", firsts.at[0], firsts.at[2], "x")
    sender.add("diagonal", firsts.at[2], firsts.at[3], "core")
    weight_load = lambda: pltpu.make_async_copy(weight_in, weight, sems.at[0])
    stores = lambda: [
        pltpu.make_async_copy(a, b, sems.at[i])
        for i, (a, b) in enumerate(
            ((tokens, tokens_out), (queries, queries_out), (keys, keys_out), (values, values_out)), 1
        )
    ]

    def block_keys(block):
        counted = counted_rows(info, block, rows, slots, width)
        span = pl.ds(block * rows, rows)
        project_keys(firsts[block], weight, value_bias, counted, keys, values, span)

    @pl.when(step == 0)
    def _():
        weight_load().start()
        filled = jnp.where(mask_column(mask), line(token), patches[...].astype(F32))
        place_rows(tokens, filled, specials[...].astype(F32), place.band)
        hat, _ = normalize(tokens[...])
        counted = counted_rows(info, 0, rows, slots, width)
        firsts[0] = jnp.where(counted, hat * line(gain) + line(shift), 0.0).astype(BF16)
        place.greet(("core", "x"))
        sender.send("near")
        sender.send("far")
        for block in range(BANDS):
            used = counted_rows(info, block, rows, slots, PAIR)
            ones[block * rows : (block + 1) * rows, :] = used.astype(F32).astype(BF16)
        weight_load().wait()
        split_pairs(queries, slice(None), dot(firsts[0], weight[:, :width]) + line(query_bias))
        block_keys(0)
        sender.arrived("near")
        block_keys(1)

    @pl.when(step == pairs)
    def _():
        sender.arrived("far")
        sender.send("diagonal")
        block_keys(2)
        sender.arrived("diagonal")
        block_keys(3)
        for copy in stores():
            copy.start()

    far_half = step >= pairs
    pair = jnp.where(far_half, step - pairs, step)
    first_row = pl.multiple_of(jnp.where(far_half, half_rows, 0), half_rows)
    span = pl.ds(first_row, half_rows)
    low, summed, total = attend_pair(
        queries[pair], keys[pair, span], values[pair, span], ones[span, :]
    )
    weights[0] = low
    first_block = jnp.where(far_half, 2, 0)
    lane = pl.ds(pl.multiple_of(pair * PAIR, PAIR), PAIR)
    columns = [firsts[first_block + i, :, lane] for i in range(2)]
    firsts_t[...] = jnp.concatenate(columns, axis=0).astype(F32).T.astype(BF16)

    @pl.when(step < pairs)
    def _():
        sums[pair] = summed
        counts[pair] = total

    @pl.when(far_half)
    def _():
        whole_total = counts[pair] + total
        attended[...] = (sums[pair] + summed) / whole_total
        totals[...] = whole_total

    @pl.when(step == 2 * pairs - 1)
    def _():
        sender.finish()
        for copy in stores():
            copy.wait()


def middle_kernel(
    slots,
    info,
    attended,
    tokens,
    weight,
    bias,
    first_scale,
    gain,
    shift,
    second_scale,
    cot_patches,
    cot_specials,
    branch,
    middle,
    second,
    incoming,
    down_in,
    down_keep,
    down_send,
    down_bias_grad,
):
    rows = tokens.shape[0]
    band = info[2 * BANDS]
    side = dot(attended[...].astype(BF16), weight[...]) + line(bias)
    branch[...] = side
    mid = tokens[...] + line(first_scale) * side
    middle[...] = mid
    hat, _ = normalize(mid)
    second[...] = (hat * line(gain) + line(shift)).astype(BF16)
    counted = counted_rows(info, 0, slots, slots, tokens.shape[1])
    given = jnp.where(counted, cot_patches[...].astype(F32), 0.0)
    place_rows(incoming, given, cot_specials[...].astype(F32), band)
    low = (incoming[...] * line(second_scale)).astype(BF16)
    down_in[...] = low
    keep, send = own_half(low, band)
    down_keep[...] = keep
    down_send[...] = send
    down_bias_grad[...] = column_sum(low.astype(F32))


def own_half(rows, band):
    half = rows.shape[1] // 2
    first = lax.rem(band, 2) == 0
    low, high = rows[:, :half], rows[:, half:]
    return jnp.where(first, low, high), jnp.where(first, high, low)


def gelu_and_slope(x):
    phi = 0.5 + 0.5 * lax.erf(x * 0.7071067811865476)
    density = jnp.exp(-0.5 * x * x) * 0.3989422804014327
    return x * phi, phi + x * density


def mlp_kernel(
    info,
    second,
    down_in,
    down_keep,
    down_send,
    up,
    up_bias,
    down,
    branch_two,
    second_grad,
    up_grad_keep,
    up_grad_send,
    up_bias_grad,
    down_grad_keep,
    down_grad_send,
):
    step = pl.program_id(0)
    low = second[...]
    hidden = dot(low, up[...]) + up_bias[...]
    active, slope = gelu_and_slope(hidden)
    active = active.astype(BF16)
    hidden_in = (slope * dot_nt(down_in[...], down[...])).astype(BF16)

    @pl.when(step == 0)
    def _():
        branch_two[...] = jnp.zeros_like(branch_two)
        second_grad[...] = jnp.zeros_like(second_grad)

    branch_two[...] += dot(active, down[...])
    second_grad[...] += dot_nt(hidden_in, up[...])
    keep, send = own_half(hidden_in, info[2 * BANDS])
    up_grad_send[...] = dot_tn(low, send).astype(BF16)
    up_grad_keep[...] = dot_tn(low, keep).astype(BF16)
    down_grad_send[...] = dot_tn(active, down_send[...]).astype(BF16)
    down_grad_keep[...] = dot_tn(active, down_keep[...]).astype(BF16)
    up_bias_grad[...] = column_sum(hidden_in.astype(F32))


def middle_back_kernel(
    slots,
    info,
    middle,
    branch,
    branch_two,
    second_grad,
    incoming,
    attended,
    weight,
    down_bias,
    second_scale,
    gain,
    first_scale,
    out_patches,
    out_specials,
    middle_grad,
    attended_grad,
    out_keep,
    out_send,
    vectors,
):
    rows = middle.shape[0]
    mid = middle[...]
    given = incoming[...]
    two = branch_two[...] + line(down_bias)
    output = mid + line(second_scale) * two
    counted = counted_rows(info, 0, slots, slots, mid.shape[1])
    out_patches[...] = jnp.where(counted, output[:slots], 0.0).astype(BF16)
    out_specials[...] = output[slots:]
    hat, scale = normalize(mid)
    grad = second_grad[...]
    back = given + normalize_back(grad * line(gain), hat, scale)
    middle_grad[...] = back
    out_in = (back * line(first_scale)).astype(BF16)
    attended_grad[...] = dot_nt(out_in, weight[...])
    keep, send = own_half(out_in, info[2 * BANDS])
    low = attended[...].astype(BF16)
    out_keep[...] = dot_tn(low, keep).astype(BF16)
    out_send[...] = dot_tn(low, send).astype(BF16)
    vectors[...] = jnp.concatenate(
        [
            column_sum(given * two),
            column_sum(grad * hat),
            column_sum(grad),
            column_sum(back * branch[...]),
            column_sum(out_in.astype(F32)),
            jnp.zeros((3, mid.shape[1]), F32),
        ],
        axis=0,
    )


def attend_back_pair(weights, queries, keys, values, attended, totals, attended_grad, outs, between):
    key_grad, value_grad = outs
    queries, keys, values = queries.at[0], keys.at[0], values.at[0]
    rows = queries.shape[0]
    factor = HEAD ** (-0.5)
    stacked = stack_pair((queries[...].astype(F32) * factor).astype(BF16))
    scaled = attended_grad[...] / totals[...]
    returned = stack_pair(scaled.astype(BF16))
    slope = jnp.sum(stack_pair(scaled * attended[...]), axis=1, keepdims=True)
    stacked_t = stacked.astype(F32).T.astype(BF16)
    returned_t = returned.astype(F32).T.astype(BF16)
    total = jnp.zeros((2 * rows, PAIR), F32)
    start = 0
    for part, size in enumerate(key_parts(keys.shape[0])):
        span = slice(start, start + size)
        start += size
        low = weights[0, :, span]
        moved = dot_nt(returned, values[span, :])
        scores = (low.astype(F32) * (moved - slope)).astype(BF16)
        total = total + dot(scores, keys[span, :])
        key_grad[span, :] = dot(stacked_t, scores).T.astype(BF16)
        value_grad[span, :] = dot(returned_t, low).T.astype(BF16)
        between(part)
    return unstack_pair(total) * factor


def key_parts(count):
    parts = [KEY_PART] * (count // KEY_PART)
    if count % KEY_PART:
        parts[-1] += count % KEY_PART
    return parts


def first_part(block, rows, query_grad, key_grad, value_grad, weight):
    width = weight.shape[0]
    span = slice(block * rows, (block + 1) * rows)
    part = jnp.zeros((rows, width), F32)
    for pair in range(0, width // PAIR, 2):
        for offset, grad in ((width, key_grad), (2 * width, value_grad), (0, query_grad)):
            if offset == 0 and block > 0:
                continue
            at = slice(0, rows) if offset == 0 else span
            low = jnp.concatenate([grad[pair, at, :], grad[pair + 1, at, :]], axis=1)
            columns = slice(offset + pair * PAIR, offset + (pair + 2) * PAIR)
            part = part + dot_nt(low, weight[:, columns])
    return part


def own_pair_first(part, band):
    core = lax.rem(band, 2)
    return 2 * part + core, 2 * part + 1 - core


def joint_columns(firsts_t, query_grad, key_grad, value_grad, pairs):
    rows = query_grad.shape[1]
    queries = dot(firsts_t[:, :rows], jnp.concatenate([query_grad[p] for p in pairs], axis=1))
    results = []
    for index, p in enumerate(pairs):
        others = dot(firsts_t[...], jnp.concatenate([key_grad[p], value_grad[p]], axis=1))
        own = queries[:, index * PAIR : (index + 1) * PAIR]
        results.append(jnp.concatenate([own, others], axis=1).astype(BF16))
    return results


def first_back(slots, info, grad, tokens, middle_grad, mask, gain):
    rows, width = tokens.shape
    grad = jnp.where(counted_rows(info, 0, rows, slots, width), grad, 0.0)
    hat, scale = normalize(tokens[...])
    token_grad = middle_grad[...] + normalize_back(grad * line(gain), hat, scale)
    masked = mask_column(mask)
    patch_grad = token_grad[:slots]
    patches = jnp.where(masked, 0.0, patch_grad).astype(BF16)
    vectors = [
        column_sum(jnp.where(masked, patch_grad, 0.0)),
        column_sum(grad * hat),
        column_sum(grad),
    ]
    return patches, token_grad[slots:], vectors


def bias_sums(info, slots, rows, query_grad, value_grad):
    ones = [
        counted_rows(info, block, rows, slots, PAIR).astype(F32).astype(BF16)
        for block in range(BANDS)
    ]
    ones = jnp.concatenate(ones, axis=0)
    pairs = range(query_grad.shape[0])
    queries = [column_sum(query_grad[pair].astype(F32)) for pair in pairs]
    values = [dot_tn(ones, value_grad[pair])[0:1] for pair in pairs]
    both = [jnp.concatenate(queries, axis=1), jnp.concatenate(values, axis=1)]
    return jnp.concatenate(both + [jnp.zeros((6, both[0].shape[1]), F32)], axis=0)


def swap(x, axis, distance):
    size = lax.axis_size(axis)
    return lax.ppermute(x, axis, [(i, i ^ distance) for i in range(size)])


def halve(x, axis, distance):
    bit = (lax.axis_index(axis) // distance) % 2
    sent = lax.dynamic_index_in_dim(x, 1 - bit, 0, keepdims=False)
    kept = lax.dynamic_index_in_dim(x, bit, 0, keepdims=False)
    got = swap(sent, axis, distance)
    return (kept.astype(F32) + got.astype(F32)).astype(BF16)


def reduce_half(kept, got, columns):
    held = (kept.astype(F32) + got.astype(F32)).astype(BF16)
    rows, half = held.shape
    crops = lax.axis_size("crop")
    held = held.reshape((crops, rows // crops, half))
    distance = 1
    while distance < crops:
        count = held.shape[0]
        held = jnp.moveaxis(held.reshape((count // 2, 2) + held.shape[1:]), 1, 0)
        held = halve(held, "crop", distance)
        distance *= 2
    held = held.reshape((rows // crops, half))
    other = swap(held, "band", 2)
    full = (held.astype(F32) + other.astype(F32)).astype(BF16)
    mate = swap(full, "band", 1)
    bit = lax.axis_index("band") % 2
    low = jnp.where(bit == 0, full, mate).astype(F32).reshape(rows // crops, -1, columns)
    high = jnp.where(bit == 0, mate, full).astype(F32).reshape(rows // crops, -1, columns)
    return jnp.stack([low, high], axis=2).reshape(rows // crops, 2 * half)


def gather_blocks(x):
    near = swap(x, "band", 1)
    far = swap(x, "band", 2)
    diagonal = swap(far, "band", 1)
    return jnp.concatenate([x, near, far, diagonal], axis=0)


def scatter_blocks(x):
    rows = x.shape[0] // BANDS
    got = swap(jnp.concatenate([x[rows : 2 * rows], x[3 * rows :]], axis=0), "band", 1)
    own = x[:rows].astype(F32) + got[:rows].astype(F32)
    far = (x[2 * rows : 3 * rows].astype(F32) + got[rows:].astype(F32)).astype(BF16)
    return own + swap(far, "band", 2).astype(F32)


def reduce_small(vectors, more, down_bias, up_bias, out_own, grad_own, special_count):
    crops = lax.axis_size("crop")
    width = vectors.shape[1]
    owned = -(-special_count // BANDS)
    both = jnp.concatenate([out_own[:owned], grad_own[:owned]], axis=1).astype(BF16)
    both = lax.all_gather(both, "band", axis=0, tiled=False)
    both = jnp.transpose(both, (1, 0, 2)).reshape(owned * BANDS, 2 * width)[:special_count]
    plain = jnp.concatenate([vectors[:5], more[:5], down_bias], axis=0)
    plain = jnp.transpose(plain.reshape(11, crops, -1), (1, 0, 2)).reshape(crops, -1)
    packed = jnp.concatenate([plain, up_bias.reshape(crops, -1)], axis=1)
    packed = lax.psum_scatter(packed, "crop", scatter_dimension=0, tiled=False)
    packed = lax.psum(packed, "band")
    part = width // crops
    rows = [packed[i * part : (i + 1) * part] for i in range(11)]
    return rows, packed[11 * part :], both[None, :, :width], both[None, :, width:]


def attend_back_kernel(
    weights, queries, keys, values, attended, totals, attended_grad, query_grad, key_grad, value_grad
):
    inputs = (weights, queries, keys, values, attended, totals, attended_grad)
    part = attend_back_pair(*inputs, (key_grad.at[0], value_grad.at[0]), lambda part: None)
    query_grad[0] = part.astype(BF16)


def joint_back_kernel(
    slots, info, firsts_t, query_grad, key_grad, value_grad, weight, joint_keep, joint_send, first_grad, sums
):
    rows, width = query_grad.shape[1], weight.shape[0]
    for block in range(BANDS):
        part = first_part(block, rows, query_grad, key_grad, value_grad, weight)
        first_grad[block * rows : (block + 1) * rows, :] = part.astype(BF16)
    third = 3 * PAIR
    for part in range(query_grad.shape[0] // 2):
        keep, send = joint_columns(
            firsts_t, query_grad, key_grad, value_grad, own_pair_first(part, info[2 * BANDS])
        )
        joint_keep[:, part * third : (part + 1) * third] = keep
        joint_send[:, part * third : (part + 1) * third] = send
    sums[...] = bias_sums(info, slots, rows, query_grad, value_grad)


def first_back_kernel(
    slots, info, first_grad, tokens, middle_grad, mask, gain, sums, patches, specials, vectors
):
    grads, special_grad, rows = first_back(
        slots, info, first_grad[...], tokens, middle_grad, mask, gain
    )
    patches[...] = grads
    specials[...] = special_grad
    vectors[...] = jnp.concatenate(rows + [sums[0:5]], axis=0)


def joint_order(x):
    rows, columns = x.shape
    x = x.reshape(rows, columns // (3 * PAIR), 3, PAIR)
    return jnp.transpose(x, (0, 2, 1, 3)).reshape(rows, columns)


def backward_general(given, slots, special_count):
    g = given
    rows, width = g["tokens"].shape
    every = BANDS * rows
    pairs = width // PAIR
    shaped = jax.ShapeDtypeStruct
    own_pair = pl.BlockSpec((rows, PAIR), lambda i: (0, i))
    grads = pl.pallas_call(
        attend_back_kernel,
        grid=(pairs,),
        out_shape=[
            shaped((pairs, rows, PAIR), BF16),
            shaped((pairs, every, PAIR), BF16),
            shaped((pairs, every, PAIR), BF16),
        ],
        in_specs=[
            pl.BlockSpec((1, 2 * rows, every), lambda i: (i, 0, 0)),
            pl.BlockSpec((1, rows, PAIR), lambda i: (i, 0, 0)),
            pl.BlockSpec((1, every, PAIR), lambda i: (i, 0, 0)),
            pl.BlockSpec((1, every, PAIR), lambda i: (i, 0, 0)),
            own_pair,
            own_pair,
            own_pair,
        ],
        out_specs=[
            pl.BlockSpec((1, rows, PAIR), lambda i: (i, 0, 0)),
            pl.BlockSpec((1, every, PAIR), lambda i: (i, 0, 0)),
            pl.BlockSpec((1, every, PAIR), lambda i: (i, 0, 0)),
        ],
        compiler_params=params(),
        name="attend_back",
    )(
        g["weights"],
        g["queries"],
        g["keys"],
        g["values"],
        g["attended"],
        g["totals"],
        g["attended_grad"],
    )
    half = width // 2
    joint_keep, joint_send, parts, sums = pl.pallas_call(
        partial(joint_back_kernel, slots),
        out_shape=[
            shaped((width, 3 * half), BF16),
            shaped((width, 3 * half), BF16),
            shaped((every, width), BF16),
            shaped((8, width), F32),
        ],
        in_specs=[SMEM] + [VMEM] * 5,
        out_specs=[VMEM] * 4,
        compiler_params=params(),
        name="joint_back",
    )(g["info"], g["firsts_t"], *grads, g["joint_weight"])
    grad_patches, grad_own, more = pl.pallas_call(
        partial(first_back_kernel, slots),
        out_shape=[
            shaped((slots, width), BF16),
            shaped((rows - slots, width), F32),
            shaped((8, width), F32),
        ],
        in_specs=[SMEM] + [VMEM] * 6,
        out_specs=[VMEM] * 3,
        compiler_params=params(),
        name="first_back",
    )(
        g["info"],
        scatter_blocks(parts),
        g["tokens"],
        g["middle_grad"],
        g["mask"],
        g["first_gain"],
        sums,
    )
    small = reduce_small(
        g["vectors"],
        more,
        g["down_bias_grad"],
        g["up_bias_grad"],
        g["out_own"],
        grad_own,
        special_count,
    )
    matrices = (
        reduce_half(g["up_keep"], g["up_got"], half),
        reduce_half(g["down_keep"], g["down_got"], half),
        reduce_half(g["out_keep"], swap(g["out_send"], "band", 1), half),
        joint_order(reduce_half(joint_keep, swap(joint_send, "band", 1), half)),
    )
    return (grad_patches,) + matrices + small


MESH = pl.DeviceIdType.MESH
CROPS = 8
X_FIRST = (0, 1, 3, 4, 9, 10)
NEIGHBOURS = ("core", "x", "diagonal")
PLACES = NEIGHBOURS + tuple(range(1, CROPS))


class Place:
    def __init__(self):
        band, crop = lax.axis_index("band"), lax.axis_index("crop")
        self.band = band
        self.core, self.x = lax.rem(band, 2), lax.div(band, 2)
        self.y, self.near, self.far = lax.rem(crop, 2), lax.rem(lax.div(crop, 2), 2), lax.div(crop, 4)
        core_step, x_step = 1 - 2 * self.core, 2 - 4 * self.x
        self.device = {
            "core": (band + core_step, crop),
            "x": (band + x_step, crop),
            "diagonal": (band + core_step + x_step, crop),
            "y": (band, crop + 1 - 2 * self.y),
            "near": (band, crop + 2 - 4 * self.near),
            "far": (band, crop + 4 - 8 * self.far),
        }
        self.crop = crop
        for step in range(1, CROPS):
            self.device[step] = (band, lax.rem(crop + step, CROPS))

    def greet(self, names):
        barrier = pltpu.get_barrier_semaphore()
        for name in names:
            pl.semaphore_signal(barrier, inc=1, device_id=self.device[name], device_id_type=MESH)
        pl.semaphore_wait(barrier, len(names))


class Sender:
    def __init__(self, place, send_sems, recv_sems):
        self.place, self.send_sems, self.recv_sems = place, send_sems, recv_sems
        self.routes = {}

    def add(self, key, source, target, name):
        self.routes[key] = (len(self.routes), source, target, name)

    def copy(self, key):
        index, source, target, name = self.routes[key]
        return pltpu.make_async_remote_copy(
            src_ref=source,
            dst_ref=target,
            send_sem=self.send_sems.at[index],
            recv_sem=self.recv_sems.at[index],
            device_id=self.place.device[name],
            device_id_type=MESH,
        )

    def send(self, key):
        self.copy(key).start()

    def arrived(self, key):
        self.copy(key).wait_recv()

    def finish(self):
        for key in self.routes:
            self.copy(key).wait_send()


def chunk_list(hidden_parts):
    chunks = []
    for part in range(hidden_parts):
        chunks += [("down", part), ("up", part)]
    return chunks + [("out", 0), ("joint", 0), ("joint", 1), ("joint", 2)]


def chunk_scratch(count, rows, columns):
    unit = (rows, columns)
    return [
        pltpu.VMEM((count, 2, 2, 2, 2) + unit, BF16),
        pltpu.VMEM((count, 2, 2, 2) + unit, BF16),
        pltpu.VMEM((count, 2, 2) + unit, BF16),
        pltpu.VMEM((count, 2) + unit, BF16),
        pltpu.VMEM((count, 2) + unit, BF16),
    ]


class ChunkSums:
    def __init__(self, place, sender, buffers, total, count):
        p, self.sender = place, sender
        own, got_a, got_b, got_c, got_d = buffers
        self.table = {}
        for n in range(count):
            if x_first(n):
                half = total.at[n, p.core, p.x]
                rows = [
                    (None, None, own.at[n, 1 - p.x], got_a.at[n], "x"),
                    (own.at[n, p.x], got_a.at[n], own.at[n, p.x, :, :, 1 - p.y], got_b.at[n], "y"),
                    (
                        own.at[n, p.x, :, :, p.y],
                        got_b.at[n],
                        own.at[n, p.x, :, 1 - p.near, p.y],
                        got_c.at[n],
                        "near",
                    ),
                    (
                        own.at[n, p.x, :, p.near, p.y],
                        got_c.at[n],
                        own.at[n, p.x, 1 - p.far, p.near, p.y],
                        got_d.at[n, 0],
                        "far",
                    ),
                    (own.at[n, p.x, p.far, p.near, p.y], got_d.at[n, 0], half, half, "x"),
                    (None, None, total.at[n, p.core], total.at[n, p.core], "core"),
                ]
                last = half
            else:
                half = total.at[n, p.core]
                rows = [
                    (None, None, own.at[n, :, :, 1 - p.y], got_a.at[n], "y"),
                    (
                        own.at[n, :, :, p.y],
                        got_a.at[n],
                        own.at[n, :, 1 - p.near, p.y],
                        got_b.at[n],
                        "near",
                    ),
                    (
                        own.at[n, :, p.near, p.y],
                        got_b.at[n],
                        own.at[n, 1 - p.far, p.near, p.y],
                        got_c.at[n],
                        "far",
                    ),
                    (
                        own.at[n, p.far, p.near, p.y],
                        got_c.at[n],
                        own.at[n, p.far, p.near, p.y],
                        got_d.at[n],
                        "x",
                    ),
                    (own.at[n, p.far, p.near, p.y], got_d.at[n], half, half, "core"),
                ]
                last = half
            self.table[n] = rows
            for stage, (_, _, source, target, name) in enumerate(rows):
                sender.add((n, stage + 1), source, target, name)
            self.table[n, "last"] = last

    def steps(self, n):
        return len(self.table[n]) + 1

    def step(self, n, stage):
        if stage > 0:
            self.sender.arrived((n, stage))
        if stage == len(self.table[n]):
            return
        into, got, source, target, _ = self.table[n][stage]
        if into is not None:
            place = self.table[n, "last"] if source is target else into
            place[...] = into[...] + got[...]
        self.sender.send((n, stage + 1))


class VectorSums:
    def __init__(self, place, sender, buffers, total):
        self.place, self.sender, self.total = place, sender, total
        self.own, self.got, self.parts = buffers
        for step in range(1, CROPS):
            source = self.own.at[lax.rem(place.crop + step, CROPS)]
            sender.add(("vector", step), source, self.got.at[place.crop], step)
        here = self.parts.at[place.band]
        for name in NEIGHBOURS:
            sender.add(("parts", name), here, here, name)

    def spread(self):
        for step in range(1, CROPS):
            self.sender.send(("vector", step))

    def share(self):
        p = self.place
        self.got[p.crop] = self.own[p.crop]
        for step in range(1, CROPS):
            self.sender.arrived(("vector", step))
        self.parts[p.band] = jnp.sum(self.got[...], axis=0)
        for name in NEIGHBOURS:
            self.sender.send(("parts", name))

    def close(self):
        for name in NEIGHBOURS:
            self.sender.arrived(("parts", name))
        self.total[...] = jnp.sum(self.parts[...], axis=0)


def pack_vectors(own, rows, up_bias, part):
    for crop in range(CROPS):
        span = slice(crop * part, (crop + 1) * part)
        wide = 4 * crop * part
        wider = [up_bias[0:1, wide + j * part : wide + (j + 1) * part] for j in range(4)]
        own[crop, 0:15, 0:part] = jnp.concatenate([rows[:, span]] + wider, axis=0)


def vector_scratch():
    return [
        pltpu.VMEM((CROPS, 16, 128), F32),
        pltpu.VMEM((CROPS, 16, 128), F32),
        pltpu.VMEM((BANDS, 16, 128), F32),
    ]


def x_first(n):
    return n in X_FIRST


def halves_of(n):
    return (0, 1) if x_first(n) else (None,)


def part_of(ref, name, part, columns, x_half):
    at = slice(None) if x_half is None else x_half
    if name == "down":
        return ref.at[:, :, :, part, at]
    return ref.at[:, :, :, at, :, pl.ds(part * columns, columns)]


def piece(ref, x_half):
    return ref if x_half is None else ref.at[x_half]


PLAN = (
    (0, 0, 0), (0, 1, 0), (0, 2, 0), (0, 3, 0), (0, 5, 0), (0, 6, 0),
    (7, 4, 0), (7, 7, 0), (9, 0, 1), (9, 2, 1), (16, 2, 2), (16, 1, 1),
    (16, 5, 1), (18, 8, 0), (19, 2, 3), (19, 3, 1), (19, 6, 1), (22, 5, 2),
    (24, 2, 4), (24, 6, 2), (24, 4, 1), (24, 7, 1), (26, 5, 3), (26, 0, 2),
    (26, 9, 0), (27, 2, 5), (29, 6, 3), (29, 1, 2), (30, 7, 2), (32, 0, 3),
    (33, 1, 3), (33, 8, 1), (33, 10, 0), (36, 7, 3), (36, 3, 2), (37, 0, 4),
    (38, 4, 2), (38, 11, 0), (39, 8, 2), (40, 1, 4), (40, 5, 4), (40, 6, 4),
    (40, 3, 3), (40, 4, 3), (40, 9, 1), (45, 8, 3), (45, 11, 1), (47, 5, 5),
    (48, 3, 4), (49, 6, 5), (50, 10, 1), (51, 4, 4), (52, 9, 2), (53, 7, 4),
    (54, 0, 5), (55, 1, 5), (56, 11, 2), (57, 7, 5), (58, 10, 2), (59, 8, 4),
    (60, 9, 3), (61, 0, 6), (62, 3, 5), (63, 1, 6), (64, 4, 5), (65, 8, 5),
    (66, 11, 3), (67, 3, 6), (68, 4, 6), (69, 10, 3), (70, 11, 4), (71, 9, 4),
    (72, 10, 4), (73, 9, 5), (74, 11, 5), (75, 10, 5), (76, 9, 6), (77, 10, 6),
)


def backward_kernel(
    chunks,
    slots,
    pairs,
    info,
    weights,
    queries,
    keys,
    values,
    attended,
    totals,
    attended_grad,
    mask,
    gain,
    vectors,
    down_bias,
    up_bias,
    out_own,
    up_keep,
    up_got,
    down_keep,
    down_got,
    out_keep,
    out_send,
    firsts_in,
    weight_in,
    tokens_in,
    middle_grad_in,
    grad_patches,
    total_out,
    vector_total,
    specials_out,
    *scratch,
):
    buffers, vector_buffers = scratch[:5], scratch[5:8]
    (
        total,
        out_got,
        joint_got,
        joint_sent,
        loaded,
        query_sum,
        query_grad,
        key_grad,
        value_grad,
        firsts_t,
        weight,
        tokens,
        middle_grad,
        parts,
        got_parts,
        got_far,
        specials,
        send_sems,
        recv_sems,
        load_sems,
        whole_sems,
    ) = scratch[8:]
    step = pl.program_id(0)
    count = len(chunks)
    columns = total.shape[4]
    rows, width = tokens.shape
    place = Place()
    sender = Sender(place, send_sems, recv_sems)
    sums = ChunkSums(place, sender, buffers, total, count)
    vector_sums = VectorSums(place, sender, vector_buffers, vector_total)
    own = buffers[0]
    keeps = dict(up=up_keep, down=down_keep, out=out_keep)
    gots = dict(up=up_got, down=down_got)

    def own_loads(n):
        name, part = chunks[n]
        return [
            pltpu.make_async_copy(
                part_of(keeps[name], name, part, columns, h), piece(own.at[n], h), load_sems.at[n, 0, i]
            )
            for i, h in enumerate(halves_of(n))
        ]

    def got_loads(n):
        name, part = chunks[n]
        return [
            pltpu.make_async_copy(
                part_of(gots[name], name, part, columns, h), piece(loaded.at[mlp.index(n) % 2], h), load_sems.at[n, 1, i]
            )
            for i, h in enumerate(halves_of(n))
        ]

    def whole_loads():
        pairs_of = ((weight_in, weight), (firsts_in, firsts_t), (tokens_in, tokens), (middle_grad_in, middle_grad))
        return [
            pltpu.make_async_copy(a, b, whole_sems.at[i]) for i, (a, b) in enumerate(pairs_of)
        ]

    early = [n for n, (name, _) in enumerate(chunks) if name != "joint"]
    mlp = [n for _, n, stage in PLAN if stage == 0 and chunks[n][0] in gots]
    out_chunk = early[-1]
    late = [n for n, (name, _) in enumerate(chunks) if name == "joint"]

    for h in halves_of(out_chunk):
        source = part_of(out_send, "out", 0, columns, h)
        sender.add((out_chunk, 0, h), source, piece(out_got, h), "core")
    for n in late:
        sender.add((n, 0), joint_sent.at[n - late[0]], joint_got.at[n - late[0]], "core")
    for index in range(2):
        sender.add(("first", index), parts.at[index], got_parts.at[index], "core")
    sender.add("far", parts.at[2], got_far, "x")
    for name in NEIGHBOURS:
        sender.add(("special", name), specials.at[place.band], specials.at[place.band], name)

    def begin():
        for n in early:
            for copy in own_loads(n):
                copy.start()
        for n in mlp[:2]:
            for copy in got_loads(n):
                copy.start()
        place.greet(PLACES)
        for h in halves_of(out_chunk):
            sender.send((out_chunk, 0, h))

    def early_stage(n, stage):
        if stage == 0:
            for copy in own_loads(n):
                copy.wait()
            if n in mlp:
                for copy in got_loads(n):
                    copy.wait()
                index = mlp.index(n)
                own[n] = own[n] + loaded[index % 2]
                if index + 2 < len(mlp):
                    for copy in got_loads(mlp[index + 2]):
                        copy.start()
            else:
                for h in halves_of(n):
                    sender.arrived((n, 0, h))
                own[n] = own[n] + out_got[...]
        sums.step(n, stage)

    def late_stage(n, stage):
        if stage == 0:
            sender.arrived((n, 0))
            own[n] = own[n] + joint_got[n - late[0]]
        sums.step(n, stage)

    def stage_of(n, stage):
        (late_stage if n in late else early_stage)(n, stage)

    def exchanges(slot):
        for place_of, n, stage in PLAN:
            if place_of == slot:
                stage_of(n, stage)

    def occupied(slot):
        return any(place_of == slot for place_of, _, _ in PLAN)

    def joint_chunk(part):
        n = late[part]
        picked = joint_columns(firsts_t, *grads, own_pair_first(part, place.band))
        shape = (2, 2, 2, 2, width // CROPS // 2, columns)
        for value, target in zip(picked, (own.at[n], joint_sent.at[part])):
            value = value.reshape(shape)
            for h in halves_of(n):
                if h is None:
                    target[...] = value
                else:
                    target[h] = value[:, :, :, h]
        sender.send((n, 0))

    half_rows = 2 * rows
    per_step = len(key_parts(half_rows))

    def between(part):
        for index in range(2 * pairs):
            if occupied(index * per_step + part):

                @pl.when(step == index)
                def _():
                    exchanges(index * per_step + part)

    grads = (query_grad, key_grad, value_grad)
    last = 2 * pairs
    after = last * per_step

    @pl.when(step == 0)
    def _():
        begin()

    @pl.when(step == 1)
    def _():
        for copy in whole_loads():
            copy.start()

    @pl.when(step == pairs)
    def _():
        for copy in whole_loads():
            copy.wait()
        parts[1] = first_part(3, rows, *grads, weight).astype(BF16)
        sender.send(("first", 1))
        parts[2] = first_part(2, rows, *grads, weight).astype(BF16)

    @pl.when(step == pairs + 1)
    def _():
        sender.arrived(("first", 1))
        parts[2] = parts[2] + got_parts[1]
        sender.send("far")

    for part in range(2):

        @pl.when(step == pairs + 2 * part + 2)
        def _():
            joint_chunk(part)

    @pl.when(step < last)
    def _():
        far_half = step < pairs
        pair = jnp.where(far_half, step, jnp.minimum(step - pairs, pairs - 1))
        first_row = pl.multiple_of(jnp.where(far_half, half_rows, 0), half_rows)
        span = pl.ds(first_row, half_rows)
        outs = (key_grad.at[pair, span], value_grad.at[pair, span])
        inputs = (weights, queries, keys, values, attended, totals, attended_grad)
        part = attend_back_pair(*inputs, outs, between)

        @pl.when(far_half)
        def _():
            query_sum[pair] = part

        @pl.when(step >= pairs)
        def _():
            query_grad[pair] = (query_sum[pair] + part).astype(BF16)

    @pl.when(step == last)
    def _():
        joint_chunk(2)
        exchanges(after)
        parts[0] = first_part(1, rows, *grads, weight).astype(BF16)
        sender.send(("first", 0))
        exchanges(after + 1)
        first_grad = first_part(0, rows, *grads, weight)
        exchanges(after + 2)
        biases = bias_sums(info, slots, rows, query_grad, value_grad)
        sender.arrived(("first", 0))
        sender.arrived("far")
        first_grad = first_grad + got_parts[0].astype(F32) + got_far[...].astype(F32)
        exchanges(after + 3)
        patches, special_grad, rows_of = first_back(
            slots, info, first_grad, tokens, middle_grad, mask, gain
        )
        grad_patches[...] = patches
        specials[place.band] = jnp.concatenate([out_own[0:4], special_grad[0:4]], axis=0)
        for name in NEIGHBOURS:
            sender.send(("special", name))
        packed = jnp.concatenate([vectors[0:5]] + rows_of + [biases[0:2], down_bias[...]], axis=0)
        pack_vectors(vector_sums.own, packed, up_bias, width // CROPS)
        vector_sums.spread()
        for slot in range(after + 4, max(entry[0] for entry in PLAN) + 1):
            exchanges(slot)
            if slot == after + 7:
                vector_sums.share()
            if slot == after + 15:
                vector_sums.close()
        for name in NEIGHBOURS:
            sender.arrived(("special", name))
        specials_out[...] = specials[...]
        sender.finish()
        copy = pltpu.make_async_copy(total, total_out, whole_sems.at[4])
        copy.start()
        copy.wait()


def finish_kernel(
    chunks,
    special_count,
    total,
    vector_total,
    specials,
    up,
    down,
    out,
    joint,
    up_bias,
    out_specials,
    grad_specials,
    *vectors,
):
    _, _, _, rows, columns = total.shape
    refs = dict(up=up, down=down, out=out, joint=joint)
    for n, (name, part) in enumerate(chunks):
        for core in range(2):
            for x in range(2):
                row, column = x * rows, core * columns
                if name == "down":
                    row += 2 * rows * part
                else:
                    column += 2 * columns * part
                value = total[n, core, x].astype(F32)
                if name == "joint":
                    for third in range(3):
                        column = third * 2 * columns + (2 * part + core) * PAIR
                        piece_of = value[:, third * PAIR : (third + 1) * PAIR]
                        joint[row : row + rows, column : column + PAIR] = piece_of
                    continue
                refs[name][row : row + rows, column : column + columns] = value
    part = vectors[0].shape[0]
    for i, vector in enumerate(vectors):
        vector[...] = vector_total[i, 0:part]
    up_bias[...] = jnp.concatenate([vector_total[i : i + 1, 0:part] for i in range(11, 15)], axis=1)[0]
    for first, target in ((0, out_specials), (4, grad_specials)):
        picked = [
            specials[s % BANDS, first + s // BANDS : first + s // BANDS + 1]
            for s in range(special_count)
        ]
        target[0] = jnp.concatenate(picked, axis=0).astype(BF16)


def backward_fused(given, slots, special_count):
    g = given
    rows, width = g["tokens"].shape
    hidden_width = g["up_bias_grad"].shape[1]
    every = BANDS * rows
    pairs = width // PAIR
    chunks = chunk_list(hidden_width // width)
    count = len(chunks)
    part = width // CROPS
    unit_rows, columns = part // 2, width // 2
    unit = (2, 2, 2, 2, unit_rows, columns)
    hidden_parts = hidden_width // width
    shaped = jax.ShapeDtypeStruct
    last = 2 * pairs - 1
    far_first = lambda i: 1 - jnp.minimum(i, last) // pairs
    pair_of = lambda i: jnp.minimum(i, last) % pairs
    own_pair = pl.BlockSpec((rows, PAIR), lambda i: (0, pair_of(i)))
    own_heads = pl.BlockSpec((1, rows, PAIR), lambda i: (pair_of(i), 0, 0))
    half_heads = pl.BlockSpec((1, 2 * rows, PAIR), lambda i: (pair_of(i), far_first(i), 0))
    kept = pl.BlockSpec((1, 2 * rows, 2 * rows), lambda i: (pair_of(i), 0, far_first(i)))
    up_shape = (2, 2, 2, 2, unit_rows, hidden_parts * columns)
    down_shape = (2, 2, 2, hidden_parts, 2, unit_rows, columns)
    grad_patches, total, vector_total, specials = pl.pallas_call(
        partial(backward_kernel, chunks, slots, pairs),
        grid=(2 * pairs + 1,),
        out_shape=[
            shaped((slots, width), BF16),
            shaped((count, 2, 2, unit_rows, columns), BF16),
            shaped((16, 128), F32),
            shaped((BANDS, 8, width), F32),
        ],
        in_specs=[SMEM, kept, own_heads, half_heads, half_heads, own_pair, own_pair, own_pair]
        + [VMEM] * 6
        + [ANY] * 10,
        out_specs=[VMEM, ANY, VMEM, VMEM],
        scratch_shapes=chunk_scratch(count, unit_rows, columns)
        + vector_scratch()
        + [
            pltpu.VMEM((count, 2, 2, unit_rows, columns), BF16),
            pltpu.VMEM(unit, BF16),
            pltpu.VMEM((3,) + unit, BF16),
            pltpu.VMEM((3,) + unit, BF16),
            pltpu.VMEM((2,) + unit, BF16),
            pltpu.VMEM((pairs, rows, PAIR), F32),
            pltpu.VMEM((pairs, rows, PAIR), BF16),
            pltpu.VMEM((pairs, every, PAIR), BF16),
            pltpu.VMEM((pairs, every, PAIR), BF16),
            pltpu.VMEM((width, every), BF16),
            pltpu.VMEM((width, 3 * width), BF16),
            pltpu.VMEM((rows, width), F32),
            pltpu.VMEM((rows, width), F32),
            pltpu.VMEM((3, rows, width), BF16),
            pltpu.VMEM((2, rows, width), BF16),
            pltpu.VMEM((rows, width), BF16),
            pltpu.VMEM((BANDS, 8, width), F32),
            pltpu.SemaphoreType.DMA((10 * count,)),
            pltpu.SemaphoreType.DMA((10 * count,)),
            pltpu.SemaphoreType.DMA((count, 2, 2)),
            pltpu.SemaphoreType.DMA((5,)),
        ],
        compiler_params=pltpu.CompilerParams(
            vmem_limit_bytes=VMEM_LIMIT, collective_id=0, has_side_effects=True
        ),
        name="backward",
    )(
        g["info"],
        g["weights"],
        g["queries"],
        g["keys"],
        g["values"],
        g["attended"],
        g["totals"],
        g["attended_grad"],
        g["mask"],
        g["first_gain"],
        g["vectors"],
        g["down_bias_grad"],
        g["up_bias_grad"],
        g["out_own"],
        g["up_keep"].reshape(up_shape),
        g["up_got"].reshape(up_shape),
        g["down_keep"].reshape(down_shape),
        g["down_got"].reshape(down_shape),
        g["out_keep"].reshape(unit),
        g["out_send"].reshape(unit),
        g["firsts_t"],
        g["joint_weight"],
        g["tokens"],
        g["middle_grad"],
    )
    special = shaped((1, special_count, width), BF16)
    results = pl.pallas_call(
        partial(finish_kernel, chunks, special_count),
        out_shape=[
            shaped((part, hidden_width), F32),
            shaped((hidden_width // CROPS, width), F32),
            shaped((part, width), F32),
            shaped((part, 3 * width), F32),
            shaped((hidden_width // CROPS,), F32),
            special,
            special,
        ]
        + [shaped((part,), F32)] * 11,
        in_specs=[VMEM] * 3,
        out_specs=[VMEM] * 18,
        compiler_params=params(),
        name="finish",
    )(total, vector_total, specials)
    up, down, out, joint, up_bias, out_specials, grad_specials = results[:7]
    return grad_patches, up, down, out, joint, results[7:], up_bias, out_specials, grad_specials


def forward_fused(
    info, mask, patches, specials, token, gain, shift, weight, query_bias, value_bias, rows
):
    slots, width = patches.shape
    every, pairs = BANDS * rows, width // PAIR
    shaped = jax.ShapeDtypeStruct
    half_of = lambda i: i // pairs
    pair_of = lambda i: i % pairs
    final_pair = pl.BlockSpec((rows, PAIR), lambda i: (0, jnp.maximum(i - pairs, 0)))
    outs = pl.pallas_call(
        partial(forward_kernel, slots, pairs),
        grid=(2 * pairs,),
        out_shape=[
            shaped((rows, width), F32),
            shaped((pairs, rows, PAIR), BF16),
            shaped((pairs, every, PAIR), BF16),
            shaped((pairs, every, PAIR), BF16),
            shaped((rows, width), F32),
            shaped((rows, width), F32),
            shaped((pairs, 2 * rows, every), BF16),
            shaped((width, every), BF16),
        ],
        in_specs=[SMEM] + [VMEM] * 8 + [ANY],
        out_specs=[
            ANY,
            ANY,
            ANY,
            ANY,
            final_pair,
            final_pair,
            pl.BlockSpec((1, 2 * rows, 2 * rows), lambda i: (pair_of(i), 0, half_of(i))),
            pl.BlockSpec((PAIR, 2 * rows), lambda i: (pair_of(i), half_of(i))),
        ],
        scratch_shapes=[
            pltpu.VMEM((rows, width), F32),
            pltpu.VMEM((BANDS, rows, width), BF16),
            pltpu.VMEM((pairs, rows, PAIR), BF16),
            pltpu.VMEM((pairs, every, PAIR), BF16),
            pltpu.VMEM((pairs, every, PAIR), BF16),
            pltpu.VMEM((every, PAIR), BF16),
            pltpu.VMEM((pairs, rows, PAIR), F32),
            pltpu.VMEM((pairs, rows, PAIR), F32),
            pltpu.VMEM((width, 3 * width), BF16),
            pltpu.SemaphoreType.DMA((3,)),
            pltpu.SemaphoreType.DMA((3,)),
            pltpu.SemaphoreType.DMA((5,)),
        ],
        compiler_params=pltpu.CompilerParams(
            vmem_limit_bytes=VMEM_LIMIT, collective_id=1, has_side_effects=True
        ),
        name="forward",
    )(info, mask, patches, specials, token, gain, shift, query_bias, value_bias, weight)
    return outs


def forward_general(
    info, mask, patches, specials, token, gain, shift, weight, query_bias, value_bias, rows
):
    slots, width = patches.shape
    every, pairs = BANDS * rows, width // PAIR
    shaped = jax.ShapeDtypeStruct
    tokens, first = pl.pallas_call(
        partial(first_kernel, slots),
        out_shape=[shaped((rows, width), F32), shaped((rows, width), BF16)],
        in_specs=[SMEM] + [VMEM] * 6,
        compiler_params=params(),
        name="first",
    )(info, mask, patches, specials, token, gain, shift)
    firsts = gather_blocks(first)
    block = pl.BlockSpec((rows, width), lambda i: (i, 0))
    pair_block = pl.BlockSpec((pairs, rows, PAIR), lambda i: (0, i, 0))
    queries, keys, values = pl.pallas_call(
        partial(project_kernel, slots),
        grid=(BANDS,),
        out_shape=[
            shaped((pairs, rows, PAIR), BF16),
            shaped((pairs, every, PAIR), BF16),
            shaped((pairs, every, PAIR), BF16),
        ],
        in_specs=[SMEM, block, whole((width, 3 * width)), VMEM, VMEM],
        out_specs=[whole((pairs, rows, PAIR)), pair_block, pair_block],
        compiler_params=params(),
        name="project",
    )(info, firsts, weight, query_bias, value_bias)
    own_pair = pl.BlockSpec((rows, PAIR), lambda i: (0, i))
    all_pair = pl.BlockSpec((every, PAIR), lambda i: (0, i))
    own_heads = pl.BlockSpec((1, rows, PAIR), lambda i: (i, 0, 0))
    all_heads = pl.BlockSpec((1, every, PAIR), lambda i: (i, 0, 0))
    attended, totals, weights, firsts_t = pl.pallas_call(
        partial(attend_kernel, slots),
        grid=(pairs,),
        out_shape=[
            shaped((rows, width), F32),
            shaped((rows, width), F32),
            shaped((pairs, 2 * rows, every), BF16),
            shaped((width, every), BF16),
        ],
        in_specs=[SMEM, own_heads, all_heads, all_heads, all_pair],
        out_specs=[
            own_pair,
            own_pair,
            pl.BlockSpec((1, 2 * rows, every), lambda i: (i, 0, 0)),
            pl.BlockSpec((PAIR, every), lambda i: (i, 0)),
        ],
        compiler_params=params(),
        name="attend",
    )(info, queries, keys, values, firsts)
    return tokens, queries, keys, values, attended, totals, weights, firsts_t


def body(
    patches,
    specials,
    patch_mask,
    band_rows,
    mask_token,
    first_gain,
    first_shift,
    joint_weight,
    query_bias,
    value_bias,
    out_weight,
    out_bias,
    first_scale,
    second_gain,
    second_shift,
    up_weight,
    up_bias,
    down_weight,
    down_bias,
    second_scale,
    cot_patches,
    cot_specials,
):
    slots, width = patches.shape[1:]
    special_count = specials.shape[1]
    hidden_width = up_weight.shape[1]
    owned = -(-special_count // BANDS)
    rows = round_up(slots + owned, 16)
    pad = rows - slots
    band = lax.axis_index("band")
    relatives = [band ^ r for r in range(BANDS)]
    info = jnp.stack(
        [band_rows[b] * GRID for b in relatives]
        + [(special_count - b + BANDS - 1) // BANDS for b in relatives]
        + [band]
    ).astype(jnp.int32)
    mask = patch_mask
    patches, specials = patches[0], specials[0]
    cot_patches, cot_specials = cot_patches[0], cot_specials[0]
    shaped = jax.ShapeDtypeStruct

    forward = forward_fused if lax.axis_size("crop") == CROPS else forward_general
    tokens, queries, keys, values, attended, totals, weights, firsts_t = forward(
        info,
        mask,
        patches,
        specials,
        mask_token,
        first_gain,
        first_shift,
        joint_weight,
        query_bias,
        value_bias,
        rows,
    )

    branch, middle, second, incoming, down_in, down_keep, down_send, down_bias_grad = pl.pallas_call(
        partial(middle_kernel, slots),
        out_shape=[
            shaped((rows, width), F32),
            shaped((rows, width), F32),
            shaped((rows, width), BF16),
            shaped((rows, width), F32),
            shaped((rows, width), BF16),
            shaped((rows, width // 2), BF16),
            shaped((rows, width // 2), BF16),
            shaped((1, width), F32),
        ],
        in_specs=[SMEM] + [VMEM] * 10,
        out_specs=[VMEM] * 8,
        compiler_params=params(),
        name="middle",
    )(
        info,
        attended,
        tokens,
        out_weight,
        out_bias,
        first_scale,
        second_gain,
        second_shift,
        second_scale,
        cot_patches,
        cot_specials,
    )

    steps = hidden_width // width
    half = width // 2
    (
        branch_two,
        second_grad,
        up_keep,
        up_send,
        up_bias_grad,
        down_grad_keep,
        down_grad_send,
    ) = pl.pallas_call(
        mlp_kernel,
        grid=(steps,),
        out_shape=[
            shaped((rows, width), F32),
            shaped((rows, width), F32),
            shaped((width, hidden_width // 2), BF16),
            shaped((width, hidden_width // 2), BF16),
            shaped((1, hidden_width), F32),
            shaped((hidden_width, half), BF16),
            shaped((hidden_width, half), BF16),
        ],
        in_specs=[
            SMEM,
            whole((rows, width)),
            whole((rows, width)),
            whole((rows, half)),
            whole((rows, half)),
            pl.BlockSpec((width, width), lambda i: (0, i)),
            pl.BlockSpec((1, width), lambda i: (0, i)),
            pl.BlockSpec((width, width), lambda i: (i, 0)),
        ],
        out_specs=[
            whole((rows, width)),
            whole((rows, width)),
            pl.BlockSpec((width, half), lambda i: (0, i)),
            pl.BlockSpec((width, half), lambda i: (0, i)),
            pl.BlockSpec((1, width), lambda i: (0, i)),
            pl.BlockSpec((width, half), lambda i: (i, 0)),
            pl.BlockSpec((width, half), lambda i: (i, 0)),
        ],
        compiler_params=params(),
        name="mlp",
    )(info, second, down_in, down_keep, down_send, up_weight, up_bias.reshape(1, -1), down_weight)
    up_got = swap(up_send, "band", 1)
    down_got = swap(down_grad_send, "band", 1)

    out_patches, out_own, middle_grad, attended_grad, out_keep, out_send, vectors = pl.pallas_call(
        partial(middle_back_kernel, slots),
        out_shape=[
            shaped((slots, width), BF16),
            shaped((pad, width), F32),
            shaped((rows, width), F32),
            shaped((rows, width), F32),
            shaped((width, half), BF16),
            shaped((width, half), BF16),
            shaped((8, width), F32),
        ],
        in_specs=[SMEM] + [VMEM] * 11,
        out_specs=[VMEM] * 7,
        compiler_params=params(),
        name="middle_back",
    )(
        info,
        middle,
        branch,
        branch_two,
        second_grad,
        incoming,
        attended,
        out_weight,
        down_bias,
        second_scale,
        second_gain,
        first_scale,
    )

    given = dict(
        info=info,
        weights=weights,
        queries=queries,
        keys=keys,
        values=values,
        attended=attended,
        totals=totals,
        attended_grad=attended_grad,
        mask=mask,
        first_gain=first_gain,
        vectors=vectors,
        down_bias_grad=down_bias_grad,
        up_bias_grad=up_bias_grad,
        out_own=out_own,
        up_keep=up_keep,
        up_got=up_got,
        down_keep=down_grad_keep,
        down_got=down_got,
        out_keep=out_keep,
        out_send=out_send,
        firsts_t=firsts_t,
        joint_weight=joint_weight,
        tokens=tokens,
        middle_grad=middle_grad,
    )
    backward = backward_fused if lax.axis_size("crop") == CROPS else backward_general
    (
        grad_patches,
        up,
        down,
        out,
        joint,
        rows_of,
        up_bias_sum,
        out_specials,
        grad_specials,
    ) = backward(given, slots, special_count)
    return (
        out_patches[None],
        out_specials,
        grad_patches[None],
        grad_specials,
        rows_of[5],
        rows_of[6],
        rows_of[7],
        joint,
        rows_of[8],
        rows_of[9],
        out,
        rows_of[4],
        rows_of[3],
        rows_of[1],
        rows_of[2],
        up,
        up_bias_sum,
        down,
        rows_of[10],
        rows_of[0],
    )


def solution(mesh):
    split = P("crop", "band", None)
    special = P("crop", None, None)
    in_specs = (
        (split, special, P("crop", "band")) + (P(),) * 17 + (split, special)
    )
    line, matrix = P("crop"), P("crop", None)
    out_specs = (
        split,
        special,
        split,
        special,
        line,
        line,
        line,
        matrix,
        line,
        line,
        matrix,
        line,
        line,
        line,
        line,
        matrix,
        line,
        matrix,
        line,
        line,
    )
    return jax.shard_map(body, mesh=mesh, in_specs=in_specs, out_specs=out_specs, check_vma=False)
```

```python
from functools import partial

import jax
import jax.numpy as jnp
from jax import lax
from jax.experimental import pallas as pl
from jax.experimental.pallas import tpu as pltpu
from jax.sharding import PartitionSpec as P

HEAD = 64
GRID = 37
PAIR = 2 * HEAD
BANDS = 4
KEY_PART = 256
F32 = jnp.float32
BF16 = jnp.bfloat16
VMEM_LIMIT = 60 << 20


def round_up(value, unit):
    return (value + unit - 1) // unit * unit


def params(semantics=None):
    return pltpu.CompilerParams(vmem_limit_bytes=VMEM_LIMIT)


def dot(a, b):
    return jnp.dot(a, b, preferred_element_type=F32)


def dot_nt(a, b):
    return lax.dot_general(a, b, (((1,), (1,)), ((), ())), preferred_element_type=F32)


def dot_tn(a, b):
    return lax.dot_general(a, b, (((0,), (0,)), ((), ())), preferred_element_type=F32)


def normalize(rows):
    centred = rows - jnp.mean(rows, axis=-1, keepdims=True)
    spread = jnp.mean(centred * centred, axis=-1, keepdims=True)
    scale = lax.rsqrt(spread + 1e-06)
    return centred * scale, scale


def normalize_back(grad, hat, scale):
    return scale * (
        grad
        - jnp.mean(grad, axis=-1, keepdims=True)
        - hat * jnp.mean(grad * hat, axis=-1, keepdims=True)
    )


def column_sum(rows):
    return jnp.sum(rows, axis=0, keepdims=True)


def line(ref):
    return ref[...].reshape(1, -1)


def whole(shape):
    return pl.BlockSpec(shape, lambda *_: (0,) * len(shape))


VMEM = pl.BlockSpec(memory_space=pltpu.VMEM)
ANY = pl.BlockSpec(memory_space=pl.ANY)
SMEM = pl.BlockSpec(memory_space=pltpu.SMEM)


def own_special(specials, band, slot):
    row = jnp.zeros((1, specials.shape[1]), F32)
    for special in range(specials.shape[0]):
        if special // BANDS == slot:
            row = row + jnp.where(band == special % BANDS, specials[special : special + 1], 0.0)
    return row


def place_rows(ref, patch_rows, specials, band):
    slots = patch_rows.shape[0]
    rows = ref.shape[0]
    ref[0:slots, :] = patch_rows
    extra = [own_special(specials, band, slot) for slot in range(rows - slots)]
    ref[slots:rows, :] = jnp.concatenate(extra, axis=0)


def counted_rows(info_ref, relative, rows, slots, width):
    index = lax.broadcasted_iota(jnp.int32, (rows, width), 0)
    used = index < info_ref[relative]
    special = (index >= slots) & (index < slots + info_ref[BANDS + relative])
    return used | special


def stack_pair(rows):
    lane = lax.broadcasted_iota(jnp.int32, rows.shape, 1)
    zero = jnp.zeros_like(rows)
    return jnp.concatenate(
        [jnp.where(lane < HEAD, rows, zero), jnp.where(lane >= HEAD, rows, zero)], axis=0
    )


def unstack_pair(rows):
    half = rows.shape[0] // 2
    lane = lax.broadcasted_iota(jnp.int32, (half, rows.shape[1]), 1)
    return jnp.where(lane < HEAD, rows[:half], rows[half:])


def mask_column(mask):
    return jnp.broadcast_to(mask[...].astype(F32), (8, mask.shape[1])).T[:, :1] > 0


def first_kernel(slots, info, mask, patches, specials, token, gain, shift, tokens, first):
    band = info[2 * BANDS]
    filled = jnp.where(mask_column(mask), line(token), patches[...].astype(F32))
    place_rows(tokens, filled, specials[...].astype(F32), band)
    hat, _ = normalize(tokens[...])
    counted = counted_rows(info, 0, tokens.shape[0], slots, tokens.shape[1])
    first[...] = jnp.where(counted, hat * line(gain) + line(shift), 0.0).astype(BF16)


def split_pairs(ref, rows, value):
    for pair in range(ref.shape[0]):
        ref[pair, rows, :] = value[:, pair * PAIR : (pair + 1) * PAIR].astype(BF16)


def project_keys(low, weight, value_bias, counted, keys, values, rows):
    width = weight.shape[0]
    split_pairs(keys, rows, dot(low, weight[:, width : 2 * width]))
    value = dot(low, weight[:, 2 * width :]) + line(value_bias)
    split_pairs(values, rows, jnp.where(counted, value, 0.0))


def attend_pair(queries, keys, values, ones):
    factor = HEAD ** (-0.5)
    stacked = stack_pair((queries.astype(F32) * factor).astype(BF16))
    low = jnp.exp(dot_nt(stacked, keys)).astype(BF16)
    summed = dot(low, jnp.concatenate([values, ones], axis=1))
    return low, unstack_pair(summed[:, :PAIR]), unstack_pair(summed[:, PAIR:])


def project_kernel(slots, info, first, weight, query_bias, value_bias, queries, keys, values):
    relative = pl.program_id(0)
    rows, width = first.shape
    counted = counted_rows(info, relative, rows, slots, width)
    low = first[...]

    @pl.when(relative == 0)
    def _():
        split_pairs(queries, slice(None), dot(low, weight[:, :width]) + line(query_bias))

    project_keys(low, weight, value_bias, counted, keys, values, slice(None))


def attend_kernel(
    slots, info, queries, keys, values, firsts, attended, totals, weights, firsts_t
):
    rows = queries.shape[1]
    ones = [
        counted_rows(info, r, rows, slots, PAIR).astype(F32).astype(BF16) for r in range(BANDS)
    ]
    low, summed, total = attend_pair(
        queries[0], keys[0], values[0], jnp.concatenate(ones, axis=0)
    )
    weights[0] = low
    firsts_t[...] = firsts[...].astype(F32).T.astype(BF16)
    attended[...] = summed / total
    totals[...] = total


def forward_kernel(
    slots,
    pairs,
    info,
    mask,
    patches,
    specials,
    token,
    gain,
    shift,
    query_bias,
    value_bias,
    weight_in,
    tokens_out,
    queries_out,
    keys_out,
    values_out,
    attended,
    totals,
    weights,
    firsts_t,
    tokens,
    firsts,
    queries,
    keys,
    values,
    ones,
    sums,
    counts,
    weight,
    send_sems,
    recv_sems,
    sems,
):
    step = pl.program_id(0)
    rows, width = tokens.shape
    half_rows = 2 * rows
    place = Place()
    sender = Sender(place, send_sems, recv_sems)
    sender.add("near", firsts.at[0], firsts.at[1], "core")
    sender.add("far", firsts.at[0], firsts.at[2], "x")
    sender.add("diagonal", firsts.at[2], firsts.at[3], "core")
    weight_load = lambda: pltpu.make_async_copy(weight_in, weight, sems.at[0])
    stores = lambda: [
        pltpu.make_async_copy(a, b, sems.at[i])
        for i, (a, b) in enumerate(
            ((tokens, tokens_out), (queries, queries_out), (keys, keys_out), (values, values_out)), 1
        )
    ]

    def block_keys(block):
        counted = counted_rows(info, block, rows, slots, width)
        span = pl.ds(block * rows, rows)
        project_keys(firsts[block], weight, value_bias, counted, keys, values, span)

    @pl.when(step == 0)
    def _():
        weight_load().start()
        filled = jnp.where(mask_column(mask), line(token), patches[...].astype(F32))
        place_rows(tokens, filled, specials[...].astype(F32), place.band)
        hat, _ = normalize(tokens[...])
        counted = counted_rows(info, 0, rows, slots, width)
        firsts[0] = jnp.where(counted, hat * line(gain) + line(shift), 0.0).astype(BF16)
        place.greet(("core", "x"))
        sender.send("near")
        sender.send("far")
        for block in range(BANDS):
            used = counted_rows(info, block, rows, slots, PAIR)
            ones[block * rows : (block + 1) * rows, :] = used.astype(F32).astype(BF16)
        weight_load().wait()
        split_pairs(queries, slice(None), dot(firsts[0], weight[:, :width]) + line(query_bias))
        block_keys(0)
        sender.arrived("near")
        block_keys(1)

    @pl.when(step == pairs)
    def _():
        sender.arrived("far")
        sender.send("diagonal")
        block_keys(2)
        sender.arrived("diagonal")
        block_keys(3)
        for copy in stores():
            copy.start()

    far_half = step >= pairs
    pair = jnp.where(far_half, step - pairs, step)
    first_row = pl.multiple_of(jnp.where(far_half, half_rows, 0), half_rows)
    span = pl.ds(first_row, half_rows)
    low, summed, total = attend_pair(
        queries[pair], keys[pair, span], values[pair, span], ones[span, :]
    )
    weights[0] = low
    first_block = jnp.where(far_half, 2, 0)
    lane = pl.ds(pl.multiple_of(pair * PAIR, PAIR), PAIR)
    columns = [firsts[first_block + i, :, lane] for i in range(2)]
    firsts_t[...] = jnp.concatenate(columns, axis=0).astype(F32).T.astype(BF16)

    @pl.when(step < pairs)
    def _():
        sums[pair] = summed
        counts[pair] = total

    @pl.when(far_half)
    def _():
        whole_total = counts[pair] + total
        attended[...] = (sums[pair] + summed) / whole_total
        totals[...] = whole_total

    @pl.when(step == 2 * pairs - 1)
    def _():
        sender.finish()
        for copy in stores():
            copy.wait()


def middle_kernel(
    slots,
    info,
    attended,
    tokens,
    weight,
    bias,
    first_scale,
    gain,
    shift,
    second_scale,
    cot_patches,
    cot_specials,
    branch,
    middle,
    second,
    incoming,
    down_in,
    down_keep,
    down_send,
    down_bias_grad,
):
    rows = tokens.shape[0]
    band = info[2 * BANDS]
    side = dot(attended[...].astype(BF16), weight[...]) + line(bias)
    branch[...] = side
    mid = tokens[...] + line(first_scale) * side
    middle[...] = mid
    hat, _ = normalize(mid)
    second[...] = (hat * line(gain) + line(shift)).astype(BF16)
    counted = counted_rows(info, 0, slots, slots, tokens.shape[1])
    given = jnp.where(counted, cot_patches[...].astype(F32), 0.0)
    place_rows(incoming, given, cot_specials[...].astype(F32), band)
    low = (incoming[...] * line(second_scale)).astype(BF16)
    down_in[...] = low
    keep, send = own_half(low, band)
    down_keep[...] = keep
    down_send[...] = send
    down_bias_grad[...] = column_sum(low.astype(F32))


def own_half(rows, band):
    half = rows.shape[1] // 2
    first = lax.rem(band, 2) == 0
    low, high = rows[:, :half], rows[:, half:]
    return jnp.where(first, low, high), jnp.where(first, high, low)


def gelu_and_slope(x):
    phi = 0.5 + 0.5 * lax.erf(x * 0.7071067811865476)
    density = jnp.exp(-0.5 * x * x) * 0.3989422804014327
    return x * phi, phi + x * density


def mlp_kernel(
    info,
    second,
    down_in,
    down_keep,
    down_send,
    up,
    up_bias,
    down,
    branch_two,
    second_grad,
    up_grad_keep,
    up_grad_send,
    up_bias_grad,
    down_grad_keep,
    down_grad_send,
):
    step = pl.program_id(0)
    low = second[...]
    hidden = dot(low, up[...]) + up_bias[...]
    active, slope = gelu_and_slope(hidden)
    active = active.astype(BF16)
    hidden_in = (slope * dot_nt(down_in[...], down[...])).astype(BF16)

    @pl.when(step == 0)
    def _():
        branch_two[...] = jnp.zeros_like(branch_two)
        second_grad[...] = jnp.zeros_like(second_grad)

    branch_two[...] += dot(active, down[...])
    second_grad[...] += dot_nt(hidden_in, up[...])
    keep, send = own_half(hidden_in, info[2 * BANDS])
    up_grad_send[...] = dot_tn(low, send).astype(BF16)
    up_grad_keep[...] = dot_tn(low, keep).astype(BF16)
    down_grad_send[...] = dot_tn(active, down_send[...]).astype(BF16)
    down_grad_keep[...] = dot_tn(active, down_keep[...]).astype(BF16)
    up_bias_grad[...] = column_sum(hidden_in.astype(F32))


def middle_back_kernel(
    slots,
    info,
    middle,
    branch,
    branch_two,
    second_grad,
    incoming,
    attended,
    weight,
    down_bias,
    second_scale,
    gain,
    first_scale,
    out_patches,
    out_specials,
    middle_grad,
    attended_grad,
    out_keep,
    out_send,
    vectors,
    between=lambda part: None,
):
    mid = middle[...]
    given = incoming[...]
    two = branch_two[...] + line(down_bias)
    output = mid + line(second_scale) * two
    counted = counted_rows(info, 0, slots, slots, mid.shape[1])
    out_patches[...] = jnp.where(counted, output[:slots], 0.0).astype(BF16)
    out_specials[...] = output[slots:]
    hat, scale = normalize(mid)
    grad = second_grad[...]
    back = given + normalize_back(grad * line(gain), hat, scale)
    middle_grad[...] = back
    between(0)
    out_in = (back * line(first_scale)).astype(BF16)
    attended_grad[...] = dot_nt(out_in, weight[...])
    between(1)
    keep, send = own_half(out_in, info[2 * BANDS])
    low = attended[...].astype(BF16)
    out_keep[...] = dot_tn(low, keep).astype(BF16)
    out_send[...] = dot_tn(low, send).astype(BF16)
    between(2)
    vectors[...] = jnp.concatenate(
        [
            column_sum(given * two),
            column_sum(grad * hat),
            column_sum(grad),
            column_sum(back * branch[...]),
            column_sum(out_in.astype(F32)),
            jnp.zeros((3, mid.shape[1]), F32),
        ],
        axis=0,
    )


def attend_back_pair(weights, queries, keys, values, attended, totals, attended_grad, outs, between):
    key_grad, value_grad = outs
    queries, keys, values = queries.at[0], keys.at[0], values.at[0]
    rows = queries.shape[0]
    factor = HEAD ** (-0.5)
    stacked = stack_pair((queries[...].astype(F32) * factor).astype(BF16))
    scaled = attended_grad[...] / totals[...]
    returned = stack_pair(scaled.astype(BF16))
    slope = jnp.sum(stack_pair(scaled * attended[...]), axis=1, keepdims=True)
    stacked_t = stacked.astype(F32).T.astype(BF16)
    returned_t = returned.astype(F32).T.astype(BF16)
    total = jnp.zeros((2 * rows, PAIR), F32)
    start = 0
    for part, size in enumerate(key_parts(keys.shape[0])):
        span = slice(start, start + size)
        start += size
        low = weights[0, :, span]
        moved = dot_nt(returned, values[span, :])
        scores = (low.astype(F32) * (moved - slope)).astype(BF16)
        total = total + dot(scores, keys[span, :])
        key_grad[span, :] = dot(stacked_t, scores).T.astype(BF16)
        value_grad[span, :] = dot(returned_t, low).T.astype(BF16)
        between(part)
    return unstack_pair(total) * factor


def key_parts(count):
    parts = [KEY_PART] * (count // KEY_PART)
    if count % KEY_PART:
        parts[-1] += count % KEY_PART
    return parts


def first_part(block, rows, query_grad, key_grad, value_grad, weight):
    width = weight.shape[0]
    span = slice(block * rows, (block + 1) * rows)
    part = jnp.zeros((rows, width), F32)
    for pair in range(0, width // PAIR, 2):
        for offset, grad in ((width, key_grad), (2 * width, value_grad), (0, query_grad)):
            if offset == 0 and block > 0:
                continue
            at = slice(0, rows) if offset == 0 else span
            low = jnp.concatenate([grad[pair, at, :], grad[pair + 1, at, :]], axis=1)
            columns = slice(offset + pair * PAIR, offset + (pair + 2) * PAIR)
            part = part + dot_nt(low, weight[:, columns])
    return part


def own_pair_first(part, band):
    core = lax.rem(band, 2)
    return 2 * part + core, 2 * part + 1 - core


def joint_columns(firsts_t, query_grad, key_grad, value_grad, pairs):
    rows = query_grad.shape[1]
    queries = dot(firsts_t[:, :rows], jnp.concatenate([query_grad[p] for p in pairs], axis=1))
    results = []
    for index, p in enumerate(pairs):
        others = dot(firsts_t[...], jnp.concatenate([key_grad[p], value_grad[p]], axis=1))
        own = queries[:, index * PAIR : (index + 1) * PAIR]
        results.append(jnp.concatenate([own, others], axis=1).astype(BF16))
    return results


def first_back(slots, info, grad, tokens, middle_grad, mask, gain):
    rows, width = tokens.shape
    grad = jnp.where(counted_rows(info, 0, rows, slots, width), grad, 0.0)
    hat, scale = normalize(tokens[...])
    token_grad = middle_grad[...] + normalize_back(grad * line(gain), hat, scale)
    masked = mask_column(mask)
    patch_grad = token_grad[:slots]
    patches = jnp.where(masked, 0.0, patch_grad).astype(BF16)
    vectors = [
        column_sum(jnp.where(masked, patch_grad, 0.0)),
        column_sum(grad * hat),
        column_sum(grad),
    ]
    return patches, token_grad[slots:], vectors


def bias_sums(info, slots, rows, query_grad, value_grad):
    ones = [
        counted_rows(info, block, rows, slots, PAIR).astype(F32).astype(BF16)
        for block in range(BANDS)
    ]
    ones = jnp.concatenate(ones, axis=0)
    pairs = range(query_grad.shape[0])
    queries = [column_sum(query_grad[pair].astype(F32)) for pair in pairs]
    values = [dot_tn(ones, value_grad[pair])[0:1] for pair in pairs]
    both = [jnp.concatenate(queries, axis=1), jnp.concatenate(values, axis=1)]
    return jnp.concatenate(both + [jnp.zeros((6, both[0].shape[1]), F32)], axis=0)


def swap(x, axis, distance):
    size = lax.axis_size(axis)
    return lax.ppermute(x, axis, [(i, i ^ distance) for i in range(size)])


def halve(x, axis, distance):
    bit = (lax.axis_index(axis) // distance) % 2
    sent = lax.dynamic_index_in_dim(x, 1 - bit, 0, keepdims=False)
    kept = lax.dynamic_index_in_dim(x, bit, 0, keepdims=False)
    got = swap(sent, axis, distance)
    return (kept.astype(F32) + got.astype(F32)).astype(BF16)


def reduce_half(kept, got, columns):
    held = (kept.astype(F32) + got.astype(F32)).astype(BF16)
    rows, half = held.shape
    crops = lax.axis_size("crop")
    held = held.reshape((crops, rows // crops, half))
    distance = 1
    while distance < crops:
        count = held.shape[0]
        held = jnp.moveaxis(held.reshape((count // 2, 2) + held.shape[1:]), 1, 0)
        held = halve(held, "crop", distance)
        distance *= 2
    held = held.reshape((rows // crops, half))
    other = swap(held, "band", 2)
    full = (held.astype(F32) + other.astype(F32)).astype(BF16)
    mate = swap(full, "band", 1)
    bit = lax.axis_index("band") % 2
    low = jnp.where(bit == 0, full, mate).astype(F32).reshape(rows // crops, -1, columns)
    high = jnp.where(bit == 0, mate, full).astype(F32).reshape(rows // crops, -1, columns)
    return jnp.stack([low, high], axis=2).reshape(rows // crops, 2 * half)


def gather_blocks(x):
    near = swap(x, "band", 1)
    far = swap(x, "band", 2)
    diagonal = swap(far, "band", 1)
    return jnp.concatenate([x, near, far, diagonal], axis=0)


def scatter_blocks(x):
    rows = x.shape[0] // BANDS
    got = swap(jnp.concatenate([x[rows : 2 * rows], x[3 * rows :]], axis=0), "band", 1)
    own = x[:rows].astype(F32) + got[:rows].astype(F32)
    far = (x[2 * rows : 3 * rows].astype(F32) + got[rows:].astype(F32)).astype(BF16)
    return own + swap(far, "band", 2).astype(F32)


def reduce_small(vectors, more, down_bias, up_bias, out_own, grad_own, special_count):
    crops = lax.axis_size("crop")
    width = vectors.shape[1]
    owned = -(-special_count // BANDS)
    both = jnp.concatenate([out_own[:owned], grad_own[:owned]], axis=1).astype(BF16)
    both = lax.all_gather(both, "band", axis=0, tiled=False)
    both = jnp.transpose(both, (1, 0, 2)).reshape(owned * BANDS, 2 * width)[:special_count]
    plain = jnp.concatenate([vectors[:5], more[:5], down_bias], axis=0)
    plain = jnp.transpose(plain.reshape(11, crops, -1), (1, 0, 2)).reshape(crops, -1)
    packed = jnp.concatenate([plain, up_bias.reshape(crops, -1)], axis=1)
    packed = lax.psum_scatter(packed, "crop", scatter_dimension=0, tiled=False)
    packed = lax.psum(packed, "band")
    part = width // crops
    rows = [packed[i * part : (i + 1) * part] for i in range(11)]
    return rows, packed[11 * part :], both[None, :, :width], both[None, :, width:]


def attend_back_kernel(
    weights, queries, keys, values, attended, totals, attended_grad, query_grad, key_grad, value_grad
):
    inputs = (weights, queries, keys, values, attended, totals, attended_grad)
    part = attend_back_pair(*inputs, (key_grad.at[0], value_grad.at[0]), lambda part: None)
    query_grad[0] = part.astype(BF16)


def joint_back_kernel(
    slots, info, firsts_t, query_grad, key_grad, value_grad, weight, joint_keep, joint_send, first_grad, sums
):
    rows, width = query_grad.shape[1], weight.shape[0]
    for block in range(BANDS):
        part = first_part(block, rows, query_grad, key_grad, value_grad, weight)
        first_grad[block * rows : (block + 1) * rows, :] = part.astype(BF16)
    third = 3 * PAIR
    for part in range(query_grad.shape[0] // 2):
        keep, send = joint_columns(
            firsts_t, query_grad, key_grad, value_grad, own_pair_first(part, info[2 * BANDS])
        )
        joint_keep[:, part * third : (part + 1) * third] = keep
        joint_send[:, part * third : (part + 1) * third] = send
    sums[...] = bias_sums(info, slots, rows, query_grad, value_grad)


def first_back_kernel(
    slots, info, first_grad, tokens, middle_grad, mask, gain, sums, patches, specials, vectors
):
    grads, special_grad, rows = first_back(
        slots, info, first_grad[...], tokens, middle_grad, mask, gain
    )
    patches[...] = grads
    specials[...] = special_grad
    vectors[...] = jnp.concatenate(rows + [sums[0:5]], axis=0)


def joint_order(x):
    rows, columns = x.shape
    x = x.reshape(rows, columns // (3 * PAIR), 3, PAIR)
    return jnp.transpose(x, (0, 2, 1, 3)).reshape(rows, columns)


def backward_general(given, slots, special_count):
    g = given
    rows, width = g["tokens"].shape
    every = BANDS * rows
    pairs = width // PAIR
    shaped = jax.ShapeDtypeStruct
    own_pair = pl.BlockSpec((rows, PAIR), lambda i: (0, i))
    grads = pl.pallas_call(
        attend_back_kernel,
        grid=(pairs,),
        out_shape=[
            shaped((pairs, rows, PAIR), BF16),
            shaped((pairs, every, PAIR), BF16),
            shaped((pairs, every, PAIR), BF16),
        ],
        in_specs=[
            pl.BlockSpec((1, 2 * rows, every), lambda i: (i, 0, 0)),
            pl.BlockSpec((1, rows, PAIR), lambda i: (i, 0, 0)),
            pl.BlockSpec((1, every, PAIR), lambda i: (i, 0, 0)),
            pl.BlockSpec((1, every, PAIR), lambda i: (i, 0, 0)),
            own_pair,
            own_pair,
            own_pair,
        ],
        out_specs=[
            pl.BlockSpec((1, rows, PAIR), lambda i: (i, 0, 0)),
            pl.BlockSpec((1, every, PAIR), lambda i: (i, 0, 0)),
            pl.BlockSpec((1, every, PAIR), lambda i: (i, 0, 0)),
        ],
        compiler_params=params(),
        name="attend_back",
    )(
        g["weights"],
        g["queries"],
        g["keys"],
        g["values"],
        g["attended"],
        g["totals"],
        g["attended_grad"],
    )
    half = width // 2
    joint_keep, joint_send, parts, sums = pl.pallas_call(
        partial(joint_back_kernel, slots),
        out_shape=[
            shaped((width, 3 * half), BF16),
            shaped((width, 3 * half), BF16),
            shaped((every, width), BF16),
            shaped((8, width), F32),
        ],
        in_specs=[SMEM] + [VMEM] * 5,
        out_specs=[VMEM] * 4,
        compiler_params=params(),
        name="joint_back",
    )(g["info"], g["firsts_t"], *grads, g["joint_weight"])
    grad_patches, grad_own, more = pl.pallas_call(
        partial(first_back_kernel, slots),
        out_shape=[
            shaped((slots, width), BF16),
            shaped((rows - slots, width), F32),
            shaped((8, width), F32),
        ],
        in_specs=[SMEM] + [VMEM] * 6,
        out_specs=[VMEM] * 3,
        compiler_params=params(),
        name="first_back",
    )(
        g["info"],
        scatter_blocks(parts),
        g["tokens"],
        g["middle_grad"],
        g["mask"],
        g["first_gain"],
        sums,
    )
    small = reduce_small(
        g["vectors"],
        more,
        g["down_bias_grad"],
        g["up_bias_grad"],
        g["out_own"],
        grad_own,
        special_count,
    )
    matrices = (
        reduce_half(g["mlp_grads"]["up_keep"], g["mlp_grads"]["up_got"], half),
        reduce_half(g["mlp_grads"]["down_keep"], g["mlp_grads"]["down_got"], half),
        reduce_half(g["out_keep"], swap(g["out_send"], "band", 1), half),
        joint_order(reduce_half(joint_keep, swap(joint_send, "band", 1), half)),
    )
    return (grad_patches,) + matrices + small


MESH = pl.DeviceIdType.MESH
CROPS = 8
X_FIRST = (1, 3, 5, 7, 8, 9)
DIRECT = (9, 10, 11)
NEIGHBOURS = ("core", "x", "diagonal")
PLACES = NEIGHBOURS + tuple(range(1, CROPS))


class Place:
    def __init__(self):
        band, crop = lax.axis_index("band"), lax.axis_index("crop")
        self.band = band
        self.core, self.x = lax.rem(band, 2), lax.div(band, 2)
        self.y, self.near, self.far = lax.rem(crop, 2), lax.rem(lax.div(crop, 2), 2), lax.div(crop, 4)
        core_step, x_step = 1 - 2 * self.core, 2 - 4 * self.x
        self.device = {
            "core": (band + core_step, crop),
            "x": (band + x_step, crop),
            "diagonal": (band + core_step + x_step, crop),
            "y": (band, crop + 1 - 2 * self.y),
            "near": (band, crop + 2 - 4 * self.near),
            "far": (band, crop + 4 - 8 * self.far),
        }
        self.crop = crop
        for step in range(1, CROPS):
            self.device[step] = (band, lax.rem(crop + step, CROPS))

    def greet(self, names):
        barrier = pltpu.get_barrier_semaphore()
        for name in names:
            pl.semaphore_signal(barrier, inc=1, device_id=self.device[name], device_id_type=MESH)
        pl.semaphore_wait(barrier, len(names))


class Sender:
    def __init__(self, place, send_sems, recv_sems):
        self.place, self.send_sems, self.recv_sems = place, send_sems, recv_sems
        self.routes = {}
        self.sent = []

    def add(self, key, source, target, name):
        self.routes[key] = (len(self.routes), source, target, name)

    def copy(self, key):
        index, source, target, name = self.routes[key]
        return pltpu.make_async_remote_copy(
            src_ref=source,
            dst_ref=target,
            send_sem=self.send_sems.at[index],
            recv_sem=self.recv_sems.at[index],
            device_id=self.place.device[name],
            device_id_type=MESH,
        )

    def send(self, key):
        self.copy(key).start()
        self.sent.append(key)

    def arrived(self, key):
        self.copy(key).wait_recv()

    def left(self, key):
        self.copy(key).wait_send()
        self.sent.remove(key)

    def finish(self):
        for key in self.sent:
            self.copy(key).wait_send()


def chunk_list(hidden_parts):
    chunks = []
    for part in range(hidden_parts):
        chunks += [("down", part), ("up", part)]
    return chunks + [("out", 0), ("joint", 0), ("joint", 1), ("joint", 2)]


def chunk_scratch(count, rows, columns):
    unit = (rows, columns)
    return [
        pltpu.VMEM((count, 2, 2, 2, 2) + unit, BF16),
        pltpu.VMEM((count, 2, 2, 2) + unit, BF16),
        pltpu.VMEM((count, 2, 2) + unit, BF16),
        pltpu.VMEM((count, 2) + unit, BF16),
        pltpu.VMEM((count, 3, 2) + unit, BF16),
    ]


class ChunkSums:
    def __init__(self, place, sender, buffers, total, count):
        p, self.sender, self.place, self.total = place, sender, place, total
        own, got_a, got_b, got_c, got_d = buffers
        self.got_d = got_d
        self.table = {}
        for n in range(count):
            both, half = total.at[n, p.core], total.at[n, p.core, p.x]
            if x_first(n):
                kept = [
                    own.at[n, p.x],
                    own.at[n, p.x, :, :, p.y],
                    own.at[n, p.x, :, p.near, p.y],
                    own.at[n, p.x, p.far, p.near, p.y],
                ]
                got = [got_a.at[n], got_b.at[n], got_c.at[n], got_d.at[n, 0, 0]]
                sent = [
                    own.at[n, 1 - p.x],
                    own.at[n, p.x, :, :, 1 - p.y],
                    own.at[n, p.x, :, 1 - p.near, p.y],
                    own.at[n, p.x, 1 - p.far, p.near, p.y],
                ]
                names = ("x", "y", "near", "far")
            else:
                kept = [
                    own.at[n, :, :, p.y],
                    own.at[n, :, p.near, p.y],
                    own.at[n, p.far, p.near, p.y],
                ]
                got = [got_a.at[n], got_b.at[n], got_c.at[n]]
                sent = [
                    own.at[n, :, :, 1 - p.y],
                    own.at[n, :, 1 - p.near, p.y],
                    own.at[n, 1 - p.far, p.near, p.y],
                ]
                names = ("y", "near", "far")
            rows = [(None, None, None, [(sent[0], got[0], names[0])])]
            for i in range(1, len(names)):
                add = (kept[i - 1], kept[i - 1], got[i - 1])
                rows.append(add + ([(sent[i], got[i], names[i])],))
            end = (kept[-1], got[-1])
            if direct(n):
                targets = [half] * 3 if x_first(n) else [got_d.at[n, i] for i in range(3)]
                last = half if x_first(n) else both
                rows.append((last,) + end + ([(last, t, m) for t, m in zip(targets, NEIGHBOURS)],))
            elif x_first(n):
                rows.append((half,) + end + ([(half, half, "x")],))
                rows.append((None, None, None, [(both, both, "core")]))
            else:
                rows.append((kept[-1],) + end + ([(kept[-1], got_d.at[n, 0], "x")],))
                rows.append((both, kept[-1], got_d.at[n, 0], [(both, both, "core")]))
            self.table[n] = rows
            for stage, row in enumerate(rows):
                for i, (source, target, name) in enumerate(row[3]):
                    sender.add((n, stage + 1, i), source, target, name)

    def steps(self, n):
        return len(self.table[n]) + 1

    def step(self, n, stage):
        rows, sender = self.table[n], self.sender
        if stage > 0:
            for i in range(len(rows[stage - 1][3])):
                sender.arrived((n, stage, i))
        if stage == len(rows):
            if direct(n) and not x_first(n):
                for i in range(3):
                    sender.left((n, stage, i))
                p, total, got = self.place, self.total, self.got_d
                total[n, p.core] = total[n, p.core] + got[n, 1]
                total[n, 1 - p.core] = got[n, 0] + got[n, 2]
            return
        into, kept, got, sent = rows[stage]
        if into is not None:
            into[...] = kept[...] + got[...]
        for i in range(len(sent)):
            sender.send((n, stage + 1, i))


class VectorSums:
    def __init__(self, place, sender, buffers, total):
        self.place, self.sender, self.total = place, sender, total
        self.own, self.got, self.parts = buffers
        for step in range(1, CROPS):
            source = self.own.at[lax.rem(place.crop + step, CROPS)]
            sender.add(("vector", step), source, self.got.at[place.crop], step)
        here = self.parts.at[place.band]
        for name in NEIGHBOURS:
            sender.add(("parts", name), here, here, name)

    def spread(self):
        for step in range(1, CROPS):
            self.sender.send(("vector", step))

    def share(self):
        p = self.place
        self.got[p.crop] = self.own[p.crop]
        for step in range(1, CROPS):
            self.sender.arrived(("vector", step))
        self.parts[p.band] = jnp.sum(self.got[...], axis=0)
        for name in NEIGHBOURS:
            self.sender.send(("parts", name))

    def close(self):
        for name in NEIGHBOURS:
            self.sender.arrived(("parts", name))
        self.total[...] = jnp.sum(self.parts[...], axis=0)


def pack_vectors(own, rows, up_bias, part):
    for crop in range(CROPS):
        span = slice(crop * part, (crop + 1) * part)
        wide = 4 * crop * part
        wider = [up_bias[0:1, wide + j * part : wide + (j + 1) * part] for j in range(4)]
        own[crop, 0:15, 0:part] = jnp.concatenate([rows[:, span]] + wider, axis=0)


def vector_scratch():
    return [
        pltpu.VMEM((CROPS, 16, 128), F32),
        pltpu.VMEM((CROPS, 16, 128), F32),
        pltpu.VMEM((BANDS, 16, 128), F32),
    ]


def x_first(n):
    return n in X_FIRST


def direct(n):
    return n in DIRECT


def halves_of(n):
    return (0, 1) if x_first(n) else (None,)


def part_of(ref, name, part, columns, x_half):
    at = slice(None) if x_half is None else x_half
    if name == "down":
        return ref.at[:, :, :, part, at]
    return ref.at[:, :, :, at, :, pl.ds(part * columns, columns)]


def piece(ref, x_half):
    return ref if x_half is None else ref.at[x_half]


def middle_all_kernel(
    chunks,
    slots,
    parts,
    info,
    attended,
    tokens,
    out_weight,
    out_bias,
    first_scale,
    gain,
    shift,
    second_scale,
    cot_patches,
    cot_specials,
    down_bias,
    up,
    up_bias,
    down,
    out_patches,
    out_specials,
    middle_grad,
    attended_grad,
    out_keep,
    out_send,
    vectors,
    down_bias_grad,
    up_bias_grad,
    kept_out,
    sent_out,
    *scratch,
):
    (
        kept,
        sent,
        branch,
        middle,
        second,
        second_t,
        incoming,
        down_in,
        down_keep,
        down_send,
        branch_two,
        second_grad,
        active_t,
        store_sems,
    ) = scratch
    step = pl.program_id(0)
    width = tokens.shape[1]
    count = kept.shape[0]
    band = lax.axis_index("band")

    def stores(n):
        return [
            pltpu.make_async_copy(kept.at[n], kept_out.at[n], store_sems.at[0, n]),
            pltpu.make_async_copy(sent.at[n], sent_out.at[n], store_sems.at[1, n]),
        ]

    def made(n, value, x_halves):
        shape = (2, 2, 2, 2, width // CROPS // 2, width // 2)
        for half, target in zip(own_half(value, band), (kept.at[n], sent.at[n])):
            half = half.reshape(shape)
            if x_halves:
                for h in range(2):
                    target[h] = half[:, :, :, h]
            else:
                target[...] = half
        for copy in stores(n):
            copy.start()

    @pl.when(step == 0)
    def _():
        middle_kernel(
            slots,
            info,
            attended,
            tokens,
            out_weight,
            out_bias,
            first_scale,
            gain,
            shift,
            second_scale,
            cot_patches,
            cot_specials,
            branch,
            middle,
            second,
            incoming,
            down_in,
            down_keep,
            down_send,
            down_bias_grad,
        )
        second_t[...] = second[...].astype(F32).T.astype(BF16)
        branch_two[...] = jnp.zeros_like(branch_two)
        second_grad[...] = jnp.zeros_like(second_grad)

    @pl.when(step < parts)
    def _():
        hidden = dot(second[...], up[...]) + up_bias[...]
        active, slope = gelu_and_slope(hidden)
        active = active.astype(BF16)
        span = pl.ds(pl.multiple_of(step * width, width), width)
        active_t[span, :] = active.astype(F32).T.astype(BF16)
        hidden_in = (slope * dot_nt(down_in[...], down[...])).astype(BF16)
        made(2 * step + 1, dot(second_t[...], hidden_in).astype(BF16), True)
        branch_two[...] += dot(active, down[...])
        second_grad[...] += dot_nt(hidden_in, up[...])
        up_bias_grad[...] = column_sum(hidden_in.astype(F32))

    @pl.when((step >= parts) & (step < 2 * parts))
    def _():
        part = step - parts
        own_rows = width // CROPS
        starts = [
            pl.multiple_of((crop * parts + part) * own_rows, own_rows) for crop in range(CROPS)
        ]
        rows = jnp.concatenate([active_t[pl.ds(i, own_rows), :] for i in starts], axis=0)
        made(2 * part, dot(rows, down_in[...]).astype(BF16), False)

    @pl.when(step == 2 * parts)
    def _():
        middle_back_kernel(
            slots,
            info,
            middle,
            branch,
            branch_two,
            second_grad,
            incoming,
            attended,
            out_weight,
            down_bias,
            second_scale,
            gain,
            first_scale,
            out_patches,
            out_specials,
            middle_grad,
            attended_grad,
            out_keep,
            out_send,
            vectors,
        )
        for n in range(count):
            for copy in stores(n):
                copy.wait()


def middle_fused(
    info,
    attended,
    tokens,
    out_weight,
    out_bias,
    first_scale,
    second_gain,
    second_shift,
    second_scale,
    cot_patches,
    cot_specials,
    down_bias,
    up_weight,
    up_bias,
    down_weight,
):
    rows, width = tokens.shape
    slots = cot_patches.shape[0]
    hidden_width = up_weight.shape[1]
    parts = hidden_width // width
    chunks = chunk_list(parts)
    count = 2 * parts
    unit_rows, half = width // CROPS // 2, width // 2
    unit = (2, 2, 2, 2, unit_rows, half)
    shaped = jax.ShapeDtypeStruct
    last = parts - 1
    outs = pl.pallas_call(
        partial(middle_all_kernel, chunks, slots, parts),
        grid=(2 * parts + 1,),
        out_shape=[
            shaped((slots, width), BF16),
            shaped((rows - slots, width), F32),
            shaped((rows, width), F32),
            shaped((rows, width), F32),
            shaped((width, half), BF16),
            shaped((width, half), BF16),
            shaped((8, width), F32),
            shaped((1, width), F32),
            shaped((1, hidden_width), F32),
            shaped((count,) + unit, BF16),
            shaped((count,) + unit, BF16),
        ],
        in_specs=[SMEM]
        + [VMEM] * 11
        + [
            pl.BlockSpec((width, width), lambda i: (0, jnp.minimum(i, last))),
            pl.BlockSpec((1, width), lambda i: (0, jnp.minimum(i, last))),
            pl.BlockSpec((width, width), lambda i: (jnp.minimum(i, last), 0)),
        ],
        out_specs=[VMEM] * 8 + [pl.BlockSpec((1, width), lambda i: (0, jnp.minimum(i, last))), ANY, ANY],
        scratch_shapes=[
            pltpu.VMEM((count,) + unit, BF16),
            pltpu.VMEM((count,) + unit, BF16),
            pltpu.VMEM((rows, width), F32),
            pltpu.VMEM((rows, width), F32),
            pltpu.VMEM((rows, width), BF16),
            pltpu.VMEM((width, rows), BF16),
            pltpu.VMEM((rows, width), F32),
            pltpu.VMEM((rows, width), BF16),
            pltpu.VMEM((rows, half), BF16),
            pltpu.VMEM((rows, half), BF16),
            pltpu.VMEM((rows, width), F32),
            pltpu.VMEM((rows, width), F32),
            pltpu.VMEM((hidden_width, rows), BF16),
            pltpu.SemaphoreType.DMA((2, count)),
        ],
        compiler_params=params(),
        name="middle_all",
    )(
        info,
        attended,
        tokens,
        out_weight,
        out_bias,
        first_scale,
        second_gain,
        second_shift,
        second_scale,
        cot_patches,
        cot_specials,
        down_bias,
        up_weight,
        up_bias,
        down_weight,
    )
    return tuple(outs[:9]) + (outs[9:],)


PLAN = (
    (2, 1, 0), (2, 0, 0), (3, 3, 0), (4, 2, 0), (9, 5, 0), (9, 4, 0),
    (10, 1, 1), (10, 0, 1), (14, 7, 0), (16, 0, 2), (16, 3, 1), (16, 2, 1),
    (18, 6, 0), (18, 8, 0), (18, 0, 3), (19, 5, 1), (19, 4, 1), (19, 2, 2),
    (22, 1, 2), (24, 4, 2), (24, 7, 1), (24, 3, 2), (24, 2, 3), (25, 1, 3),
    (26, 9, 0), (28, 8, 1), (28, 6, 1), (28, 3, 3), (28, 4, 3), (29, 0, 4),
    (29, 1, 4), (30, 5, 2), (30, 0, 5), (31, 6, 2), (31, 7, 2), (31, 3, 4),
    (32, 10, 0), (33, 5, 3), (33, 8, 2), (36, 6, 3), (36, 7, 3), (36, 5, 4),
    (37, 8, 3), (38, 11, 0), (38, 10, 1), (39, 2, 4), (39, 7, 4), (40, 8, 4),
    (40, 2, 5), (40, 10, 2), (40, 9, 1), (44, 4, 4), (44, 11, 1), (45, 1, 5),
    (47, 3, 5), (48, 6, 4), (49, 4, 5), (50, 5, 5), (51, 10, 3), (52, 9, 2),
    (53, 1, 6), (54, 7, 5), (55, 3, 6), (56, 8, 5), (57, 6, 5), (58, 11, 2),
    (59, 5, 6), (60, 7, 6), (61, 9, 3), (62, 8, 6), (63, 10, 4), (64, 11, 3),
    (65, 9, 4), (66, 11, 4), (67, 9, 5),
)


def backward_kernel(
    chunks,
    slots,
    pairs,
    info,
    weights,
    queries,
    keys,
    values,
    attended,
    totals,
    attended_grad,
    mask,
    gain,
    vectors,
    down_bias,
    up_bias,
    out_own,
    kept_in,
    sent_in,
    out_keep,
    out_send,
    firsts_in,
    weight_in,
    tokens_in,
    middle_grad_in,
    grad_patches,
    total_out,
    vector_total,
    specials_out,
    *scratch,
):
    buffers, vector_buffers = scratch[:5], scratch[5:8]
    (
        total,
        got,
        out_got,
        joint_got,
        joint_sent,
        query_sum,
        query_grad,
        key_grad,
        value_grad,
        firsts_t,
        weight,
        tokens,
        middle_grad,
        parts,
        got_parts,
        got_far,
        specials,
        send_sems,
        recv_sems,
        load_sems,
        whole_sems,
    ) = scratch[8:]
    step = pl.program_id(0)
    count = len(chunks)
    columns = total.shape[4]
    rows, width = tokens.shape
    place = Place()
    sender = Sender(place, send_sems, recv_sems)
    sums = ChunkSums(place, sender, buffers, total, count)
    vector_sums = VectorSums(place, sender, vector_buffers, vector_total)
    own = buffers[0]
    passed = kept_in.shape[0]

    def own_loads(n):
        if n < passed:
            return [pltpu.make_async_copy(kept_in.at[n], own.at[n], load_sems.at[n, 0])]
        return [
            pltpu.make_async_copy(
                part_of(out_keep, "out", 0, columns, h), piece(own.at[n], h), load_sems.at[n, i]
            )
            for i, h in enumerate(halves_of(n))
        ]

    def whole_loads():
        pairs_of = ((weight_in, weight), (firsts_in, firsts_t), (tokens_in, tokens), (middle_grad_in, middle_grad))
        return [
            pltpu.make_async_copy(a, b, whole_sems.at[i]) for i, (a, b) in enumerate(pairs_of)
        ]

    early = [n for n, (name, _) in enumerate(chunks) if name != "joint"]
    out_chunk = early[-1]
    late = [n for n, (name, _) in enumerate(chunks) if name == "joint"]

    for n in range(passed):
        sender.add((n, 0), sent_in.at[n], got.at[n], "core")
    for h in halves_of(out_chunk):
        source = part_of(out_send, "out", 0, columns, h)
        sender.add((out_chunk, 0, h), source, piece(out_got, h), "core")
    for n in late:
        sender.add((n, 0), joint_sent.at[n - late[0]], joint_got.at[n - late[0]], "core")
    for index in range(2):
        sender.add(("first", index), parts.at[index], got_parts.at[index], "core")
    sender.add("far", parts.at[2], got_far, "x")
    for name in NEIGHBOURS:
        sender.add(("special", name), specials.at[place.band], specials.at[place.band], name)

    def begin():
        for n in early:
            for copy in own_loads(n):
                copy.start()
        place.greet(PLACES)
        for _, n, stage in PLAN:
            if stage == 0 and n < passed:
                sender.send((n, 0))
        for h in halves_of(out_chunk):
            sender.send((out_chunk, 0, h))

    def early_stage(n, stage):
        if stage == 0:
            for copy in own_loads(n):
                copy.wait()
            if n == out_chunk:
                for h in halves_of(n):
                    sender.arrived((n, 0, h))
                own[n] = own[n] + out_got[...]
            else:
                sender.arrived((n, 0))
                own[n] = own[n] + got[n]
        sums.step(n, stage)

    def late_stage(n, stage):
        if stage == 0:
            sender.arrived((n, 0))
            own[n] = own[n] + joint_got[n - late[0]]
        sums.step(n, stage)

    def stage_of(n, stage):
        (late_stage if n in late else early_stage)(n, stage)

    def exchanges(slot):
        for place_of, n, stage in PLAN:
            if place_of == slot:
                stage_of(n, stage)

    def occupied(slot):
        return any(place_of == slot for place_of, _, _ in PLAN)

    def joint_chunk(part):
        n = late[part]
        picked = joint_columns(firsts_t, *grads, own_pair_first(part, place.band))
        shape = (2, 2, 2, 2, width // CROPS // 2, columns)
        for value, target in zip(picked, (own.at[n], joint_sent.at[part])):
            value = value.reshape(shape)
            for h in halves_of(n):
                if h is None:
                    target[...] = value
                else:
                    target[h] = value[:, :, :, h]
        sender.send((n, 0))

    half_rows = 2 * rows
    per_step = len(key_parts(half_rows))

    def between(part):
        for index in range(2 * pairs):
            if occupied(index * per_step + part):

                @pl.when(step == index)
                def _():
                    exchanges(index * per_step + part)

    grads = (query_grad, key_grad, value_grad)
    last = 2 * pairs
    after = last * per_step

    @pl.when(step == 0)
    def _():
        begin()

    @pl.when(step == 1)
    def _():
        for copy in whole_loads():
            copy.start()

    @pl.when(step == pairs)
    def _():
        for copy in whole_loads():
            copy.wait()
        parts[1] = first_part(3, rows, *grads, weight).astype(BF16)
        sender.send(("first", 1))
        parts[2] = first_part(2, rows, *grads, weight).astype(BF16)

    @pl.when(step == pairs + 1)
    def _():
        sender.arrived(("first", 1))
        parts[2] = parts[2] + got_parts[1]
        sender.send("far")

    for part in range(2):

        @pl.when(step == pairs + 2 * part + 2)
        def _():
            joint_chunk(part)

    @pl.when(step < last)
    def _():
        far_half = step < pairs
        pair = jnp.where(far_half, step, jnp.minimum(step - pairs, pairs - 1))
        first_row = pl.multiple_of(jnp.where(far_half, half_rows, 0), half_rows)
        span = pl.ds(first_row, half_rows)
        outs = (key_grad.at[pair, span], value_grad.at[pair, span])
        inputs = (weights, queries, keys, values, attended, totals, attended_grad)
        part = attend_back_pair(*inputs, outs, between)

        @pl.when(far_half)
        def _():
            query_sum[pair] = part

        @pl.when(step >= pairs)
        def _():
            query_grad[pair] = (query_sum[pair] + part).astype(BF16)

    @pl.when(step == last)
    def _():
        joint_chunk(2)
        exchanges(after)
        parts[0] = first_part(1, rows, *grads, weight).astype(BF16)
        sender.send(("first", 0))
        exchanges(after + 1)
        first_grad = first_part(0, rows, *grads, weight)
        exchanges(after + 2)
        biases = bias_sums(info, slots, rows, query_grad, value_grad)
        sender.arrived(("first", 0))
        sender.arrived("far")
        first_grad = first_grad + got_parts[0].astype(F32) + got_far[...].astype(F32)
        exchanges(after + 3)
        patches, special_grad, rows_of = first_back(
            slots, info, first_grad, tokens, middle_grad, mask, gain
        )
        grad_patches[...] = patches
        specials[place.band] = jnp.concatenate([out_own[0:4], special_grad[0:4]], axis=0)
        for name in NEIGHBOURS:
            sender.send(("special", name))
        packed = jnp.concatenate([vectors[0:5]] + rows_of + [biases[0:2], down_bias[...]], axis=0)
        pack_vectors(vector_sums.own, packed, up_bias, width // CROPS)
        vector_sums.spread()
        for slot in range(after + 4, max(entry[0] for entry in PLAN) + 1):
            exchanges(slot)
            if slot == after + 7:
                vector_sums.share()
            if slot == after + 15:
                vector_sums.close()
        for name in NEIGHBOURS:
            sender.arrived(("special", name))
        specials_out[...] = specials[...]
        sender.finish()
        copy = pltpu.make_async_copy(total, total_out, whole_sems.at[4])
        copy.start()
        copy.wait()


def finish_kernel(
    chunks,
    special_count,
    total,
    vector_total,
    specials,
    up,
    down,
    out,
    joint,
    up_bias,
    out_specials,
    grad_specials,
    *vectors,
):
    _, _, _, rows, columns = total.shape
    refs = dict(up=up, down=down, out=out, joint=joint)
    for n, (name, part) in enumerate(chunks):
        for core in range(2):
            for x in range(2):
                row, column = x * rows, core * columns
                if name == "down":
                    row += 2 * rows * part
                else:
                    column += 2 * columns * part
                value = total[n, core, x].astype(F32)
                if name == "joint":
                    for third in range(3):
                        column = third * 2 * columns + (2 * part + core) * PAIR
                        piece_of = value[:, third * PAIR : (third + 1) * PAIR]
                        joint[row : row + rows, column : column + PAIR] = piece_of
                    continue
                refs[name][row : row + rows, column : column + columns] = value
    part = vectors[0].shape[0]
    for i, vector in enumerate(vectors):
        vector[...] = vector_total[i, 0:part]
    up_bias[...] = jnp.concatenate([vector_total[i : i + 1, 0:part] for i in range(11, 15)], axis=1)[0]
    for first, target in ((0, out_specials), (4, grad_specials)):
        picked = [
            specials[s % BANDS, first + s // BANDS : first + s // BANDS + 1]
            for s in range(special_count)
        ]
        target[0] = jnp.concatenate(picked, axis=0).astype(BF16)


def backward_fused(given, slots, special_count):
    g = given
    rows, width = g["tokens"].shape
    hidden_width = g["up_bias_grad"].shape[1]
    every = BANDS * rows
    pairs = width // PAIR
    chunks = chunk_list(hidden_width // width)
    count = len(chunks)
    part = width // CROPS
    unit_rows, columns = part // 2, width // 2
    unit = (2, 2, 2, 2, unit_rows, columns)
    hidden_parts = hidden_width // width
    shaped = jax.ShapeDtypeStruct
    last = 2 * pairs - 1
    far_first = lambda i: 1 - jnp.minimum(i, last) // pairs
    pair_of = lambda i: jnp.minimum(i, last) % pairs
    own_pair = pl.BlockSpec((rows, PAIR), lambda i: (0, pair_of(i)))
    own_heads = pl.BlockSpec((1, rows, PAIR), lambda i: (pair_of(i), 0, 0))
    half_heads = pl.BlockSpec((1, 2 * rows, PAIR), lambda i: (pair_of(i), far_first(i), 0))
    kept = pl.BlockSpec((1, 2 * rows, 2 * rows), lambda i: (pair_of(i), 0, far_first(i)))
    grad_patches, total, vector_total, specials = pl.pallas_call(
        partial(backward_kernel, chunks, slots, pairs),
        grid=(2 * pairs + 1,),
        out_shape=[
            shaped((slots, width), BF16),
            shaped((count, 2, 2, unit_rows, columns), BF16),
            shaped((16, 128), F32),
            shaped((BANDS, 8, width), F32),
        ],
        in_specs=[SMEM, kept, own_heads, half_heads, half_heads, own_pair, own_pair, own_pair]
        + [VMEM] * 6
        + [ANY] * 8,
        out_specs=[VMEM, ANY, VMEM, VMEM],
        scratch_shapes=chunk_scratch(count, unit_rows, columns)
        + vector_scratch()
        + [
            pltpu.VMEM((count, 2, 2, unit_rows, columns), BF16),
            pltpu.VMEM((2 * hidden_parts,) + unit, BF16),
            pltpu.VMEM(unit, BF16),
            pltpu.VMEM((3,) + unit, BF16),
            pltpu.VMEM((3,) + unit, BF16),
            pltpu.VMEM((pairs, rows, PAIR), F32),
            pltpu.VMEM((pairs, rows, PAIR), BF16),
            pltpu.VMEM((pairs, every, PAIR), BF16),
            pltpu.VMEM((pairs, every, PAIR), BF16),
            pltpu.VMEM((width, every), BF16),
            pltpu.VMEM((width, 3 * width), BF16),
            pltpu.VMEM((rows, width), F32),
            pltpu.VMEM((rows, width), F32),
            pltpu.VMEM((3, rows, width), BF16),
            pltpu.VMEM((2, rows, width), BF16),
            pltpu.VMEM((rows, width), BF16),
            pltpu.VMEM((BANDS, 8, width), F32),
            pltpu.SemaphoreType.DMA((10 * count,)),
            pltpu.SemaphoreType.DMA((10 * count,)),
            pltpu.SemaphoreType.DMA((count, 2)),
            pltpu.SemaphoreType.DMA((5,)),
        ],
        compiler_params=pltpu.CompilerParams(
            vmem_limit_bytes=VMEM_LIMIT, collective_id=0, has_side_effects=True
        ),
        name="backward",
    )(
        g["info"],
        g["weights"],
        g["queries"],
        g["keys"],
        g["values"],
        g["attended"],
        g["totals"],
        g["attended_grad"],
        g["mask"],
        g["first_gain"],
        g["vectors"],
        g["down_bias_grad"],
        g["up_bias_grad"],
        g["out_own"],
        *g["mlp_grads"],
        g["out_keep"].reshape(unit),
        g["out_send"].reshape(unit),
        g["firsts_t"],
        g["joint_weight"],
        g["tokens"],
        g["middle_grad"],
    )
    special = shaped((1, special_count, width), BF16)
    results = pl.pallas_call(
        partial(finish_kernel, chunks, special_count),
        out_shape=[
            shaped((part, hidden_width), F32),
            shaped((hidden_width // CROPS, width), F32),
            shaped((part, width), F32),
            shaped((part, 3 * width), F32),
            shaped((hidden_width // CROPS,), F32),
            special,
            special,
        ]
        + [shaped((part,), F32)] * 11,
        in_specs=[VMEM] * 3,
        out_specs=[VMEM] * 18,
        compiler_params=params(),
        name="finish",
    )(total, vector_total, specials)
    up, down, out, joint, up_bias, out_specials, grad_specials = results[:7]
    return grad_patches, up, down, out, joint, results[7:], up_bias, out_specials, grad_specials


def forward_fused(
    info, mask, patches, specials, token, gain, shift, weight, query_bias, value_bias, rows
):
    slots, width = patches.shape
    every, pairs = BANDS * rows, width // PAIR
    shaped = jax.ShapeDtypeStruct
    half_of = lambda i: i // pairs
    pair_of = lambda i: i % pairs
    final_pair = pl.BlockSpec((rows, PAIR), lambda i: (0, jnp.maximum(i - pairs, 0)))
    outs = pl.pallas_call(
        partial(forward_kernel, slots, pairs),
        grid=(2 * pairs,),
        out_shape=[
            shaped((rows, width), F32),
            shaped((pairs, rows, PAIR), BF16),
            shaped((pairs, every, PAIR), BF16),
            shaped((pairs, every, PAIR), BF16),
            shaped((rows, width), F32),
            shaped((rows, width), F32),
            shaped((pairs, 2 * rows, every), BF16),
            shaped((width, every), BF16),
        ],
        in_specs=[SMEM] + [VMEM] * 8 + [ANY],
        out_specs=[
            ANY,
            ANY,
            ANY,
            ANY,
            final_pair,
            final_pair,
            pl.BlockSpec((1, 2 * rows, 2 * rows), lambda i: (pair_of(i), 0, half_of(i))),
            pl.BlockSpec((PAIR, 2 * rows), lambda i: (pair_of(i), half_of(i))),
        ],
        scratch_shapes=[
            pltpu.VMEM((rows, width), F32),
            pltpu.VMEM((BANDS, rows, width), BF16),
            pltpu.VMEM((pairs, rows, PAIR), BF16),
            pltpu.VMEM((pairs, every, PAIR), BF16),
            pltpu.VMEM((pairs, every, PAIR), BF16),
            pltpu.VMEM((every, PAIR), BF16),
            pltpu.VMEM((pairs, rows, PAIR), F32),
            pltpu.VMEM((pairs, rows, PAIR), F32),
            pltpu.VMEM((width, 3 * width), BF16),
            pltpu.SemaphoreType.DMA((3,)),
            pltpu.SemaphoreType.DMA((3,)),
            pltpu.SemaphoreType.DMA((5,)),
        ],
        compiler_params=pltpu.CompilerParams(
            vmem_limit_bytes=VMEM_LIMIT, collective_id=1, has_side_effects=True
        ),
        name="forward",
    )(info, mask, patches, specials, token, gain, shift, query_bias, value_bias, weight)
    return outs


def forward_general(
    info, mask, patches, specials, token, gain, shift, weight, query_bias, value_bias, rows
):
    slots, width = patches.shape
    every, pairs = BANDS * rows, width // PAIR
    shaped = jax.ShapeDtypeStruct
    tokens, first = pl.pallas_call(
        partial(first_kernel, slots),
        out_shape=[shaped((rows, width), F32), shaped((rows, width), BF16)],
        in_specs=[SMEM] + [VMEM] * 6,
        compiler_params=params(),
        name="first",
    )(info, mask, patches, specials, token, gain, shift)
    firsts = gather_blocks(first)
    block = pl.BlockSpec((rows, width), lambda i: (i, 0))
    pair_block = pl.BlockSpec((pairs, rows, PAIR), lambda i: (0, i, 0))
    queries, keys, values = pl.pallas_call(
        partial(project_kernel, slots),
        grid=(BANDS,),
        out_shape=[
            shaped((pairs, rows, PAIR), BF16),
            shaped((pairs, every, PAIR), BF16),
            shaped((pairs, every, PAIR), BF16),
        ],
        in_specs=[SMEM, block, whole((width, 3 * width)), VMEM, VMEM],
        out_specs=[whole((pairs, rows, PAIR)), pair_block, pair_block],
        compiler_params=params(),
        name="project",
    )(info, firsts, weight, query_bias, value_bias)
    own_pair = pl.BlockSpec((rows, PAIR), lambda i: (0, i))
    all_pair = pl.BlockSpec((every, PAIR), lambda i: (0, i))
    own_heads = pl.BlockSpec((1, rows, PAIR), lambda i: (i, 0, 0))
    all_heads = pl.BlockSpec((1, every, PAIR), lambda i: (i, 0, 0))
    attended, totals, weights, firsts_t = pl.pallas_call(
        partial(attend_kernel, slots),
        grid=(pairs,),
        out_shape=[
            shaped((rows, width), F32),
            shaped((rows, width), F32),
            shaped((pairs, 2 * rows, every), BF16),
            shaped((width, every), BF16),
        ],
        in_specs=[SMEM, own_heads, all_heads, all_heads, all_pair],
        out_specs=[
            own_pair,
            own_pair,
            pl.BlockSpec((1, 2 * rows, every), lambda i: (i, 0, 0)),
            pl.BlockSpec((PAIR, every), lambda i: (i, 0)),
        ],
        compiler_params=params(),
        name="attend",
    )(info, queries, keys, values, firsts)
    return tokens, queries, keys, values, attended, totals, weights, firsts_t


def middle_general(
    info,
    attended,
    tokens,
    out_weight,
    out_bias,
    first_scale,
    second_gain,
    second_shift,
    second_scale,
    cot_patches,
    cot_specials,
    down_bias,
    up_weight,
    up_bias,
    down_weight,
):
    rows, width = tokens.shape
    slots = cot_patches.shape[0]
    hidden_width = up_weight.shape[1]
    pad = rows - slots
    shaped = jax.ShapeDtypeStruct
    branch, middle, second, incoming, down_in, down_keep, down_send, down_bias_grad = pl.pallas_call(
        partial(middle_kernel, slots),
        out_shape=[
            shaped((rows, width), F32),
            shaped((rows, width), F32),
            shaped((rows, width), BF16),
            shaped((rows, width), F32),
            shaped((rows, width), BF16),
            shaped((rows, width // 2), BF16),
            shaped((rows, width // 2), BF16),
            shaped((1, width), F32),
        ],
        in_specs=[SMEM] + [VMEM] * 10,
        out_specs=[VMEM] * 8,
        compiler_params=params(),
        name="middle",
    )(
        info,
        attended,
        tokens,
        out_weight,
        out_bias,
        first_scale,
        second_gain,
        second_shift,
        second_scale,
        cot_patches,
        cot_specials,
    )

    steps = hidden_width // width
    half = width // 2
    (
        branch_two,
        second_grad,
        up_keep,
        up_send,
        up_bias_grad,
        down_grad_keep,
        down_grad_send,
    ) = pl.pallas_call(
        mlp_kernel,
        grid=(steps,),
        out_shape=[
            shaped((rows, width), F32),
            shaped((rows, width), F32),
            shaped((width, hidden_width // 2), BF16),
            shaped((width, hidden_width // 2), BF16),
            shaped((1, hidden_width), F32),
            shaped((hidden_width, half), BF16),
            shaped((hidden_width, half), BF16),
        ],
        in_specs=[
            SMEM,
            whole((rows, width)),
            whole((rows, width)),
            whole((rows, half)),
            whole((rows, half)),
            pl.BlockSpec((width, width), lambda i: (0, i)),
            pl.BlockSpec((1, width), lambda i: (0, i)),
            pl.BlockSpec((width, width), lambda i: (i, 0)),
        ],
        out_specs=[
            whole((rows, width)),
            whole((rows, width)),
            pl.BlockSpec((width, half), lambda i: (0, i)),
            pl.BlockSpec((width, half), lambda i: (0, i)),
            pl.BlockSpec((1, width), lambda i: (0, i)),
            pl.BlockSpec((width, half), lambda i: (i, 0)),
            pl.BlockSpec((width, half), lambda i: (i, 0)),
        ],
        compiler_params=params(),
        name="mlp",
    )(info, second, down_in, down_keep, down_send, up_weight, up_bias, down_weight)
    up_got = swap(up_send, "band", 1)
    down_got = swap(down_grad_send, "band", 1)

    out_patches, out_own, middle_grad, attended_grad, out_keep, out_send, vectors = pl.pallas_call(
        partial(middle_back_kernel, slots),
        out_shape=[
            shaped((slots, width), BF16),
            shaped((pad, width), F32),
            shaped((rows, width), F32),
            shaped((rows, width), F32),
            shaped((width, half), BF16),
            shaped((width, half), BF16),
            shaped((8, width), F32),
        ],
        in_specs=[SMEM] + [VMEM] * 11,
        out_specs=[VMEM] * 7,
        compiler_params=params(),
        name="middle_back",
    )(
        info,
        middle,
        branch,
        branch_two,
        second_grad,
        incoming,
        attended,
        out_weight,
        down_bias,
        second_scale,
        second_gain,
        first_scale,
    )

    shared = (out_patches, out_own, middle_grad, attended_grad, out_keep, out_send, vectors)
    halves = dict(up_keep=up_keep, up_got=up_got, down_keep=down_grad_keep, down_got=down_got)
    return shared + (down_bias_grad, up_bias_grad, halves)


def body(
    patches,
    specials,
    patch_mask,
    band_rows,
    mask_token,
    first_gain,
    first_shift,
    joint_weight,
    query_bias,
    value_bias,
    out_weight,
    out_bias,
    first_scale,
    second_gain,
    second_shift,
    up_weight,
    up_bias,
    down_weight,
    down_bias,
    second_scale,
    cot_patches,
    cot_specials,
):
    slots, width = patches.shape[1:]
    special_count = specials.shape[1]
    hidden_width = up_weight.shape[1]
    owned = -(-special_count // BANDS)
    rows = round_up(slots + owned, 16)
    pad = rows - slots
    band = lax.axis_index("band")
    relatives = [band ^ r for r in range(BANDS)]
    info = jnp.stack(
        [band_rows[b] * GRID for b in relatives]
        + [(special_count - b + BANDS - 1) // BANDS for b in relatives]
        + [band]
    ).astype(jnp.int32)
    mask = patch_mask
    patches, specials = patches[0], specials[0]
    cot_patches, cot_specials = cot_patches[0], cot_specials[0]
    shaped = jax.ShapeDtypeStruct

    forward = forward_fused if lax.axis_size("crop") == CROPS else forward_general
    tokens, queries, keys, values, attended, totals, weights, firsts_t = forward(
        info,
        mask,
        patches,
        specials,
        mask_token,
        first_gain,
        first_shift,
        joint_weight,
        query_bias,
        value_bias,
        rows,
    )

    middle = middle_fused if lax.axis_size("crop") == CROPS else middle_general
    (
        out_patches,
        out_own,
        middle_grad,
        attended_grad,
        out_keep,
        out_send,
        vectors,
        down_bias_grad,
        up_bias_grad,
        mlp_grads,
    ) = middle(
        info,
        attended,
        tokens,
        out_weight,
        out_bias,
        first_scale,
        second_gain,
        second_shift,
        second_scale,
        cot_patches,
        cot_specials,
        down_bias,
        up_weight,
        up_bias.reshape(1, -1),
        down_weight,
    )
    given = dict(
        info=info,
        weights=weights,
        queries=queries,
        keys=keys,
        values=values,
        attended=attended,
        totals=totals,
        attended_grad=attended_grad,
        mask=mask,
        first_gain=first_gain,
        vectors=vectors,
        down_bias_grad=down_bias_grad,
        up_bias_grad=up_bias_grad,
        out_own=out_own,
        mlp_grads=mlp_grads,
        out_keep=out_keep,
        out_send=out_send,
        firsts_t=firsts_t,
        joint_weight=joint_weight,
        tokens=tokens,
        middle_grad=middle_grad,
    )
    backward = backward_fused if lax.axis_size("crop") == CROPS else backward_general
    (
        grad_patches,
        up,
        down,
        out,
        joint,
        rows_of,
        up_bias_sum,
        out_specials,
        grad_specials,
    ) = backward(given, slots, special_count)
    return (
        out_patches[None],
        out_specials,
        grad_patches[None],
        grad_specials,
        rows_of[5],
        rows_of[6],
        rows_of[7],
        joint,
        rows_of[8],
        rows_of[9],
        out,
        rows_of[4],
        rows_of[3],
        rows_of[1],
        rows_of[2],
        up,
        up_bias_sum,
        down,
        rows_of[10],
        rows_of[0],
    )


def solution(mesh):
    split = P("crop", "band", None)
    special = P("crop", None, None)
    in_specs = (
        (split, special, P("crop", "band")) + (P(),) * 17 + (split, special)
    )
    line, matrix = P("crop"), P("crop", None)
    out_specs = (
        split,
        special,
        split,
        special,
        line,
        line,
        line,
        matrix,
        line,
        line,
        matrix,
        line,
        line,
        line,
        line,
        matrix,
        line,
        matrix,
        line,
        line,
    )
    return jax.shard_map(body, mesh=mesh, in_specs=in_specs, out_specs=out_specs, check_vma=False)
```

```python
from functools import partial

import jax
import jax.numpy as jnp
from jax import lax
from jax.experimental import pallas as pl
from jax.experimental.pallas import tpu as pltpu
from jax.sharding import PartitionSpec as P

HEAD = 64
GRID = 37
PAIR = 2 * HEAD
BANDS = 4
SPECIALS = 5
ROW_PART = 64
KEY_PART = 256
F32 = jnp.float32
BF16 = jnp.bfloat16
VMEM_LIMIT = 60 << 20


def round_up(value, unit):
    return (value + unit - 1) // unit * unit


def params(semantics=None):
    return pltpu.CompilerParams(vmem_limit_bytes=VMEM_LIMIT)


def dot(a, b):
    return jnp.dot(a, b, preferred_element_type=F32)


def dot_nt(a, b):
    return lax.dot_general(a, b, (((1,), (1,)), ((), ())), preferred_element_type=F32)


def dot_tn(a, b):
    return lax.dot_general(a, b, (((0,), (0,)), ((), ())), preferred_element_type=F32)


def normalize(rows):
    centred = rows - jnp.mean(rows, axis=-1, keepdims=True)
    spread = jnp.mean(centred * centred, axis=-1, keepdims=True)
    scale = lax.rsqrt(spread + 1e-06)
    return centred * scale, scale


def normalize_back(grad, hat, scale):
    return scale * (
        grad
        - jnp.mean(grad, axis=-1, keepdims=True)
        - hat * jnp.mean(grad * hat, axis=-1, keepdims=True)
    )


def column_sum(rows):
    return jnp.sum(rows, axis=0, keepdims=True)


def line(ref):
    return ref[...].reshape(1, -1)


def whole(shape):
    return pl.BlockSpec(shape, lambda *_: (0,) * len(shape))


VMEM = pl.BlockSpec(memory_space=pltpu.VMEM)
ANY = pl.BlockSpec(memory_space=pl.ANY)
SMEM = pl.BlockSpec(memory_space=pltpu.SMEM)


def own_special(specials, band, slot):
    row = jnp.zeros((1, specials.shape[1]), F32)
    for special in range(specials.shape[0]):
        if special // BANDS == slot:
            row = row + jnp.where(band == special % BANDS, specials[special : special + 1], 0.0)
    return row


def place_rows(ref, patch_rows, specials, band):
    slots = patch_rows.shape[0]
    rows = ref.shape[0]
    ref[0:slots, :] = patch_rows
    extra = [own_special(specials, band, slot) for slot in range(rows - slots)]
    ref[slots:rows, :] = jnp.concatenate(extra, axis=0)


def block_counts(band_rows, relative):
    band = lax.axis_index("band")
    core, x = lax.rem(band, 2), lax.div(band, 2)
    core = core + lax.rem(relative, 2) * (1 - 2 * core)
    x = x + lax.div(relative, 2) * (1 - 2 * x)
    owner = 2 * x + core
    return band_rows[owner] * GRID, lax.div(SPECIALS - owner + BANDS - 1, BANDS)


def counted_rows(band_rows, relative, rows, slots, width):
    used, specials = block_counts(band_rows, relative)
    index = lax.broadcasted_iota(jnp.int32, (rows, width), 0)
    return (index < used) | ((index >= slots) & (index < slots + specials))


def stack_pair(rows):
    lane = lax.broadcasted_iota(jnp.int32, rows.shape, 1)
    zero = jnp.zeros_like(rows)
    return jnp.concatenate(
        [jnp.where(lane < HEAD, rows, zero), jnp.where(lane >= HEAD, rows, zero)], axis=0
    )


def unstack_pair(rows):
    half = rows.shape[0] // 2
    lane = lax.broadcasted_iota(jnp.int32, (half, rows.shape[1]), 1)
    return jnp.where(lane < HEAD, rows[:half], rows[half:])


def mask_column(mask):
    return jnp.broadcast_to(mask[...].astype(F32), (8, mask.shape[1])).T[:, :1] > 0


def first_kernel(slots, info, mask, patches, specials, token, gain, shift, tokens, first):
    band = lax.axis_index("band")
    filled = jnp.where(mask_column(mask), line(token), patches[...].astype(F32))
    place_rows(tokens, filled, specials[...].astype(F32), band)
    hat, _ = normalize(tokens[...])
    counted = counted_rows(info, 0, tokens.shape[0], slots, tokens.shape[1])
    first[...] = jnp.where(counted, hat * line(gain) + line(shift), 0.0).astype(BF16)


def split_pairs(ref, rows, value):
    for pair in range(ref.shape[0]):
        ref[pair, rows, :] = value[:, pair * PAIR : (pair + 1) * PAIR].astype(BF16)


def project_keys(low, weight, value_bias, counted, keys, values, rows):
    width = weight.shape[0]
    split_pairs(keys, rows, dot(low, weight[:, width : 2 * width]))
    value = dot(low, weight[:, 2 * width :]) + line(value_bias)
    split_pairs(values, rows, jnp.where(counted, value, 0.0))


def attend_pair(queries, keys, values, ones):
    factor = HEAD ** (-0.5)
    stacked = stack_pair((queries.astype(F32) * factor).astype(BF16))
    low = jnp.exp(dot_nt(stacked, keys)).astype(BF16)
    summed = dot(low, jnp.concatenate([values, ones], axis=1))
    return low, unstack_pair(summed[:, :PAIR]), unstack_pair(summed[:, PAIR:])


def project_kernel(slots, info, first, weight, query_bias, value_bias, queries, keys, values):
    relative = pl.program_id(0)
    rows, width = first.shape
    counted = counted_rows(info, relative, rows, slots, width)
    low = first[...]

    @pl.when(relative == 0)
    def _():
        split_pairs(queries, slice(None), dot(low, weight[:, :width]) + line(query_bias))

    project_keys(low, weight, value_bias, counted, keys, values, slice(None))


def attend_kernel(
    slots, info, queries, keys, values, firsts, attended, totals, weights, firsts_t
):
    rows = queries.shape[1]
    ones = [
        counted_rows(info, r, rows, slots, PAIR).astype(F32).astype(BF16) for r in range(BANDS)
    ]
    low, summed, total = attend_pair(
        queries[0], keys[0], values[0], jnp.concatenate(ones, axis=0)
    )
    weights[0] = low
    firsts_t[...] = firsts[...].astype(F32).T.astype(BF16)
    attended[...] = summed / total
    totals[...] = total


def forward_kernel(
    slots,
    pairs,
    info,
    mask,
    patches,
    specials,
    token,
    gain,
    shift,
    query_bias,
    value_bias,
    weight_in,
    tokens_out,
    queries_out,
    keys_out,
    values_out,
    attended,
    totals,
    weights,
    firsts_t,
    tokens,
    firsts,
    queries,
    keys,
    values,
    ones,
    sums,
    counts,
    weight,
    send_sems,
    recv_sems,
    sems,
):
    step = pl.program_id(0)
    rows, width = tokens.shape
    half_rows = 2 * rows
    place = Place()
    sender = Sender(place, send_sems, recv_sems)
    sender.add("near", firsts.at[0], firsts.at[1], "core")
    sender.add("far", firsts.at[0], firsts.at[2], "x")
    sender.add("diagonal", firsts.at[2], firsts.at[3], "core")
    weight_load = lambda: pltpu.make_async_copy(weight_in, weight, sems.at[0])
    stores = lambda: [
        pltpu.make_async_copy(a, b, sems.at[i])
        for i, (a, b) in enumerate(
            ((tokens, tokens_out), (queries, queries_out), (keys, keys_out), (values, values_out)), 1
        )
    ]

    def block_keys(block):
        counted = counted_rows(info, block, rows, slots, width)
        span = pl.ds(block * rows, rows)
        project_keys(firsts[block], weight, value_bias, counted, keys, values, span)

    @pl.when(step == 0)
    def _():
        weight_load().start()
        filled = jnp.where(mask_column(mask), line(token), patches[...].astype(F32))
        place_rows(tokens, filled, specials[...].astype(F32), place.band)
        hat, _ = normalize(tokens[...])
        counted = counted_rows(info, 0, rows, slots, width)
        firsts[0] = jnp.where(counted, hat * line(gain) + line(shift), 0.0).astype(BF16)
        place.greet(("core", "x"))
        sender.send("near")
        sender.send("far")
        for block in range(BANDS):
            used = counted_rows(info, block, rows, slots, PAIR)
            ones[block * rows : (block + 1) * rows, :] = used.astype(F32).astype(BF16)
        weight_load().wait()
        split_pairs(queries, slice(None), dot(firsts[0], weight[:, :width]) + line(query_bias))
        block_keys(0)
        sender.arrived("near")
        block_keys(1)

    @pl.when(step == pairs)
    def _():
        sender.arrived("far")
        sender.send("diagonal")
        block_keys(2)
        sender.arrived("diagonal")
        block_keys(3)
        for copy in stores():
            copy.start()

    far_half = step >= pairs
    pair = jnp.where(far_half, step - pairs, step)
    first_row = pl.multiple_of(jnp.where(far_half, half_rows, 0), half_rows)
    span = pl.ds(first_row, half_rows)
    low, summed, total = attend_pair(
        queries[pair], keys[pair, span], values[pair, span], ones[span, :]
    )
    weights[0] = low
    first_block = jnp.where(far_half, 2, 0)
    lane = pl.ds(pl.multiple_of(pair * PAIR, PAIR), PAIR)
    columns = [firsts[first_block + i, :, lane] for i in range(2)]
    firsts_t[...] = jnp.concatenate(columns, axis=0).astype(F32).T.astype(BF16)

    @pl.when(step < pairs)
    def _():
        sums[pair] = summed
        counts[pair] = total

    @pl.when(far_half)
    def _():
        whole_total = counts[pair] + total
        attended[...] = (sums[pair] + summed) / whole_total
        totals[...] = whole_total

    @pl.when(step == 2 * pairs - 1)
    def _():
        sender.finish()
        for copy in stores():
            copy.wait()


def middle_kernel(
    slots,
    info,
    attended,
    tokens,
    weight,
    bias,
    first_scale,
    gain,
    shift,
    second_scale,
    cot_patches,
    cot_specials,
    branch,
    middle,
    second,
    incoming,
    down_in,
    down_keep,
    down_send,
    down_bias_grad,
):
    rows = tokens.shape[0]
    band = lax.axis_index("band")
    side = dot(attended[...].astype(BF16), weight[...]) + line(bias)
    branch[...] = side
    mid = tokens[...] + line(first_scale) * side
    middle[...] = mid
    hat, _ = normalize(mid)
    second[...] = (hat * line(gain) + line(shift)).astype(BF16)
    counted = counted_rows(info, 0, slots, slots, tokens.shape[1])
    given = jnp.where(counted, cot_patches[...].astype(F32), 0.0)
    place_rows(incoming, given, cot_specials[...].astype(F32), band)
    low = (incoming[...] * line(second_scale)).astype(BF16)
    down_in[...] = low
    keep, send = own_half(low, band)
    down_keep[...] = keep
    down_send[...] = send
    down_bias_grad[...] = column_sum(low.astype(F32))


def own_half(rows, band):
    half = rows.shape[1] // 2
    first = lax.rem(band, 2) == 0
    low, high = rows[:, :half], rows[:, half:]
    return jnp.where(first, low, high), jnp.where(first, high, low)


def gelu_and_slope(x):
    phi = 0.5 + 0.5 * lax.erf(x * 0.7071067811865476)
    density = jnp.exp(-0.5 * x * x) * 0.3989422804014327
    return x * phi, phi + x * density


def mlp_kernel(
    info,
    second,
    down_in,
    down_keep,
    down_send,
    up,
    up_bias,
    down,
    branch_two,
    second_grad,
    up_grad_keep,
    up_grad_send,
    up_bias_grad,
    down_grad_keep,
    down_grad_send,
):
    step = pl.program_id(0)
    low = second[...]
    hidden = dot(low, up[...]) + up_bias[...]
    active, slope = gelu_and_slope(hidden)
    active = active.astype(BF16)
    hidden_in = (slope * dot_nt(down_in[...], down[...])).astype(BF16)

    @pl.when(step == 0)
    def _():
        branch_two[...] = jnp.zeros_like(branch_two)
        second_grad[...] = jnp.zeros_like(second_grad)

    branch_two[...] += dot(active, down[...])
    second_grad[...] += dot_nt(hidden_in, up[...])
    keep, send = own_half(hidden_in, lax.axis_index("band"))
    up_grad_send[...] = dot_tn(low, send).astype(BF16)
    up_grad_keep[...] = dot_tn(low, keep).astype(BF16)
    down_grad_send[...] = dot_tn(active, down_send[...]).astype(BF16)
    down_grad_keep[...] = dot_tn(active, down_keep[...]).astype(BF16)
    up_bias_grad[...] = column_sum(hidden_in.astype(F32))


def middle_back_kernel(
    slots,
    info,
    middle,
    branch,
    branch_two,
    second_grad,
    incoming,
    attended,
    weight,
    down_bias,
    second_scale,
    gain,
    first_scale,
    out_patches,
    out_specials,
    middle_grad,
    attended_grad,
    out_keep,
    out_send,
    vectors,
    between=lambda part: None,
):
    mid = middle[...]
    given = incoming[...]
    two = branch_two[...] + line(down_bias)
    output = mid + line(second_scale) * two
    counted = counted_rows(info, 0, slots, slots, mid.shape[1])
    out_patches[...] = jnp.where(counted, output[:slots], 0.0).astype(BF16)
    out_specials[...] = output[slots:]
    hat, scale = normalize(mid)
    grad = second_grad[...]
    back = given + normalize_back(grad * line(gain), hat, scale)
    middle_grad[...] = back
    between(0)
    out_in = (back * line(first_scale)).astype(BF16)
    attended_grad[...] = dot_nt(out_in, weight[...])
    between(1)
    keep, send = own_half(out_in, lax.axis_index("band"))
    low = attended[...].astype(BF16)
    out_keep[...] = dot_tn(low, keep).astype(BF16)
    out_send[...] = dot_tn(low, send).astype(BF16)
    between(2)
    vectors[...] = jnp.concatenate(
        [
            column_sum(given * two),
            column_sum(grad * hat),
            column_sum(grad),
            column_sum(back * branch[...]),
            column_sum(out_in.astype(F32)),
            jnp.zeros((3, mid.shape[1]), F32),
        ],
        axis=0,
    )


def attend_back_pair(weights, queries, keys, values, attended, totals, attended_grad, outs):
    key_grad, value_grad = outs
    queries, keys, values = queries.at[0], keys.at[0], values.at[0]
    rows = queries.shape[0]
    factor = HEAD ** (-0.5)
    stacked = stack_pair((queries[...].astype(F32) * factor).astype(BF16))
    scaled = attended_grad[...] / totals[...]
    returned = stack_pair(scaled.astype(BF16))
    slope = jnp.sum(stack_pair(scaled * attended[...]), axis=1, keepdims=True)
    stacked_t = stacked.astype(F32).T.astype(BF16)
    returned_t = returned.astype(F32).T.astype(BF16)
    total = jnp.zeros((2 * rows, PAIR), F32)
    start = 0
    for size in key_parts(keys.shape[0]):
        span = slice(start, start + size)
        start += size
        low = weights[0, :, span]
        moved = dot_nt(returned, values[span, :])
        scores = (low.astype(F32) * (moved - slope)).astype(BF16)
        total = total + dot(scores, keys[span, :])
        key_grad[span, :] = dot(stacked_t, scores).T.astype(BF16)
        value_grad[span, :] = dot(returned_t, low).T.astype(BF16)
    return unstack_pair(total) * factor


def key_parts(count):
    parts = [KEY_PART] * (count // KEY_PART)
    if count % KEY_PART:
        parts[-1] += count % KEY_PART
    return parts


def first_part(block, rows, query_grad, key_grad, value_grad, weight):
    width = weight.shape[0]
    span = slice(block * rows, (block + 1) * rows)
    part = jnp.zeros((rows, width), F32)
    for pair in range(0, width // PAIR, 2):
        for offset, grad in ((width, key_grad), (2 * width, value_grad), (0, query_grad)):
            if offset == 0 and block > 0:
                continue
            at = slice(0, rows) if offset == 0 else span
            low = jnp.concatenate([grad[pair, at, :], grad[pair + 1, at, :]], axis=1)
            columns = slice(offset + pair * PAIR, offset + (pair + 2) * PAIR)
            part = part + dot_nt(low, weight[:, columns])
    return part


def own_pair_first(part, band):
    core = lax.rem(band, 2)
    return 2 * part + core, 2 * part + 1 - core


def joint_columns(firsts_t, query_grad, key_grad, value_grad, pairs):
    rows = query_grad.shape[1]
    queries = dot(firsts_t[:, :rows], jnp.concatenate([query_grad[p] for p in pairs], axis=1))
    results = []
    for index, p in enumerate(pairs):
        others = dot(firsts_t[...], jnp.concatenate([key_grad[p], value_grad[p]], axis=1))
        own = queries[:, index * PAIR : (index + 1) * PAIR]
        results.append(jnp.concatenate([own, others], axis=1).astype(BF16))
    return results


def first_back(slots, info, grad, tokens, middle_grad, mask, gain, patches, between=lambda part: None):
    rows, width = tokens.shape
    masked = mask_column(mask)
    counted = counted_rows(info, 0, rows, slots, width)
    sums = None
    for part, start in enumerate(range(0, rows, ROW_PART)):
        at = slice(start, start + ROW_PART)
        some = jnp.where(counted[at], grad[at], 0.0)
        hat, scale = normalize(tokens[at, :])
        token_grad = middle_grad[at, :] + normalize_back(some * line(gain), hat, scale)
        end = min(start + ROW_PART, slots)
        hidden = masked[start:end]
        patch_grad = token_grad[: end - start]
        patches[start:end, :] = jnp.where(hidden, 0.0, patch_grad).astype(BF16)
        terms = [
            column_sum(jnp.where(hidden, patch_grad, 0.0)),
            column_sum(some * hat),
            column_sum(some),
        ]
        sums = terms if sums is None else [x + y for x, y in zip(sums, terms)]
        between(part)
    return token_grad[slots - start :], sums


def bias_sums(info, slots, rows, query_grad, value_grad):
    ones = [
        counted_rows(info, block, rows, slots, PAIR).astype(F32).astype(BF16)
        for block in range(BANDS)
    ]
    ones = jnp.concatenate(ones, axis=0)
    pairs = range(query_grad.shape[0])
    queries = [column_sum(query_grad[pair].astype(F32)) for pair in pairs]
    values = [dot_tn(ones, value_grad[pair])[0:1] for pair in pairs]
    both = [jnp.concatenate(queries, axis=1), jnp.concatenate(values, axis=1)]
    return jnp.concatenate(both + [jnp.zeros((6, both[0].shape[1]), F32)], axis=0)


def swap(x, axis, distance):
    size = lax.axis_size(axis)
    return lax.ppermute(x, axis, [(i, i ^ distance) for i in range(size)])


def halve(x, axis, distance):
    bit = (lax.axis_index(axis) // distance) % 2
    sent = lax.dynamic_index_in_dim(x, 1 - bit, 0, keepdims=False)
    kept = lax.dynamic_index_in_dim(x, bit, 0, keepdims=False)
    got = swap(sent, axis, distance)
    return (kept.astype(F32) + got.astype(F32)).astype(BF16)


def reduce_half(kept, got, columns):
    held = (kept.astype(F32) + got.astype(F32)).astype(BF16)
    rows, half = held.shape
    crops = lax.axis_size("crop")
    held = held.reshape((crops, rows // crops, half))
    distance = 1
    while distance < crops:
        count = held.shape[0]
        held = jnp.moveaxis(held.reshape((count // 2, 2) + held.shape[1:]), 1, 0)
        held = halve(held, "crop", distance)
        distance *= 2
    held = held.reshape((rows // crops, half))
    other = swap(held, "band", 2)
    full = (held.astype(F32) + other.astype(F32)).astype(BF16)
    mate = swap(full, "band", 1)
    bit = lax.axis_index("band") % 2
    low = jnp.where(bit == 0, full, mate).astype(F32).reshape(rows // crops, -1, columns)
    high = jnp.where(bit == 0, mate, full).astype(F32).reshape(rows // crops, -1, columns)
    return jnp.stack([low, high], axis=2).reshape(rows // crops, 2 * half)


def gather_blocks(x):
    near = swap(x, "band", 1)
    far = swap(x, "band", 2)
    diagonal = swap(far, "band", 1)
    return jnp.concatenate([x, near, far, diagonal], axis=0)


def scatter_blocks(x):
    rows = x.shape[0] // BANDS
    got = swap(jnp.concatenate([x[rows : 2 * rows], x[3 * rows :]], axis=0), "band", 1)
    own = x[:rows].astype(F32) + got[:rows].astype(F32)
    far = (x[2 * rows : 3 * rows].astype(F32) + got[rows:].astype(F32)).astype(BF16)
    return own + swap(far, "band", 2).astype(F32)


def reduce_small(vectors, more, down_bias, up_bias, out_own, grad_own, special_count):
    crops = lax.axis_size("crop")
    width = vectors.shape[1]
    owned = -(-special_count // BANDS)
    both = jnp.concatenate([out_own[:owned], grad_own[:owned]], axis=1).astype(BF16)
    both = lax.all_gather(both, "band", axis=0, tiled=False)
    both = jnp.transpose(both, (1, 0, 2)).reshape(owned * BANDS, 2 * width)[:special_count]
    plain = jnp.concatenate([vectors[:5], more[:5], down_bias], axis=0)
    plain = jnp.transpose(plain.reshape(11, crops, -1), (1, 0, 2)).reshape(crops, -1)
    packed = jnp.concatenate([plain, up_bias.reshape(crops, -1)], axis=1)
    packed = lax.psum_scatter(packed, "crop", scatter_dimension=0, tiled=False)
    packed = lax.psum(packed, "band")
    part = width // crops
    rows = [packed[i * part : (i + 1) * part] for i in range(11)]
    return rows, packed[11 * part :], both[None, :, :width], both[None, :, width:]


def attend_back_kernel(
    weights, queries, keys, values, attended, totals, attended_grad, query_grad, key_grad, value_grad
):
    inputs = (weights, queries, keys, values, attended, totals, attended_grad)
    part = attend_back_pair(*inputs, (key_grad.at[0], value_grad.at[0]))
    query_grad[0] = part.astype(BF16)


def joint_back_kernel(
    slots, info, firsts_t, query_grad, key_grad, value_grad, weight, joint_keep, joint_send, first_grad, sums
):
    rows, width = query_grad.shape[1], weight.shape[0]
    for block in range(BANDS):
        part = first_part(block, rows, query_grad, key_grad, value_grad, weight)
        first_grad[block * rows : (block + 1) * rows, :] = part.astype(BF16)
    third = 3 * PAIR
    for part in range(query_grad.shape[0] // 2):
        keep, send = joint_columns(
            firsts_t, query_grad, key_grad, value_grad, own_pair_first(part, lax.axis_index("band"))
        )
        joint_keep[:, part * third : (part + 1) * third] = keep
        joint_send[:, part * third : (part + 1) * third] = send
    sums[...] = bias_sums(info, slots, rows, query_grad, value_grad)


def first_back_kernel(
    slots, info, first_grad, tokens, middle_grad, mask, gain, sums, patches, specials, vectors
):
    special_grad, rows = first_back(
        slots, info, first_grad[...], tokens, middle_grad, mask, gain, patches
    )
    specials[...] = special_grad
    vectors[...] = jnp.concatenate(rows + [sums[0:5]], axis=0)


def joint_order(x):
    rows, columns = x.shape
    x = x.reshape(rows, columns // (3 * PAIR), 3, PAIR)
    return jnp.transpose(x, (0, 2, 1, 3)).reshape(rows, columns)


def backward_general(given, slots, special_count):
    g = given
    rows, width = g["tokens"].shape
    every = BANDS * rows
    pairs = width // PAIR
    shaped = jax.ShapeDtypeStruct
    own_pair = pl.BlockSpec((rows, PAIR), lambda i: (0, i))
    grads = pl.pallas_call(
        attend_back_kernel,
        grid=(pairs,),
        out_shape=[
            shaped((pairs, rows, PAIR), BF16),
            shaped((pairs, every, PAIR), BF16),
            shaped((pairs, every, PAIR), BF16),
        ],
        in_specs=[
            pl.BlockSpec((1, 2 * rows, every), lambda i: (i, 0, 0)),
            pl.BlockSpec((1, rows, PAIR), lambda i: (i, 0, 0)),
            pl.BlockSpec((1, every, PAIR), lambda i: (i, 0, 0)),
            pl.BlockSpec((1, every, PAIR), lambda i: (i, 0, 0)),
            own_pair,
            own_pair,
            own_pair,
        ],
        out_specs=[
            pl.BlockSpec((1, rows, PAIR), lambda i: (i, 0, 0)),
            pl.BlockSpec((1, every, PAIR), lambda i: (i, 0, 0)),
            pl.BlockSpec((1, every, PAIR), lambda i: (i, 0, 0)),
        ],
        compiler_params=params(),
        name="attend_back",
    )(
        g["weights"],
        g["queries"],
        g["keys"],
        g["values"],
        g["attended"],
        g["totals"],
        g["attended_grad"],
    )
    half = width // 2
    joint_keep, joint_send, parts, sums = pl.pallas_call(
        partial(joint_back_kernel, slots),
        out_shape=[
            shaped((width, 3 * half), BF16),
            shaped((width, 3 * half), BF16),
            shaped((every, width), BF16),
            shaped((8, width), F32),
        ],
        in_specs=[SMEM] + [VMEM] * 5,
        out_specs=[VMEM] * 4,
        compiler_params=params(),
        name="joint_back",
    )(g["info"], g["firsts_t"], *grads, g["joint_weight"])
    grad_patches, grad_own, more = pl.pallas_call(
        partial(first_back_kernel, slots),
        out_shape=[
            shaped((slots, width), BF16),
            shaped((rows - slots, width), F32),
            shaped((8, width), F32),
        ],
        in_specs=[SMEM] + [VMEM] * 6,
        out_specs=[VMEM] * 3,
        compiler_params=params(),
        name="first_back",
    )(
        g["info"],
        scatter_blocks(parts),
        g["tokens"],
        g["middle_grad"],
        g["mask"],
        g["first_gain"],
        sums,
    )
    small = reduce_small(
        g["vectors"],
        more,
        g["down_bias_grad"],
        g["up_bias_grad"],
        g["out_own"],
        grad_own,
        special_count,
    )
    matrices = (
        reduce_half(g["mlp_grads"]["up_keep"], g["mlp_grads"]["up_got"], half),
        reduce_half(g["mlp_grads"]["down_keep"], g["mlp_grads"]["down_got"], half),
        reduce_half(g["out_keep"], swap(g["out_send"], "band", 1), half),
        joint_order(reduce_half(joint_keep, swap(joint_send, "band", 1), half)),
    )
    return (grad_patches,) + matrices + small


MESH = pl.DeviceIdType.MESH
CROPS = 8
X_FIRST = (1, 3, 5, 7, 9, 10)
DIRECT = (11,)
NEIGHBOURS = ("core", "x", "diagonal")
PLACES = NEIGHBOURS + tuple(range(1, CROPS))


class Place:
    def __init__(self):
        band, crop = lax.axis_index("band"), lax.axis_index("crop")
        self.band = band
        self.core, self.x = lax.rem(band, 2), lax.div(band, 2)
        self.y, self.near, self.far = lax.rem(crop, 2), lax.rem(lax.div(crop, 2), 2), lax.div(crop, 4)
        core_step, x_step = 1 - 2 * self.core, 2 - 4 * self.x
        self.device = {
            "core": (band + core_step, crop),
            "x": (band + x_step, crop),
            "diagonal": (band + core_step + x_step, crop),
            "y": (band, crop + 1 - 2 * self.y),
            "near": (band, crop + 2 - 4 * self.near),
            "far": (band, crop + 4 - 8 * self.far),
        }
        self.crop = crop
        for step in range(1, CROPS):
            self.device[step] = (band, lax.rem(crop + step, CROPS))

    def greet(self, names):
        barrier = pltpu.get_barrier_semaphore()
        for name in names:
            pl.semaphore_signal(barrier, inc=1, device_id=self.device[name], device_id_type=MESH)
        pl.semaphore_wait(barrier, len(names))


class Sender:
    def __init__(self, place, send_sems, recv_sems):
        self.place, self.send_sems, self.recv_sems = place, send_sems, recv_sems
        self.routes = {}
        self.sent = []

    def add(self, key, source, target, name):
        self.routes[key] = (len(self.routes), source, target, name)

    def copy(self, key):
        index, source, target, name = self.routes[key]
        return pltpu.make_async_remote_copy(
            src_ref=source,
            dst_ref=target,
            send_sem=self.send_sems.at[index],
            recv_sem=self.recv_sems.at[index],
            device_id=self.place.device[name],
            device_id_type=MESH,
        )

    def send(self, key):
        self.copy(key).start()
        self.sent.append(key)

    def arrived(self, key):
        self.copy(key).wait_recv()

    def left(self, key):
        self.copy(key).wait_send()
        self.sent.remove(key)

    def finish(self):
        for key in self.sent:
            self.copy(key).wait_send()


def chunk_list(hidden_parts):
    chunks = []
    for part in range(hidden_parts):
        chunks += [("down", part), ("up", part)]
    return chunks + [("out", 0), ("joint", 0), ("joint", 1), ("joint", 2)]


def chunk_scratch(count, rows, columns):
    unit = (rows, columns)
    return [
        pltpu.VMEM((count, 2, 2, 2, 2) + unit, BF16),
        pltpu.VMEM((count, 2, 2, 2) + unit, BF16),
        pltpu.VMEM((count, 2, 2) + unit, BF16),
        pltpu.VMEM((count, 2) + unit, BF16),
        pltpu.VMEM((count, 3, 2) + unit, BF16),
    ]


class ChunkSums:
    def __init__(self, place, sender, buffers, total, count):
        p, self.sender, self.place, self.total = place, sender, place, total
        own, got_a, got_b, got_c, got_d = buffers
        self.got_d = got_d
        self.table = {}
        for n in range(count):
            both, half = total.at[n, p.core], total.at[n, p.core, p.x]
            if x_first(n):
                kept = [
                    own.at[n, p.x],
                    own.at[n, p.x, :, :, p.y],
                    own.at[n, p.x, :, p.near, p.y],
                    own.at[n, p.x, p.far, p.near, p.y],
                ]
                got = [got_a.at[n], got_b.at[n], got_c.at[n], got_d.at[n, 0, 0]]
                sent = [
                    own.at[n, 1 - p.x],
                    own.at[n, p.x, :, :, 1 - p.y],
                    own.at[n, p.x, :, 1 - p.near, p.y],
                    own.at[n, p.x, 1 - p.far, p.near, p.y],
                ]
                names = ("x", "y", "near", "far")
            else:
                kept = [
                    own.at[n, :, :, p.y],
                    own.at[n, :, p.near, p.y],
                    own.at[n, p.far, p.near, p.y],
                ]
                got = [got_a.at[n], got_b.at[n], got_c.at[n]]
                sent = [
                    own.at[n, :, :, 1 - p.y],
                    own.at[n, :, 1 - p.near, p.y],
                    own.at[n, 1 - p.far, p.near, p.y],
                ]
                names = ("y", "near", "far")
            rows = [(None, None, None, [(sent[0], got[0], names[0])])]
            for i in range(1, len(names)):
                add = (kept[i - 1], kept[i - 1], got[i - 1])
                rows.append(add + ([(sent[i], got[i], names[i])],))
            end = (kept[-1], got[-1])
            if direct(n):
                targets = [half] * 3 if x_first(n) else [got_d.at[n, i] for i in range(3)]
                last = half if x_first(n) else both
                rows.append((last,) + end + ([(last, t, m) for t, m in zip(targets, NEIGHBOURS)],))
            elif x_first(n):
                rows.append((half,) + end + ([(half, half, "x")],))
                rows.append((None, None, None, [(both, both, "core")]))
            else:
                rows.append((kept[-1],) + end + ([(kept[-1], got_d.at[n, 0], "x")],))
                rows.append((both, kept[-1], got_d.at[n, 0], [(both, both, "core")]))
            self.table[n] = rows
            for stage, row in enumerate(rows):
                for i, (source, target, name) in enumerate(row[3]):
                    sender.add((n, stage + 1, i), source, target, name)

    def steps(self, n):
        return len(self.table[n]) + 1

    def step(self, n, stage):
        rows, sender = self.table[n], self.sender
        if stage > 0:
            for i in range(len(rows[stage - 1][3])):
                sender.arrived((n, stage, i))
        if stage == len(rows):
            if direct(n) and not x_first(n):
                for i in range(3):
                    sender.left((n, stage, i))
                p, total, got = self.place, self.total, self.got_d
                total[n, p.core] = total[n, p.core] + got[n, 1]
                total[n, 1 - p.core] = got[n, 0] + got[n, 2]
            return
        into, kept, got, sent = rows[stage]
        if into is not None:
            into[...] = kept[...] + got[...]
        for i in range(len(sent)):
            sender.send((n, stage + 1, i))


class VectorSums:
    def __init__(self, place, sender, buffers, total):
        self.place, self.sender, self.total = place, sender, total
        self.own, self.got, self.parts = buffers
        for step in range(1, CROPS):
            source = self.own.at[lax.rem(place.crop + step, CROPS)]
            sender.add(("vector", step), source, self.got.at[place.crop], step)
        here = self.parts.at[place.band]
        for name in NEIGHBOURS:
            sender.add(("parts", name), here, here, name)

    def spread(self):
        for step in range(1, CROPS):
            self.sender.send(("vector", step))

    def share(self):
        p = self.place
        self.got[p.crop] = self.own[p.crop]
        for step in range(1, CROPS):
            self.sender.arrived(("vector", step))
        self.parts[p.band] = jnp.sum(self.got[...], axis=0)
        for name in NEIGHBOURS:
            self.sender.send(("parts", name))

    def close(self):
        for name in NEIGHBOURS:
            self.sender.arrived(("parts", name))
        self.total[...] = jnp.sum(self.parts[...], axis=0)


def pack_vectors(own, rows, up_bias, part):
    for crop in range(CROPS):
        span = slice(crop * part, (crop + 1) * part)
        wide = 4 * crop * part
        wider = [up_bias[0:1, wide + j * part : wide + (j + 1) * part] for j in range(4)]
        own[crop, 0:15, 0:part] = jnp.concatenate([rows[:, span]] + wider, axis=0)


def vector_scratch():
    return [
        pltpu.VMEM((CROPS, 16, 128), F32),
        pltpu.VMEM((CROPS, 16, 128), F32),
        pltpu.VMEM((BANDS, 16, 128), F32),
    ]


def x_first(n):
    return n in X_FIRST


def direct(n):
    return n in DIRECT


def halves_of(n):
    return (0, 1) if x_first(n) else (None,)


def part_of(ref, name, part, columns, x_half):
    at = slice(None) if x_half is None else x_half
    if name == "down":
        return ref.at[:, :, :, part, at]
    return ref.at[:, :, :, at, :, pl.ds(part * columns, columns)]


def piece(ref, x_half):
    return ref if x_half is None else ref.at[x_half]


def middle_all_kernel(
    chunks,
    slots,
    parts,
    info,
    attended,
    tokens,
    out_weight,
    out_bias,
    first_scale,
    gain,
    shift,
    second_scale,
    cot_patches,
    cot_specials,
    down_bias,
    up,
    up_bias,
    down,
    out_patches,
    out_specials,
    middle_grad,
    attended_grad,
    out_keep,
    out_send,
    vectors,
    down_bias_grad,
    up_bias_grad,
    kept_out,
    sent_out,
    *scratch,
):
    (
        kept,
        sent,
        branch,
        middle,
        second,
        second_t,
        incoming,
        down_in,
        down_keep,
        down_send,
        branch_two,
        second_grad,
        active_t,
        store_sems,
    ) = scratch
    step = pl.program_id(0)
    width = tokens.shape[1]
    count = kept.shape[0]
    band = lax.axis_index("band")

    def stores(n):
        return [
            pltpu.make_async_copy(kept.at[n], kept_out.at[n], store_sems.at[0, n]),
            pltpu.make_async_copy(sent.at[n], sent_out.at[n], store_sems.at[1, n]),
        ]

    def made(n, value, x_halves):
        shape = (2, 2, 2, 2, width // CROPS // 2, width // 2)
        for half, target in zip(own_half(value, band), (kept.at[n], sent.at[n])):
            half = half.reshape(shape)
            if x_halves:
                for h in range(2):
                    target[h] = half[:, :, :, h]
            else:
                target[...] = half
        for copy in stores(n):
            copy.start()

    @pl.when(step == 0)
    def _():
        middle_kernel(
            slots,
            info,
            attended,
            tokens,
            out_weight,
            out_bias,
            first_scale,
            gain,
            shift,
            second_scale,
            cot_patches,
            cot_specials,
            branch,
            middle,
            second,
            incoming,
            down_in,
            down_keep,
            down_send,
            down_bias_grad,
        )
        second_t[...] = second[...].astype(F32).T.astype(BF16)
        branch_two[...] = jnp.zeros_like(branch_two)
        second_grad[...] = jnp.zeros_like(second_grad)

    @pl.when(step < parts)
    def _():
        hidden = dot(second[...], up[...]) + up_bias[...]
        active, slope = gelu_and_slope(hidden)
        active = active.astype(BF16)
        span = pl.ds(pl.multiple_of(step * width, width), width)
        active_t[span, :] = active.astype(F32).T.astype(BF16)
        hidden_in = (slope * dot_nt(down_in[...], down[...])).astype(BF16)
        made(2 * step + 1, dot(second_t[...], hidden_in).astype(BF16), True)
        branch_two[...] += dot(active, down[...])
        second_grad[...] += dot_nt(hidden_in, up[...])
        up_bias_grad[...] = column_sum(hidden_in.astype(F32))

    @pl.when((step >= parts) & (step < 2 * parts))
    def _():
        part = step - parts
        own_rows = width // CROPS
        starts = [
            pl.multiple_of((crop * parts + part) * own_rows, own_rows) for crop in range(CROPS)
        ]
        rows = jnp.concatenate([active_t[pl.ds(i, own_rows), :] for i in starts], axis=0)
        made(2 * part, dot(rows, down_in[...]).astype(BF16), False)

    @pl.when(step == 2 * parts)
    def _():
        middle_back_kernel(
            slots,
            info,
            middle,
            branch,
            branch_two,
            second_grad,
            incoming,
            attended,
            out_weight,
            down_bias,
            second_scale,
            gain,
            first_scale,
            out_patches,
            out_specials,
            middle_grad,
            attended_grad,
            out_keep,
            out_send,
            vectors,
        )
        for n in range(count):
            for copy in stores(n):
                copy.wait()


def middle_fused(
    info,
    attended,
    tokens,
    out_weight,
    out_bias,
    first_scale,
    second_gain,
    second_shift,
    second_scale,
    cot_patches,
    cot_specials,
    down_bias,
    up_weight,
    up_bias,
    down_weight,
):
    rows, width = tokens.shape
    slots = cot_patches.shape[0]
    hidden_width = up_weight.shape[1]
    parts = hidden_width // width
    chunks = chunk_list(parts)
    count = 2 * parts
    unit_rows, half = width // CROPS // 2, width // 2
    unit = (2, 2, 2, 2, unit_rows, half)
    shaped = jax.ShapeDtypeStruct
    last = parts - 1
    outs = pl.pallas_call(
        partial(middle_all_kernel, chunks, slots, parts),
        grid=(2 * parts + 1,),
        out_shape=[
            shaped((slots, width), BF16),
            shaped((rows - slots, width), F32),
            shaped((rows, width), F32),
            shaped((rows, width), F32),
            shaped((width, half), BF16),
            shaped((width, half), BF16),
            shaped((8, width), F32),
            shaped((1, width), F32),
            shaped((1, hidden_width), F32),
            shaped((count,) + unit, BF16),
            shaped((count,) + unit, BF16),
        ],
        in_specs=[SMEM]
        + [VMEM] * 11
        + [
            pl.BlockSpec((width, width), lambda i: (0, jnp.minimum(i, last))),
            pl.BlockSpec((1, width), lambda i: (0, jnp.minimum(i, last))),
            pl.BlockSpec((width, width), lambda i: (jnp.minimum(i, last), 0)),
        ],
        out_specs=[VMEM] * 8 + [pl.BlockSpec((1, width), lambda i: (0, jnp.minimum(i, last))), ANY, ANY],
        scratch_shapes=[
            pltpu.VMEM((count,) + unit, BF16),
            pltpu.VMEM((count,) + unit, BF16),
            pltpu.VMEM((rows, width), F32),
            pltpu.VMEM((rows, width), F32),
            pltpu.VMEM((rows, width), BF16),
            pltpu.VMEM((width, rows), BF16),
            pltpu.VMEM((rows, width), F32),
            pltpu.VMEM((rows, width), BF16),
            pltpu.VMEM((rows, half), BF16),
            pltpu.VMEM((rows, half), BF16),
            pltpu.VMEM((rows, width), F32),
            pltpu.VMEM((rows, width), F32),
            pltpu.VMEM((hidden_width, rows), BF16),
            pltpu.SemaphoreType.DMA((2, count)),
        ],
        compiler_params=params(),
        name="middle_all",
    )(
        info,
        attended,
        tokens,
        out_weight,
        out_bias,
        first_scale,
        second_gain,
        second_shift,
        second_scale,
        cot_patches,
        cot_specials,
        down_bias,
        up_weight,
        up_bias,
        down_weight,
    )
    return tuple(outs[:9]) + (outs[9:],)


PLAN = (
    (0, 1, 0), (0, 0, 0), (1, 3, 0), (1, 2, 0), (1, 5, 0), (1, 4, 0),
    (2, 7, 0), (2, 6, 0), (3, 8, 0), (3, 1, 1), (3, 0, 1), (5, 0, 2),
    (5, 3, 1), (5, 2, 1), (6, 0, 3), (7, 2, 2), (7, 5, 1), (7, 4, 1),
    (8, 7, 1), (8, 2, 3), (8, 6, 1), (8, 9, 0), (9, 0, 4), (9, 4, 2),
    (10, 6, 2), (10, 0, 5), (10, 8, 1), (10, 10, 0), (10, 4, 3), (11, 1, 2),
    (12, 3, 2), (12, 6, 3), (13, 8, 2), (14, 5, 2), (14, 1, 3), (14, 11, 0),
    (14, 3, 3), (14, 2, 4), (16, 7, 2), (17, 8, 3), (17, 2, 5), (17, 5, 3),
    (18, 1, 4), (20, 3, 4), (20, 7, 3), (20, 9, 1), (21, 5, 4), (21, 11, 1),
    (23, 7, 4), (24, 9, 2), (25, 10, 1), (26, 11, 2), (27, 4, 4), (28, 9, 3),
    (29, 6, 4), (30, 4, 5), (31, 10, 2), (32, 8, 4), (33, 11, 3), (34, 1, 5),
    (35, 6, 5), (36, 3, 5), (37, 9, 4), (38, 5, 5), (39, 8, 5), (40, 10, 3),
    (41, 7, 5), (42, 1, 6), (43, 3, 6), (44, 5, 6), (45, 7, 6), (46, 10, 4),
    (47, 11, 4), (48, 9, 5), (49, 10, 5), (50, 9, 6), (51, 10, 6),
)


def backward_kernel(
    chunks,
    slots,
    pairs,
    info,
    weights,
    queries,
    keys,
    values,
    attended,
    totals,
    attended_grad,
    mask,
    gain,
    vectors,
    down_bias,
    up_bias,
    out_own,
    kept_in,
    sent_in,
    out_keep,
    out_send,
    firsts_in,
    weight_in,
    tokens_in,
    middle_grad_in,
    grad_patches,
    total_out,
    vector_total,
    specials_out,
    *scratch,
):
    buffers, vector_buffers = scratch[:5], scratch[5:8]
    (
        total,
        got,
        out_got,
        joint_got,
        joint_sent,
        query_sum,
        query_grad,
        key_grad,
        value_grad,
        firsts_t,
        weight,
        tokens,
        middle_grad,
        parts,
        got_parts,
        got_far,
        specials,
        send_sems,
        recv_sems,
        load_sems,
        whole_sems,
    ) = scratch[8:]
    step = pl.program_id(0)
    count = len(chunks)
    columns = total.shape[4]
    rows, width = tokens.shape
    place = Place()
    sender = Sender(place, send_sems, recv_sems)
    sums = ChunkSums(place, sender, buffers, total, count)
    vector_sums = VectorSums(place, sender, vector_buffers, vector_total)
    own = buffers[0]
    passed = kept_in.shape[0]

    def own_loads(n):
        if n < passed:
            return [pltpu.make_async_copy(kept_in.at[n], own.at[n], load_sems.at[n, 0])]
        return [
            pltpu.make_async_copy(
                part_of(out_keep, "out", 0, columns, h), piece(own.at[n], h), load_sems.at[n, i]
            )
            for i, h in enumerate(halves_of(n))
        ]

    def whole_loads():
        pairs_of = ((weight_in, weight), (firsts_in, firsts_t), (tokens_in, tokens), (middle_grad_in, middle_grad))
        return [
            pltpu.make_async_copy(a, b, whole_sems.at[i]) for i, (a, b) in enumerate(pairs_of)
        ]

    early = [n for n, (name, _) in enumerate(chunks) if name != "joint"]
    out_chunk = early[-1]
    late = [n for n, (name, _) in enumerate(chunks) if name == "joint"]

    for n in range(passed):
        sender.add((n, 0), sent_in.at[n], got.at[n], "core")
    for h in halves_of(out_chunk):
        source = part_of(out_send, "out", 0, columns, h)
        sender.add((out_chunk, 0, h), source, piece(out_got, h), "core")
    for n in late:
        sender.add((n, 0), joint_sent.at[n - late[0]], joint_got.at[n - late[0]], "core")
    for index in range(2):
        sender.add(("first", index), parts.at[index], got_parts.at[index], "core")
    sender.add("far", parts.at[2], got_far, "x")
    for name in NEIGHBOURS:
        sender.add(("special", name), specials.at[place.band], specials.at[place.band], name)

    def begin():
        for n in early:
            for copy in own_loads(n):
                copy.start()
        place.greet(PLACES)
        for _, n, stage in PLAN:
            if stage == 0 and n < passed:
                sender.send((n, 0))
        for h in halves_of(out_chunk):
            sender.send((out_chunk, 0, h))

    def early_stage(n, stage):
        if stage == 0:
            for copy in own_loads(n):
                copy.wait()
            if n == out_chunk:
                for h in halves_of(n):
                    sender.arrived((n, 0, h))
                own[n] = own[n] + out_got[...]
            else:
                sender.arrived((n, 0))
                own[n] = own[n] + got[n]
        sums.step(n, stage)

    def late_stage(n, stage):
        if stage == 0:
            sender.arrived((n, 0))
            own[n] = own[n] + joint_got[n - late[0]]
        sums.step(n, stage)

    def stage_of(n, stage):
        (late_stage if n in late else early_stage)(n, stage)

    def exchanges(slot):
        for place_of, n, stage in PLAN:
            if place_of == slot:
                stage_of(n, stage)

    def occupied(slot):
        return any(place_of == slot for place_of, _, _ in PLAN)

    def joint_chunk(part):
        n = late[part]
        picked = joint_columns(firsts_t, *grads, own_pair_first(part, place.band))
        shape = (2, 2, 2, 2, width // CROPS // 2, columns)
        for value, target in zip(picked, (own.at[n], joint_sent.at[part])):
            value = value.reshape(shape)
            for h in halves_of(n):
                if h is None:
                    target[...] = value
                else:
                    target[h] = value[:, :, :, h]
        sender.send((n, 0))

    half_rows = 2 * rows
    per_step = 1

    def between(index):
        for i in range(2 * pairs):
            if occupied(i):

                @pl.when(index == i)
                def _():
                    exchanges(i)

    grads = (query_grad, key_grad, value_grad)
    last = 2 * pairs
    after = last * per_step

    @pl.when(step == 0)
    def _():
        begin()

    @pl.when(step == 1)
    def _():
        for copy in whole_loads():
            copy.start()

    @pl.when(step == pairs)
    def _():
        for copy in whole_loads():
            copy.wait()
        parts[1] = first_part(3, rows, *grads, weight).astype(BF16)
        sender.send(("first", 1))
        parts[2] = first_part(2, rows, *grads, weight).astype(BF16)

    @pl.when(step == pairs + 1)
    def _():
        sender.arrived(("first", 1))
        parts[2] = parts[2] + got_parts[1]
        sender.send("far")

    for part in range(2):

        @pl.when(step == pairs + 2 * part + 2)
        def _():
            joint_chunk(part)

    @pl.when(step < last)
    def _():
        far_half = step < pairs
        pair = jnp.where(far_half, step, jnp.minimum(step - pairs, pairs - 1))
        first_row = pl.multiple_of(jnp.where(far_half, half_rows, 0), half_rows)
        span = pl.ds(first_row, half_rows)
        outs = (key_grad.at[pair, span], value_grad.at[pair, span])
        inputs = (weights, queries, keys, values, attended, totals, attended_grad)
        part = attend_back_pair(*inputs, outs)
        between(step)

        @pl.when(far_half)
        def _():
            query_sum[pair] = part

        @pl.when(step >= pairs)
        def _():
            query_grad[pair] = (query_sum[pair] + part).astype(BF16)

    @pl.when(step == last)
    def _():
        joint_chunk(2)
        exchanges(after)
        parts[0] = first_part(1, rows, *grads, weight).astype(BF16)
        sender.send(("first", 0))
        exchanges(after + 1)
        first_grad = first_part(0, rows, *grads, weight)
        exchanges(after + 2)
        biases = bias_sums(info, slots, rows, query_grad, value_grad)
        exchanges(after + 3)
        sender.arrived(("first", 0))
        sender.arrived("far")
        first_grad = first_grad + got_parts[0].astype(F32) + got_far[...].astype(F32)
        special_grad, rows_of = first_back(
            slots,
            info,
            first_grad,
            tokens,
            middle_grad,
            mask,
            gain,
            grad_patches,
            lambda part: exchanges(after + 4 + part),
        )
        specials[place.band] = jnp.concatenate([out_own[0:4], special_grad[0:4]], axis=0)
        for name in NEIGHBOURS:
            sender.send(("special", name))
        packed = jnp.concatenate([vectors[0:5]] + rows_of + [biases[0:2], down_bias[...]], axis=0)
        pack_vectors(vector_sums.own, packed, up_bias, width // CROPS)
        vector_sums.spread()
        ends = max(entry[0] for entry in PLAN) + 1
        start = after + 4 + rows // ROW_PART
        shared = min(start + 5, ends - 1)
        closed = min(start + 12, ends - 1)
        for slot in range(start, ends):
            exchanges(slot)
            if slot == shared:
                vector_sums.share()
            if slot == closed:
                vector_sums.close()
        for name in NEIGHBOURS:
            sender.arrived(("special", name))
        specials_out[...] = specials[...]
        sender.finish()
        copy = pltpu.make_async_copy(total, total_out, whole_sems.at[4])
        copy.start()
        copy.wait()


def finish_kernel(
    chunks,
    special_count,
    total,
    vector_total,
    specials,
    grad_patches,
    up,
    down,
    out,
    joint,
    up_bias,
    out_specials,
    grad_specials,
    grad_patches_out,
    *vectors,
):
    grad_patches_out[...] = grad_patches[...]
    _, _, _, rows, columns = total.shape
    refs = dict(up=up, down=down, out=out, joint=joint)
    for n, (name, part) in enumerate(chunks):
        for core in range(2):
            for x in range(2):
                row, column = x * rows, core * columns
                if name == "down":
                    row += 2 * rows * part
                else:
                    column += 2 * columns * part
                value = total[n, core, x].astype(F32)
                if name == "joint":
                    for third in range(3):
                        column = third * 2 * columns + (2 * part + core) * PAIR
                        piece_of = value[:, third * PAIR : (third + 1) * PAIR]
                        joint[row : row + rows, column : column + PAIR] = piece_of
                    continue
                refs[name][row : row + rows, column : column + columns] = value
    part = vectors[0].shape[0]
    for i, vector in enumerate(vectors):
        vector[...] = vector_total[i, 0:part]
    up_bias[...] = jnp.concatenate([vector_total[i : i + 1, 0:part] for i in range(11, 15)], axis=1)[0]
    for first, target in ((0, out_specials), (4, grad_specials)):
        picked = [
            specials[s % BANDS, first + s // BANDS : first + s // BANDS + 1]
            for s in range(special_count)
        ]
        target[0] = jnp.concatenate(picked, axis=0).astype(BF16)


def backward_fused(given, slots, special_count):
    g = given
    rows, width = g["tokens"].shape
    hidden_width = g["up_bias_grad"].shape[1]
    every = BANDS * rows
    pairs = width // PAIR
    chunks = chunk_list(hidden_width // width)
    count = len(chunks)
    part = width // CROPS
    unit_rows, columns = part // 2, width // 2
    unit = (2, 2, 2, 2, unit_rows, columns)
    hidden_parts = hidden_width // width
    shaped = jax.ShapeDtypeStruct
    last = 2 * pairs - 1
    far_first = lambda i: 1 - jnp.minimum(i, last) // pairs
    pair_of = lambda i: jnp.minimum(i, last) % pairs
    own_pair = pl.BlockSpec((rows, PAIR), lambda i: (0, pair_of(i)))
    own_heads = pl.BlockSpec((1, rows, PAIR), lambda i: (pair_of(i), 0, 0))
    half_heads = pl.BlockSpec((1, 2 * rows, PAIR), lambda i: (pair_of(i), far_first(i), 0))
    kept = pl.BlockSpec((1, 2 * rows, 2 * rows), lambda i: (pair_of(i), 0, far_first(i)))
    grad_patches, total, vector_total, specials = pl.pallas_call(
        partial(backward_kernel, chunks, slots, pairs),
        grid=(2 * pairs + 1,),
        out_shape=[
            shaped((slots, width), BF16),
            shaped((count, 2, 2, unit_rows, columns), BF16),
            shaped((16, 128), F32),
            shaped((BANDS, 8, width), F32),
        ],
        in_specs=[SMEM, kept, own_heads, half_heads, half_heads, own_pair, own_pair, own_pair]
        + [VMEM] * 6
        + [ANY] * 8,
        out_specs=[VMEM, ANY, VMEM, VMEM],
        scratch_shapes=chunk_scratch(count, unit_rows, columns)
        + vector_scratch()
        + [
            pltpu.VMEM((count, 2, 2, unit_rows, columns), BF16),
            pltpu.VMEM((2 * hidden_parts,) + unit, BF16),
            pltpu.VMEM(unit, BF16),
            pltpu.VMEM((3,) + unit, BF16),
            pltpu.VMEM((3,) + unit, BF16),
            pltpu.VMEM((pairs, rows, PAIR), F32),
            pltpu.VMEM((pairs, rows, PAIR), BF16),
            pltpu.VMEM((pairs, every, PAIR), BF16),
            pltpu.VMEM((pairs, every, PAIR), BF16),
            pltpu.VMEM((width, every), BF16),
            pltpu.VMEM((width, 3 * width), BF16),
            pltpu.VMEM((rows, width), F32),
            pltpu.VMEM((rows, width), F32),
            pltpu.VMEM((3, rows, width), BF16),
            pltpu.VMEM((2, rows, width), BF16),
            pltpu.VMEM((rows, width), BF16),
            pltpu.VMEM((BANDS, 8, width), F32),
            pltpu.SemaphoreType.DMA((10 * count,)),
            pltpu.SemaphoreType.DMA((10 * count,)),
            pltpu.SemaphoreType.DMA((count, 2)),
            pltpu.SemaphoreType.DMA((5,)),
        ],
        compiler_params=pltpu.CompilerParams(
            vmem_limit_bytes=VMEM_LIMIT, collective_id=0, has_side_effects=True
        ),
        name="backward",
    )(
        g["info"],
        g["weights"],
        g["queries"],
        g["keys"],
        g["values"],
        g["attended"],
        g["totals"],
        g["attended_grad"],
        g["mask"],
        g["first_gain"],
        g["vectors"],
        g["down_bias_grad"],
        g["up_bias_grad"],
        g["out_own"],
        *g["mlp_grads"],
        g["out_keep"].reshape(unit),
        g["out_send"].reshape(unit),
        g["firsts_t"],
        g["joint_weight"],
        g["tokens"],
        g["middle_grad"],
    )
    special = shaped((1, special_count, width), BF16)
    results = pl.pallas_call(
        partial(finish_kernel, chunks, special_count),
        out_shape=[
            shaped((part, hidden_width), F32),
            shaped((hidden_width // CROPS, width), F32),
            shaped((part, width), F32),
            shaped((part, 3 * width), F32),
            shaped((hidden_width // CROPS,), F32),
            special,
            special,
            shaped((slots, width), BF16),
        ]
        + [shaped((part,), F32)] * 11,
        in_specs=[VMEM] * 4,
        out_specs=[VMEM] * 19,
        compiler_params=params(),
        name="finish",
    )(total, vector_total, specials, grad_patches)
    up, down, out, joint, up_bias, out_specials, grad_specials, grad_patches = results[:8]
    return grad_patches, up, down, out, joint, results[8:], up_bias, out_specials, grad_specials


def forward_fused(
    info, mask, patches, specials, token, gain, shift, weight, query_bias, value_bias, rows
):
    slots, width = patches.shape
    every, pairs = BANDS * rows, width // PAIR
    shaped = jax.ShapeDtypeStruct
    half_of = lambda i: i // pairs
    pair_of = lambda i: i % pairs
    final_pair = pl.BlockSpec((rows, PAIR), lambda i: (0, jnp.maximum(i - pairs, 0)))
    outs = pl.pallas_call(
        partial(forward_kernel, slots, pairs),
        grid=(2 * pairs,),
        out_shape=[
            shaped((rows, width), F32),
            shaped((pairs, rows, PAIR), BF16),
            shaped((pairs, every, PAIR), BF16),
            shaped((pairs, every, PAIR), BF16),
            shaped((rows, width), F32),
            shaped((rows, width), F32),
            shaped((pairs, 2 * rows, every), BF16),
            shaped((width, every), BF16),
        ],
        in_specs=[SMEM] + [VMEM] * 8 + [ANY],
        out_specs=[
            ANY,
            ANY,
            ANY,
            ANY,
            final_pair,
            final_pair,
            pl.BlockSpec((1, 2 * rows, 2 * rows), lambda i: (pair_of(i), 0, half_of(i))),
            pl.BlockSpec((PAIR, 2 * rows), lambda i: (pair_of(i), half_of(i))),
        ],
        scratch_shapes=[
            pltpu.VMEM((rows, width), F32),
            pltpu.VMEM((BANDS, rows, width), BF16),
            pltpu.VMEM((pairs, rows, PAIR), BF16),
            pltpu.VMEM((pairs, every, PAIR), BF16),
            pltpu.VMEM((pairs, every, PAIR), BF16),
            pltpu.VMEM((every, PAIR), BF16),
            pltpu.VMEM((pairs, rows, PAIR), F32),
            pltpu.VMEM((pairs, rows, PAIR), F32),
            pltpu.VMEM((width, 3 * width), BF16),
            pltpu.SemaphoreType.DMA((3,)),
            pltpu.SemaphoreType.DMA((3,)),
            pltpu.SemaphoreType.DMA((5,)),
        ],
        compiler_params=pltpu.CompilerParams(
            vmem_limit_bytes=VMEM_LIMIT, collective_id=1, has_side_effects=True
        ),
        name="forward",
    )(info, mask, patches, specials, token, gain, shift, query_bias, value_bias, weight)
    return outs


def forward_general(
    info, mask, patches, specials, token, gain, shift, weight, query_bias, value_bias, rows
):
    slots, width = patches.shape
    every, pairs = BANDS * rows, width // PAIR
    shaped = jax.ShapeDtypeStruct
    tokens, first = pl.pallas_call(
        partial(first_kernel, slots),
        out_shape=[shaped((rows, width), F32), shaped((rows, width), BF16)],
        in_specs=[SMEM] + [VMEM] * 6,
        compiler_params=params(),
        name="first",
    )(info, mask, patches, specials, token, gain, shift)
    firsts = gather_blocks(first)
    block = pl.BlockSpec((rows, width), lambda i: (i, 0))
    pair_block = pl.BlockSpec((pairs, rows, PAIR), lambda i: (0, i, 0))
    queries, keys, values = pl.pallas_call(
        partial(project_kernel, slots),
        grid=(BANDS,),
        out_shape=[
            shaped((pairs, rows, PAIR), BF16),
            shaped((pairs, every, PAIR), BF16),
            shaped((pairs, every, PAIR), BF16),
        ],
        in_specs=[SMEM, block, whole((width, 3 * width)), VMEM, VMEM],
        out_specs=[whole((pairs, rows, PAIR)), pair_block, pair_block],
        compiler_params=params(),
        name="project",
    )(info, firsts, weight, query_bias, value_bias)
    own_pair = pl.BlockSpec((rows, PAIR), lambda i: (0, i))
    all_pair = pl.BlockSpec((every, PAIR), lambda i: (0, i))
    own_heads = pl.BlockSpec((1, rows, PAIR), lambda i: (i, 0, 0))
    all_heads = pl.BlockSpec((1, every, PAIR), lambda i: (i, 0, 0))
    attended, totals, weights, firsts_t = pl.pallas_call(
        partial(attend_kernel, slots),
        grid=(pairs,),
        out_shape=[
            shaped((rows, width), F32),
            shaped((rows, width), F32),
            shaped((pairs, 2 * rows, every), BF16),
            shaped((width, every), BF16),
        ],
        in_specs=[SMEM, own_heads, all_heads, all_heads, all_pair],
        out_specs=[
            own_pair,
            own_pair,
            pl.BlockSpec((1, 2 * rows, every), lambda i: (i, 0, 0)),
            pl.BlockSpec((PAIR, every), lambda i: (i, 0)),
        ],
        compiler_params=params(),
        name="attend",
    )(info, queries, keys, values, firsts)
    return tokens, queries, keys, values, attended, totals, weights, firsts_t


def middle_general(
    info,
    attended,
    tokens,
    out_weight,
    out_bias,
    first_scale,
    second_gain,
    second_shift,
    second_scale,
    cot_patches,
    cot_specials,
    down_bias,
    up_weight,
    up_bias,
    down_weight,
):
    rows, width = tokens.shape
    slots = cot_patches.shape[0]
    hidden_width = up_weight.shape[1]
    pad = rows - slots
    shaped = jax.ShapeDtypeStruct
    branch, middle, second, incoming, down_in, down_keep, down_send, down_bias_grad = pl.pallas_call(
        partial(middle_kernel, slots),
        out_shape=[
            shaped((rows, width), F32),
            shaped((rows, width), F32),
            shaped((rows, width), BF16),
            shaped((rows, width), F32),
            shaped((rows, width), BF16),
            shaped((rows, width // 2), BF16),
            shaped((rows, width // 2), BF16),
            shaped((1, width), F32),
        ],
        in_specs=[SMEM] + [VMEM] * 10,
        out_specs=[VMEM] * 8,
        compiler_params=params(),
        name="middle",
    )(
        info,
        attended,
        tokens,
        out_weight,
        out_bias,
        first_scale,
        second_gain,
        second_shift,
        second_scale,
        cot_patches,
        cot_specials,
    )

    steps = hidden_width // width
    half = width // 2
    (
        branch_two,
        second_grad,
        up_keep,
        up_send,
        up_bias_grad,
        down_grad_keep,
        down_grad_send,
    ) = pl.pallas_call(
        mlp_kernel,
        grid=(steps,),
        out_shape=[
            shaped((rows, width), F32),
            shaped((rows, width), F32),
            shaped((width, hidden_width // 2), BF16),
            shaped((width, hidden_width // 2), BF16),
            shaped((1, hidden_width), F32),
            shaped((hidden_width, half), BF16),
            shaped((hidden_width, half), BF16),
        ],
        in_specs=[
            SMEM,
            whole((rows, width)),
            whole((rows, width)),
            whole((rows, half)),
            whole((rows, half)),
            pl.BlockSpec((width, width), lambda i: (0, i)),
            pl.BlockSpec((1, width), lambda i: (0, i)),
            pl.BlockSpec((width, width), lambda i: (i, 0)),
        ],
        out_specs=[
            whole((rows, width)),
            whole((rows, width)),
            pl.BlockSpec((width, half), lambda i: (0, i)),
            pl.BlockSpec((width, half), lambda i: (0, i)),
            pl.BlockSpec((1, width), lambda i: (0, i)),
            pl.BlockSpec((width, half), lambda i: (i, 0)),
            pl.BlockSpec((width, half), lambda i: (i, 0)),
        ],
        compiler_params=params(),
        name="mlp",
    )(info, second, down_in, down_keep, down_send, up_weight, up_bias, down_weight)
    up_got = swap(up_send, "band", 1)
    down_got = swap(down_grad_send, "band", 1)

    out_patches, out_own, middle_grad, attended_grad, out_keep, out_send, vectors = pl.pallas_call(
        partial(middle_back_kernel, slots),
        out_shape=[
            shaped((slots, width), BF16),
            shaped((pad, width), F32),
            shaped((rows, width), F32),
            shaped((rows, width), F32),
            shaped((width, half), BF16),
            shaped((width, half), BF16),
            shaped((8, width), F32),
        ],
        in_specs=[SMEM] + [VMEM] * 11,
        out_specs=[VMEM] * 7,
        compiler_params=params(),
        name="middle_back",
    )(
        info,
        middle,
        branch,
        branch_two,
        second_grad,
        incoming,
        attended,
        out_weight,
        down_bias,
        second_scale,
        second_gain,
        first_scale,
    )

    shared = (out_patches, out_own, middle_grad, attended_grad, out_keep, out_send, vectors)
    halves = dict(up_keep=up_keep, up_got=up_got, down_keep=down_grad_keep, down_got=down_got)
    return shared + (down_bias_grad, up_bias_grad, halves)


def body(
    patches,
    specials,
    patch_mask,
    band_rows,
    mask_token,
    first_gain,
    first_shift,
    joint_weight,
    query_bias,
    value_bias,
    out_weight,
    out_bias,
    first_scale,
    second_gain,
    second_shift,
    up_weight,
    up_bias,
    down_weight,
    down_bias,
    second_scale,
    cot_patches,
    cot_specials,
):
    slots, width = patches.shape[1:]
    special_count = specials.shape[1]
    hidden_width = up_weight.shape[1]
    owned = -(-special_count // BANDS)
    rows = round_up(slots + owned, 16)
    pad = rows - slots
    info = band_rows
    mask = patch_mask
    patches, specials = patches[0], specials[0]
    cot_patches, cot_specials = cot_patches[0], cot_specials[0]
    shaped = jax.ShapeDtypeStruct

    forward = forward_fused if lax.axis_size("crop") == CROPS else forward_general
    tokens, queries, keys, values, attended, totals, weights, firsts_t = forward(
        info,
        mask,
        patches,
        specials,
        mask_token,
        first_gain,
        first_shift,
        joint_weight,
        query_bias,
        value_bias,
        rows,
    )

    middle = middle_fused if lax.axis_size("crop") == CROPS else middle_general
    (
        out_patches,
        out_own,
        middle_grad,
        attended_grad,
        out_keep,
        out_send,
        vectors,
        down_bias_grad,
        up_bias_grad,
        mlp_grads,
    ) = middle(
        info,
        attended,
        tokens,
        out_weight,
        out_bias,
        first_scale,
        second_gain,
        second_shift,
        second_scale,
        cot_patches,
        cot_specials,
        down_bias,
        up_weight,
        up_bias.reshape(1, -1),
        down_weight,
    )
    given = dict(
        info=info,
        weights=weights,
        queries=queries,
        keys=keys,
        values=values,
        attended=attended,
        totals=totals,
        attended_grad=attended_grad,
        mask=mask,
        first_gain=first_gain,
        vectors=vectors,
        down_bias_grad=down_bias_grad,
        up_bias_grad=up_bias_grad,
        out_own=out_own,
        mlp_grads=mlp_grads,
        out_keep=out_keep,
        out_send=out_send,
        firsts_t=firsts_t,
        joint_weight=joint_weight,
        tokens=tokens,
        middle_grad=middle_grad,
    )
    backward = backward_fused if lax.axis_size("crop") == CROPS else backward_general
    (
        grad_patches,
        up,
        down,
        out,
        joint,
        rows_of,
        up_bias_sum,
        out_specials,
        grad_specials,
    ) = backward(given, slots, special_count)
    return (
        out_patches[None],
        out_specials,
        grad_patches[None],
        grad_specials,
        rows_of[5],
        rows_of[6],
        rows_of[7],
        joint,
        rows_of[8],
        rows_of[9],
        out,
        rows_of[4],
        rows_of[3],
        rows_of[1],
        rows_of[2],
        up,
        up_bias_sum,
        down,
        rows_of[10],
        rows_of[0],
    )


def solution(mesh):
    split = P("crop", "band", None)
    special = P("crop", None, None)
    in_specs = (
        (split, special, P("crop", "band")) + (P(),) * 17 + (split, special)
    )
    line, matrix = P("crop"), P("crop", None)
    out_specs = (
        split,
        special,
        split,
        special,
        line,
        line,
        line,
        matrix,
        line,
        line,
        matrix,
        line,
        line,
        line,
        line,
        matrix,
        line,
        matrix,
        line,
        line,
    )
    return jax.shard_map(body, mesh=mesh, in_specs=in_specs, out_specs=out_specs, check_vma=False)
```

```python
from functools import partial

import jax
import jax.numpy as jnp
from jax import lax
from jax.experimental import pallas as pl
from jax.experimental.pallas import tpu as pltpu
from jax.sharding import PartitionSpec as P

HEAD = 64
GRID = 37
PAIR = 2 * HEAD
BANDS = 4
SPECIALS = 5
ROW_PART = 64
KEY_PART = 256
F32 = jnp.float32
BF16 = jnp.bfloat16
VMEM_LIMIT = 60 << 20


def round_up(value, unit):
    return (value + unit - 1) // unit * unit


def params(semantics=None):
    return pltpu.CompilerParams(vmem_limit_bytes=VMEM_LIMIT)


def dot(a, b):
    return jnp.dot(a, b, preferred_element_type=F32)


def dot_nt(a, b):
    return lax.dot_general(a, b, (((1,), (1,)), ((), ())), preferred_element_type=F32)


def dot_tn(a, b):
    return lax.dot_general(a, b, (((0,), (0,)), ((), ())), preferred_element_type=F32)


def normalize(rows):
    centred = rows - jnp.mean(rows, axis=-1, keepdims=True)
    spread = jnp.mean(centred * centred, axis=-1, keepdims=True)
    scale = lax.rsqrt(spread + 1e-06)
    return centred * scale, scale


def normalize_back(grad, hat, scale):
    return scale * (
        grad
        - jnp.mean(grad, axis=-1, keepdims=True)
        - hat * jnp.mean(grad * hat, axis=-1, keepdims=True)
    )


def column_sum(rows):
    return jnp.sum(rows, axis=0, keepdims=True)


def line(ref):
    return ref[...].reshape(1, -1)


def whole(shape):
    return pl.BlockSpec(shape, lambda *_: (0,) * len(shape))


VMEM = pl.BlockSpec(memory_space=pltpu.VMEM)
ANY = pl.BlockSpec(memory_space=pl.ANY)
SMEM = pl.BlockSpec(memory_space=pltpu.SMEM)


def own_special(specials, band, slot):
    row = jnp.zeros((1, specials.shape[1]), F32)
    for special in range(specials.shape[0]):
        if special // BANDS == slot:
            row = row + jnp.where(band == special % BANDS, specials[special : special + 1], 0.0)
    return row


def place_rows(ref, patch_rows, specials, band):
    slots = patch_rows.shape[0]
    rows = ref.shape[0]
    ref[0:slots, :] = patch_rows
    extra = [own_special(specials, band, slot) for slot in range(rows - slots)]
    ref[slots:rows, :] = jnp.concatenate(extra, axis=0)


def block_counts(band_rows, relative):
    band = lax.axis_index("band")
    core, x = lax.rem(band, 2), lax.div(band, 2)
    core = core + lax.rem(relative, 2) * (1 - 2 * core)
    x = x + lax.div(relative, 2) * (1 - 2 * x)
    owner = 2 * x + core
    return band_rows[owner] * GRID, lax.div(SPECIALS - owner + BANDS - 1, BANDS)


def counted_rows(band_rows, relative, rows, slots, width):
    used, specials = block_counts(band_rows, relative)
    index = lax.broadcasted_iota(jnp.int32, (rows, width), 0)
    return (index < used) | ((index >= slots) & (index < slots + specials))


def stack_pair(rows):
    lane = lax.broadcasted_iota(jnp.int32, rows.shape, 1)
    zero = jnp.zeros_like(rows)
    return jnp.concatenate(
        [jnp.where(lane < HEAD, rows, zero), jnp.where(lane >= HEAD, rows, zero)], axis=0
    )


def unstack_pair(rows):
    half = rows.shape[0] // 2
    lane = lax.broadcasted_iota(jnp.int32, (half, rows.shape[1]), 1)
    return jnp.where(lane < HEAD, rows[:half], rows[half:])


def mask_column(mask):
    return jnp.broadcast_to(mask[...].astype(F32), (8, mask.shape[1])).T[:, :1] > 0


def first_kernel(slots, info, mask, patches, specials, token, gain, shift, tokens, first):
    band = lax.axis_index("band")
    filled = jnp.where(mask_column(mask), line(token), patches[...].astype(F32))
    place_rows(tokens, filled, specials[...].astype(F32), band)
    hat, _ = normalize(tokens[...])
    counted = counted_rows(info, 0, tokens.shape[0], slots, tokens.shape[1])
    first[...] = jnp.where(counted, hat * line(gain) + line(shift), 0.0).astype(BF16)


def split_pairs(ref, rows, value):
    for pair in range(ref.shape[0]):
        ref[pair, rows, :] = value[:, pair * PAIR : (pair + 1) * PAIR].astype(BF16)


def project_keys(low, weight, value_bias, counted, keys, values, rows):
    width = weight.shape[0]
    split_pairs(keys, rows, dot(low, weight[:, width : 2 * width]))
    value = dot(low, weight[:, 2 * width :]) + line(value_bias)
    split_pairs(values, rows, jnp.where(counted, value, 0.0))


def attend_pair(queries, keys, values, ones):
    factor = HEAD ** (-0.5)
    stacked = stack_pair((queries.astype(F32) * factor).astype(BF16))
    low = jnp.exp(dot_nt(stacked, keys)).astype(BF16)
    summed = dot(low, jnp.concatenate([values, ones], axis=1))
    return low, unstack_pair(summed[:, :PAIR]), unstack_pair(summed[:, PAIR:])


def project_kernel(slots, info, first, weight, query_bias, value_bias, queries, keys, values):
    relative = pl.program_id(0)
    rows, width = first.shape
    counted = counted_rows(info, relative, rows, slots, width)
    low = first[...]

    @pl.when(relative == 0)
    def _():
        split_pairs(queries, slice(None), dot(low, weight[:, :width]) + line(query_bias))

    project_keys(low, weight, value_bias, counted, keys, values, slice(None))


def attend_kernel(
    slots, info, queries, keys, values, firsts, attended, totals, weights, firsts_t
):
    rows = queries.shape[1]
    ones = [
        counted_rows(info, r, rows, slots, PAIR).astype(F32).astype(BF16) for r in range(BANDS)
    ]
    low, summed, total = attend_pair(
        queries[0], keys[0], values[0], jnp.concatenate(ones, axis=0)
    )
    weights[0] = low
    firsts_t[...] = firsts[...].astype(F32).T.astype(BF16)
    attended[...] = summed / total
    totals[...] = total


def forward_kernel(
    slots,
    pairs,
    info,
    mask,
    patches,
    specials,
    token,
    gain,
    shift,
    query_bias,
    value_bias,
    weight_in,
    tokens_out,
    queries_out,
    keys_out,
    values_out,
    attended,
    totals,
    weights,
    firsts_t,
    tokens,
    firsts,
    queries,
    keys,
    values,
    ones,
    sums,
    counts,
    weight,
    send_sems,
    recv_sems,
    sems,
):
    step = pl.program_id(0)
    rows, width = tokens.shape
    half_rows = 2 * rows
    place = Place()
    sender = Sender(place, send_sems, recv_sems)
    sender.add("near", firsts.at[0], firsts.at[1], "core")
    sender.add("far", firsts.at[0], firsts.at[2], "x")
    sender.add("diagonal", firsts.at[2], firsts.at[3], "core")
    weight_load = lambda: pltpu.make_async_copy(weight_in, weight, sems.at[0])
    stores = lambda: [
        pltpu.make_async_copy(a, b, sems.at[i])
        for i, (a, b) in enumerate(
            ((tokens, tokens_out), (queries, queries_out), (keys, keys_out), (values, values_out)), 1
        )
    ]

    def block_keys(block):
        counted = counted_rows(info, block, rows, slots, width)
        span = pl.ds(block * rows, rows)
        project_keys(firsts[block], weight, value_bias, counted, keys, values, span)

    @pl.when(step == 0)
    def _():
        weight_load().start()
        filled = jnp.where(mask_column(mask), line(token), patches[...].astype(F32))
        place_rows(tokens, filled, specials[...].astype(F32), place.band)
        hat, _ = normalize(tokens[...])
        counted = counted_rows(info, 0, rows, slots, width)
        firsts[0] = jnp.where(counted, hat * line(gain) + line(shift), 0.0).astype(BF16)
        place.greet(("core", "x"))
        sender.send("near")
        sender.send("far")
        for block in range(BANDS):
            used = counted_rows(info, block, rows, slots, PAIR)
            ones[block * rows : (block + 1) * rows, :] = used.astype(F32).astype(BF16)
        weight_load().wait()
        split_pairs(queries, slice(None), dot(firsts[0], weight[:, :width]) + line(query_bias))
        block_keys(0)
        sender.arrived("near")
        block_keys(1)

    @pl.when(step == pairs)
    def _():
        sender.arrived("far")
        sender.send("diagonal")
        block_keys(2)
        sender.arrived("diagonal")
        block_keys(3)
        for copy in stores():
            copy.start()

    far_half = step >= pairs
    pair = jnp.where(far_half, step - pairs, step)
    first_row = pl.multiple_of(jnp.where(far_half, half_rows, 0), half_rows)
    span = pl.ds(first_row, half_rows)
    low, summed, total = attend_pair(
        queries[pair], keys[pair, span], values[pair, span], ones[span, :]
    )
    weights[0] = low
    first_block = jnp.where(far_half, 2, 0)
    lane = pl.ds(pl.multiple_of(pair * PAIR, PAIR), PAIR)
    columns = [firsts[first_block + i, :, lane] for i in range(2)]
    firsts_t[...] = jnp.concatenate(columns, axis=0).astype(F32).T.astype(BF16)

    @pl.when(step < pairs)
    def _():
        sums[pair] = summed
        counts[pair] = total

    @pl.when(far_half)
    def _():
        whole_total = counts[pair] + total
        attended[...] = (sums[pair] + summed) / whole_total
        totals[...] = whole_total

    @pl.when(step == 2 * pairs - 1)
    def _():
        sender.finish()
        for copy in stores():
            copy.wait()


def middle_kernel(
    slots,
    info,
    attended,
    tokens,
    weight,
    bias,
    first_scale,
    gain,
    shift,
    second_scale,
    cot_patches,
    cot_specials,
    branch,
    middle,
    second,
    incoming,
    down_in,
    down_keep,
    down_send,
    down_bias_grad,
):
    rows = tokens.shape[0]
    band = lax.axis_index("band")
    side = dot(attended[...].astype(BF16), weight[...]) + line(bias)
    branch[...] = side
    mid = tokens[...] + line(first_scale) * side
    middle[...] = mid
    hat, _ = normalize(mid)
    second[...] = (hat * line(gain) + line(shift)).astype(BF16)
    counted = counted_rows(info, 0, slots, slots, tokens.shape[1])
    given = jnp.where(counted, cot_patches[...].astype(F32), 0.0)
    place_rows(incoming, given, cot_specials[...].astype(F32), band)
    low = (incoming[...] * line(second_scale)).astype(BF16)
    down_in[...] = low
    keep, send = own_half(low, band)
    down_keep[...] = keep
    down_send[...] = send
    down_bias_grad[...] = column_sum(low.astype(F32))


def own_half(rows, band):
    half = rows.shape[1] // 2
    first = lax.rem(band, 2) == 0
    low, high = rows[:, :half], rows[:, half:]
    return jnp.where(first, low, high), jnp.where(first, high, low)


def gelu_and_slope(x):
    phi = 0.5 + 0.5 * lax.erf(x * 0.7071067811865476)
    density = jnp.exp(-0.5 * x * x) * 0.3989422804014327
    return x * phi, phi + x * density


def mlp_kernel(
    info,
    second,
    down_in,
    down_keep,
    down_send,
    up,
    up_bias,
    down,
    branch_two,
    second_grad,
    up_grad_keep,
    up_grad_send,
    up_bias_grad,
    down_grad_keep,
    down_grad_send,
):
    step = pl.program_id(0)
    low = second[...]
    hidden = dot(low, up[...]) + up_bias[...]
    active, slope = gelu_and_slope(hidden)
    active = active.astype(BF16)
    hidden_in = (slope * dot_nt(down_in[...], down[...])).astype(BF16)

    @pl.when(step == 0)
    def _():
        branch_two[...] = jnp.zeros_like(branch_two)
        second_grad[...] = jnp.zeros_like(second_grad)

    branch_two[...] += dot(active, down[...])
    second_grad[...] += dot_nt(hidden_in, up[...])
    keep, send = own_half(hidden_in, lax.axis_index("band"))
    up_grad_send[...] = dot_tn(low, send).astype(BF16)
    up_grad_keep[...] = dot_tn(low, keep).astype(BF16)
    down_grad_send[...] = dot_tn(active, down_send[...]).astype(BF16)
    down_grad_keep[...] = dot_tn(active, down_keep[...]).astype(BF16)
    up_bias_grad[...] = column_sum(hidden_in.astype(F32))


def middle_back_kernel(
    slots,
    info,
    middle,
    branch,
    branch_two,
    second_grad,
    incoming,
    attended,
    weight,
    down_bias,
    second_scale,
    gain,
    first_scale,
    out_patches,
    out_specials,
    middle_grad,
    attended_grad,
    out_keep,
    out_send,
    vectors,
    between=lambda part: None,
):
    mid = middle[...]
    given = incoming[...]
    two = branch_two[...] + line(down_bias)
    output = mid + line(second_scale) * two
    counted = counted_rows(info, 0, slots, slots, mid.shape[1])
    out_patches[...] = jnp.where(counted, output[:slots], 0.0).astype(BF16)
    out_specials[...] = output[slots:]
    hat, scale = normalize(mid)
    grad = second_grad[...]
    back = given + normalize_back(grad * line(gain), hat, scale)
    middle_grad[...] = back
    between(0)
    out_in = (back * line(first_scale)).astype(BF16)
    attended_grad[...] = dot_nt(out_in, weight[...])
    between(1)
    keep, send = own_half(out_in, lax.axis_index("band"))
    low = attended[...].astype(BF16)
    out_keep[...] = dot_tn(low, keep).astype(BF16)
    out_send[...] = dot_tn(low, send).astype(BF16)
    between(2)
    vectors[...] = jnp.concatenate(
        [
            column_sum(given * two),
            column_sum(grad * hat),
            column_sum(grad),
            column_sum(back * branch[...]),
            column_sum(out_in.astype(F32)),
            jnp.zeros((3, mid.shape[1]), F32),
        ],
        axis=0,
    )


def attend_back_pair(weights, queries, keys, values, attended, totals, attended_grad, outs):
    key_grad, value_grad = outs
    queries, keys, values = queries.at[0], keys.at[0], values.at[0]
    rows = queries.shape[0]
    factor = HEAD ** (-0.5)
    stacked = stack_pair((queries[...].astype(F32) * factor).astype(BF16))
    scaled = attended_grad[...] / totals[...]
    returned = stack_pair(scaled.astype(BF16))
    slope = jnp.sum(stack_pair(scaled * attended[...]), axis=1, keepdims=True)
    stacked_t = stacked.astype(F32).T.astype(BF16)
    returned_t = returned.astype(F32).T.astype(BF16)
    total = jnp.zeros((2 * rows, PAIR), F32)
    start = 0
    for size in key_parts(keys.shape[0]):
        span = slice(start, start + size)
        start += size
        low = weights[0, :, span]
        moved = dot_nt(returned, values[span, :])
        scores = (low.astype(F32) * (moved - slope)).astype(BF16)
        total = total + dot(scores, keys[span, :])
        key_grad[span, :] = dot(stacked_t, scores).T.astype(BF16)
        value_grad[span, :] = dot(returned_t, low).T.astype(BF16)
    return unstack_pair(total) * factor


def key_parts(count):
    parts = [KEY_PART] * (count // KEY_PART)
    if count % KEY_PART:
        parts[-1] += count % KEY_PART
    return parts


def first_part(block, rows, query_grad, key_grad, value_grad, weight):
    width = weight.shape[0]
    span = slice(block * rows, (block + 1) * rows)
    part = jnp.zeros((rows, width), F32)
    for pair in range(0, width // PAIR, 2):
        for offset, grad in ((width, key_grad), (2 * width, value_grad), (0, query_grad)):
            if offset == 0 and block > 0:
                continue
            at = slice(0, rows) if offset == 0 else span
            low = jnp.concatenate([grad[pair, at, :], grad[pair + 1, at, :]], axis=1)
            columns = slice(offset + pair * PAIR, offset + (pair + 2) * PAIR)
            part = part + dot_nt(low, weight[:, columns])
    return part


def own_pair_first(part, band):
    core = lax.rem(band, 2)
    return 2 * part + core, 2 * part + 1 - core


def joint_columns(firsts_t, query_grad, key_grad, value_grad, pairs):
    rows = query_grad.shape[1]
    queries = dot(firsts_t[:, :rows], jnp.concatenate([query_grad[p] for p in pairs], axis=1))
    results = []
    for index, p in enumerate(pairs):
        others = dot(firsts_t[...], jnp.concatenate([key_grad[p], value_grad[p]], axis=1))
        own = queries[:, index * PAIR : (index + 1) * PAIR]
        results.append(jnp.concatenate([own, others], axis=1).astype(BF16))
    return results


def first_back(slots, info, grad, tokens, middle_grad, mask, gain, patches, between=lambda part: None):
    rows, width = tokens.shape
    masked = mask_column(mask)
    counted = counted_rows(info, 0, rows, slots, width)
    sums = None
    for part, start in enumerate(range(0, rows, ROW_PART)):
        at = slice(start, start + ROW_PART)
        some = jnp.where(counted[at], grad[at], 0.0)
        hat, scale = normalize(tokens[at, :])
        token_grad = middle_grad[at, :] + normalize_back(some * line(gain), hat, scale)
        end = min(start + ROW_PART, slots)
        hidden = masked[start:end]
        patch_grad = token_grad[: end - start]
        patches[start:end, :] = jnp.where(hidden, 0.0, patch_grad).astype(BF16)
        terms = [
            column_sum(jnp.where(hidden, patch_grad, 0.0)),
            column_sum(some * hat),
            column_sum(some),
        ]
        sums = terms if sums is None else [x + y for x, y in zip(sums, terms)]
        between(part)
    return token_grad[slots - start :], sums


def bias_sums(info, slots, rows, query_grad, value_grad):
    ones = [
        counted_rows(info, block, rows, slots, PAIR).astype(F32).astype(BF16)
        for block in range(BANDS)
    ]
    ones = jnp.concatenate(ones, axis=0)
    pairs = range(query_grad.shape[0])
    queries = [column_sum(query_grad[pair].astype(F32)) for pair in pairs]
    values = [dot_tn(ones, value_grad[pair])[0:1] for pair in pairs]
    both = [jnp.concatenate(queries, axis=1), jnp.concatenate(values, axis=1)]
    return jnp.concatenate(both + [jnp.zeros((6, both[0].shape[1]), F32)], axis=0)


def swap(x, axis, distance):
    size = lax.axis_size(axis)
    return lax.ppermute(x, axis, [(i, i ^ distance) for i in range(size)])


def halve(x, axis, distance):
    bit = (lax.axis_index(axis) // distance) % 2
    sent = lax.dynamic_index_in_dim(x, 1 - bit, 0, keepdims=False)
    kept = lax.dynamic_index_in_dim(x, bit, 0, keepdims=False)
    got = swap(sent, axis, distance)
    return (kept.astype(F32) + got.astype(F32)).astype(BF16)


def reduce_half(kept, got, columns):
    held = (kept.astype(F32) + got.astype(F32)).astype(BF16)
    rows, half = held.shape
    crops = lax.axis_size("crop")
    held = held.reshape((crops, rows // crops, half))
    distance = 1
    while distance < crops:
        count = held.shape[0]
        held = jnp.moveaxis(held.reshape((count // 2, 2) + held.shape[1:]), 1, 0)
        held = halve(held, "crop", distance)
        distance *= 2
    held = held.reshape((rows // crops, half))
    other = swap(held, "band", 2)
    full = (held.astype(F32) + other.astype(F32)).astype(BF16)
    mate = swap(full, "band", 1)
    bit = lax.axis_index("band") % 2
    low = jnp.where(bit == 0, full, mate).astype(F32).reshape(rows // crops, -1, columns)
    high = jnp.where(bit == 0, mate, full).astype(F32).reshape(rows // crops, -1, columns)
    return jnp.stack([low, high], axis=2).reshape(rows // crops, 2 * half)


def gather_blocks(x):
    near = swap(x, "band", 1)
    far = swap(x, "band", 2)
    diagonal = swap(far, "band", 1)
    return jnp.concatenate([x, near, far, diagonal], axis=0)


def scatter_blocks(x):
    rows = x.shape[0] // BANDS
    got = swap(jnp.concatenate([x[rows : 2 * rows], x[3 * rows :]], axis=0), "band", 1)
    own = x[:rows].astype(F32) + got[:rows].astype(F32)
    far = (x[2 * rows : 3 * rows].astype(F32) + got[rows:].astype(F32)).astype(BF16)
    return own + swap(far, "band", 2).astype(F32)


def reduce_small(vectors, more, down_bias, up_bias, out_own, grad_own, special_count):
    crops = lax.axis_size("crop")
    width = vectors.shape[1]
    owned = -(-special_count // BANDS)
    both = jnp.concatenate([out_own[:owned], grad_own[:owned]], axis=1).astype(BF16)
    both = lax.all_gather(both, "band", axis=0, tiled=False)
    both = jnp.transpose(both, (1, 0, 2)).reshape(owned * BANDS, 2 * width)[:special_count]
    plain = jnp.concatenate([vectors[:5], more[:5], down_bias], axis=0)
    plain = jnp.transpose(plain.reshape(11, crops, -1), (1, 0, 2)).reshape(crops, -1)
    packed = jnp.concatenate([plain, up_bias.reshape(crops, -1)], axis=1)
    packed = lax.psum_scatter(packed, "crop", scatter_dimension=0, tiled=False)
    packed = lax.psum(packed, "band")
    part = width // crops
    rows = [packed[i * part : (i + 1) * part] for i in range(11)]
    return rows, packed[11 * part :], both[None, :, :width], both[None, :, width:]


def attend_back_kernel(
    weights, queries, keys, values, attended, totals, attended_grad, query_grad, key_grad, value_grad
):
    inputs = (weights, queries, keys, values, attended, totals, attended_grad)
    part = attend_back_pair(*inputs, (key_grad.at[0], value_grad.at[0]))
    query_grad[0] = part.astype(BF16)


def joint_back_kernel(
    slots, info, firsts_t, query_grad, key_grad, value_grad, weight, joint_keep, joint_send, first_grad, sums
):
    rows, width = query_grad.shape[1], weight.shape[0]
    for block in range(BANDS):
        part = first_part(block, rows, query_grad, key_grad, value_grad, weight)
        first_grad[block * rows : (block + 1) * rows, :] = part.astype(BF16)
    third = 3 * PAIR
    for part in range(query_grad.shape[0] // 2):
        keep, send = joint_columns(
            firsts_t, query_grad, key_grad, value_grad, own_pair_first(part, lax.axis_index("band"))
        )
        joint_keep[:, part * third : (part + 1) * third] = keep
        joint_send[:, part * third : (part + 1) * third] = send
    sums[...] = bias_sums(info, slots, rows, query_grad, value_grad)


def first_back_kernel(
    slots, info, first_grad, tokens, middle_grad, mask, gain, sums, patches, specials, vectors
):
    special_grad, rows = first_back(
        slots, info, first_grad[...], tokens, middle_grad, mask, gain, patches
    )
    specials[...] = special_grad
    vectors[...] = jnp.concatenate(rows + [sums[0:5]], axis=0)


def joint_order(x):
    rows, columns = x.shape
    x = x.reshape(rows, columns // (3 * PAIR), 3, PAIR)
    return jnp.transpose(x, (0, 2, 1, 3)).reshape(rows, columns)


def backward_general(given, slots, special_count):
    g = given
    rows, width = g["tokens"].shape
    every = BANDS * rows
    pairs = width // PAIR
    shaped = jax.ShapeDtypeStruct
    own_pair = pl.BlockSpec((rows, PAIR), lambda i: (0, i))
    grads = pl.pallas_call(
        attend_back_kernel,
        grid=(pairs,),
        out_shape=[
            shaped((pairs, rows, PAIR), BF16),
            shaped((pairs, every, PAIR), BF16),
            shaped((pairs, every, PAIR), BF16),
        ],
        in_specs=[
            pl.BlockSpec((1, 2 * rows, every), lambda i: (i, 0, 0)),
            pl.BlockSpec((1, rows, PAIR), lambda i: (i, 0, 0)),
            pl.BlockSpec((1, every, PAIR), lambda i: (i, 0, 0)),
            pl.BlockSpec((1, every, PAIR), lambda i: (i, 0, 0)),
            own_pair,
            own_pair,
            own_pair,
        ],
        out_specs=[
            pl.BlockSpec((1, rows, PAIR), lambda i: (i, 0, 0)),
            pl.BlockSpec((1, every, PAIR), lambda i: (i, 0, 0)),
            pl.BlockSpec((1, every, PAIR), lambda i: (i, 0, 0)),
        ],
        compiler_params=params(),
        name="attend_back",
    )(
        g["weights"],
        g["queries"],
        g["keys"],
        g["values"],
        g["attended"],
        g["totals"],
        g["attended_grad"],
    )
    half = width // 2
    joint_keep, joint_send, parts, sums = pl.pallas_call(
        partial(joint_back_kernel, slots),
        out_shape=[
            shaped((width, 3 * half), BF16),
            shaped((width, 3 * half), BF16),
            shaped((every, width), BF16),
            shaped((8, width), F32),
        ],
        in_specs=[SMEM] + [VMEM] * 5,
        out_specs=[VMEM] * 4,
        compiler_params=params(),
        name="joint_back",
    )(g["info"], g["firsts_t"], *grads, g["joint_weight"])
    grad_patches, grad_own, more = pl.pallas_call(
        partial(first_back_kernel, slots),
        out_shape=[
            shaped((slots, width), BF16),
            shaped((rows - slots, width), F32),
            shaped((8, width), F32),
        ],
        in_specs=[SMEM] + [VMEM] * 6,
        out_specs=[VMEM] * 3,
        compiler_params=params(),
        name="first_back",
    )(
        g["info"],
        scatter_blocks(parts),
        g["tokens"],
        g["middle_grad"],
        g["mask"],
        g["first_gain"],
        sums,
    )
    small = reduce_small(
        g["vectors"],
        more,
        g["down_bias_grad"],
        g["up_bias_grad"],
        g["out_own"],
        grad_own,
        special_count,
    )
    matrices = (
        reduce_half(g["mlp_grads"]["up_keep"], g["mlp_grads"]["up_got"], half),
        reduce_half(g["mlp_grads"]["down_keep"], g["mlp_grads"]["down_got"], half),
        reduce_half(g["out_keep"], swap(g["out_send"], "band", 1), half),
        joint_order(reduce_half(joint_keep, swap(joint_send, "band", 1), half)),
    )
    return (grad_patches,) + matrices + small


MESH = pl.DeviceIdType.MESH
CROPS = 8
X_FIRST = (1, 3, 5, 7, 11)
DIRECT = (11,)
NEIGHBOURS = ("core", "x", "diagonal")
PLACES = NEIGHBOURS + tuple(range(1, CROPS))


class Place:
    def __init__(self):
        band, crop = lax.axis_index("band"), lax.axis_index("crop")
        self.band = band
        self.core, self.x = lax.rem(band, 2), lax.div(band, 2)
        self.y, self.near, self.far = lax.rem(crop, 2), lax.rem(lax.div(crop, 2), 2), lax.div(crop, 4)
        core_step, x_step = 1 - 2 * self.core, 2 - 4 * self.x
        self.device = {
            "core": (band + core_step, crop),
            "x": (band + x_step, crop),
            "diagonal": (band + core_step + x_step, crop),
            "y": (band, crop + 1 - 2 * self.y),
            "near": (band, crop + 2 - 4 * self.near),
            "far": (band, crop + 4 - 8 * self.far),
        }
        self.crop = crop
        for step in range(1, CROPS):
            self.device[step] = (band, lax.rem(crop + step, CROPS))

    def greet(self, names):
        barrier = pltpu.get_barrier_semaphore()
        for name in names:
            pl.semaphore_signal(barrier, inc=1, device_id=self.device[name], device_id_type=MESH)
        pl.semaphore_wait(barrier, len(names))


class Sender:
    def __init__(self, place, send_sems, recv_sems):
        self.place, self.send_sems, self.recv_sems = place, send_sems, recv_sems
        self.routes = {}
        self.sent = []

    def add(self, key, source, target, name):
        self.routes[key] = (len(self.routes), source, target, name)

    def copy(self, key):
        index, source, target, name = self.routes[key]
        return pltpu.make_async_remote_copy(
            src_ref=source,
            dst_ref=target,
            send_sem=self.send_sems.at[index],
            recv_sem=self.recv_sems.at[index],
            device_id=self.place.device[name],
            device_id_type=MESH,
        )

    def send(self, key):
        self.copy(key).start()
        self.sent.append(key)

    def arrived(self, key):
        self.copy(key).wait_recv()

    def left(self, key):
        self.copy(key).wait_send()
        self.sent.remove(key)

    def finish(self):
        for key in self.sent:
            self.copy(key).wait_send()


def chunk_list(hidden_parts):
    chunks = []
    for part in range(hidden_parts):
        chunks += [("down", part), ("up", part)]
    return chunks + [("out", 0), ("joint", 0), ("joint", 1), ("joint", 2)]


def chunk_scratch(count, rows, columns):
    unit = (rows, columns)
    return [
        pltpu.VMEM((count, 2, 2, 2, 2) + unit, BF16),
        pltpu.VMEM((count, 2, 2, 2) + unit, BF16),
        pltpu.VMEM((count, 2, 2) + unit, BF16),
        pltpu.VMEM((count, 2) + unit, BF16),
        pltpu.VMEM((count, 3, 2) + unit, BF16),
    ]


class ChunkSums:
    def __init__(self, place, sender, buffers, total, count):
        p, self.sender, self.place, self.total = place, sender, place, total
        own, got_a, got_b, got_c, got_d = buffers
        self.got_d = got_d
        self.table = {}
        for n in range(count):
            both, half = total.at[n, p.core], total.at[n, p.core, p.x]
            if x_first(n):
                kept = [
                    own.at[n, p.x],
                    own.at[n, p.x, :, :, p.y],
                    own.at[n, p.x, :, p.near, p.y],
                    own.at[n, p.x, p.far, p.near, p.y],
                ]
                got = [got_a.at[n], got_b.at[n], got_c.at[n], got_d.at[n, 0, 0]]
                sent = [
                    own.at[n, 1 - p.x],
                    own.at[n, p.x, :, :, 1 - p.y],
                    own.at[n, p.x, :, 1 - p.near, p.y],
                    own.at[n, p.x, 1 - p.far, p.near, p.y],
                ]
                names = ("x", "y", "near", "far")
            else:
                kept = [
                    own.at[n, :, :, p.y],
                    own.at[n, :, p.near, p.y],
                    own.at[n, p.far, p.near, p.y],
                ]
                got = [got_a.at[n], got_b.at[n], got_c.at[n]]
                sent = [
                    own.at[n, :, :, 1 - p.y],
                    own.at[n, :, 1 - p.near, p.y],
                    own.at[n, 1 - p.far, p.near, p.y],
                ]
                names = ("y", "near", "far")
            rows = [(None, None, None, [(sent[0], got[0], names[0])])]
            for i in range(1, len(names)):
                add = (kept[i - 1], kept[i - 1], got[i - 1])
                rows.append(add + ([(sent[i], got[i], names[i])],))
            end = (kept[-1], got[-1])
            if direct(n):
                targets = [half] * 3 if x_first(n) else [got_d.at[n, i] for i in range(3)]
                last = half if x_first(n) else both
                rows.append((last,) + end + ([(last, t, m) for t, m in zip(targets, NEIGHBOURS)],))
            elif x_first(n):
                rows.append((half,) + end + ([(half, half, "x")],))
                rows.append((None, None, None, [(both, both, "core")]))
            else:
                rows.append((kept[-1],) + end + ([(kept[-1], got_d.at[n, 0], "x")],))
                rows.append((both, kept[-1], got_d.at[n, 0], [(both, both, "core")]))
            self.table[n] = rows
            for stage, row in enumerate(rows):
                for i, (source, target, name) in enumerate(row[3]):
                    sender.add((n, stage + 1, i), source, target, name)

    def steps(self, n):
        return len(self.table[n]) + 1

    def step(self, n, stage):
        rows, sender = self.table[n], self.sender
        if stage > 0:
            for i in range(len(rows[stage - 1][3])):
                sender.arrived((n, stage, i))
        if stage == len(rows):
            if direct(n) and not x_first(n):
                for i in range(3):
                    sender.left((n, stage, i))
                p, total, got = self.place, self.total, self.got_d
                total[n, p.core] = total[n, p.core] + got[n, 1]
                total[n, 1 - p.core] = got[n, 0] + got[n, 2]
            return
        into, kept, got, sent = rows[stage]
        if into is not None:
            into[...] = kept[...] + got[...]
        for i in range(len(sent)):
            sender.send((n, stage + 1, i))


class VectorSums:
    def __init__(self, place, sender, buffers, total):
        self.place, self.sender, self.total = place, sender, total
        self.own, self.got, self.parts = buffers
        for step in range(1, CROPS):
            source = self.own.at[lax.rem(place.crop + step, CROPS)]
            sender.add(("vector", step), source, self.got.at[place.crop], step)
        here = self.parts.at[place.band]
        for name in NEIGHBOURS:
            sender.add(("parts", name), here, here, name)

    def spread(self):
        for step in range(1, CROPS):
            self.sender.send(("vector", step))

    def share(self):
        p = self.place
        self.got[p.crop] = self.own[p.crop]
        for step in range(1, CROPS):
            self.sender.arrived(("vector", step))
        self.parts[p.band] = jnp.sum(self.got[...], axis=0)
        for name in NEIGHBOURS:
            self.sender.send(("parts", name))

    def close(self):
        for name in NEIGHBOURS:
            self.sender.arrived(("parts", name))
        self.total[...] = jnp.sum(self.parts[...], axis=0)


def pack_vectors(own, rows, up_bias, part):
    for crop in range(CROPS):
        span = slice(crop * part, (crop + 1) * part)
        wide = 4 * crop * part
        wider = [up_bias[0:1, wide + j * part : wide + (j + 1) * part] for j in range(4)]
        own[crop, 0:15, 0:part] = jnp.concatenate([rows[:, span]] + wider, axis=0)


def vector_scratch():
    return [
        pltpu.VMEM((CROPS, 16, 128), F32),
        pltpu.VMEM((CROPS, 16, 128), F32),
        pltpu.VMEM((BANDS, 16, 128), F32),
    ]


def x_first(n):
    return n in X_FIRST


def direct(n):
    return n in DIRECT


def halves_of(n):
    return (0, 1) if x_first(n) else (None,)


def part_of(ref, name, part, columns, x_half):
    at = slice(None) if x_half is None else x_half
    if name == "down":
        return ref.at[:, :, :, part, at]
    return ref.at[:, :, :, at, :, pl.ds(part * columns, columns)]


def piece(ref, x_half):
    return ref if x_half is None else ref.at[x_half]


def middle_all_kernel(
    chunks,
    slots,
    parts,
    info,
    attended,
    tokens,
    out_weight,
    out_bias,
    first_scale,
    gain,
    shift,
    second_scale,
    cot_patches,
    cot_specials,
    down_bias,
    up,
    up_bias,
    down,
    out_patches,
    out_specials,
    middle_grad,
    attended_grad,
    out_keep,
    out_send,
    vectors,
    down_bias_grad,
    up_bias_grad,
    kept_out,
    sent_out,
    *scratch,
):
    (
        kept,
        sent,
        branch,
        middle,
        second,
        second_t,
        incoming,
        down_in,
        down_keep,
        down_send,
        branch_two,
        second_grad,
        active_t,
        store_sems,
    ) = scratch
    step = pl.program_id(0)
    width = tokens.shape[1]
    count = kept.shape[0]
    band = lax.axis_index("band")

    def stores(n):
        return [
            pltpu.make_async_copy(kept.at[n], kept_out.at[n], store_sems.at[0, n]),
            pltpu.make_async_copy(sent.at[n], sent_out.at[n], store_sems.at[1, n]),
        ]

    def made(n, value, x_halves):
        shape = (2, 2, 2, 2, width // CROPS // 2, width // 2)
        for half, target in zip(own_half(value, band), (kept.at[n], sent.at[n])):
            half = half.reshape(shape)
            if x_halves:
                for h in range(2):
                    target[h] = half[:, :, :, h]
            else:
                target[...] = half
        for copy in stores(n):
            copy.start()

    @pl.when(step == 0)
    def _():
        middle_kernel(
            slots,
            info,
            attended,
            tokens,
            out_weight,
            out_bias,
            first_scale,
            gain,
            shift,
            second_scale,
            cot_patches,
            cot_specials,
            branch,
            middle,
            second,
            incoming,
            down_in,
            down_keep,
            down_send,
            down_bias_grad,
        )
        second_t[...] = second[...].astype(F32).T.astype(BF16)
        branch_two[...] = jnp.zeros_like(branch_two)
        second_grad[...] = jnp.zeros_like(second_grad)

    @pl.when(step < parts)
    def _():
        hidden = dot(second[...], up[...]) + up_bias[...]
        active, slope = gelu_and_slope(hidden)
        active = active.astype(BF16)
        span = pl.ds(pl.multiple_of(step * width, width), width)
        active_t[span, :] = active.astype(F32).T.astype(BF16)
        hidden_in = (slope * dot_nt(down_in[...], down[...])).astype(BF16)
        made(2 * step + 1, dot(second_t[...], hidden_in).astype(BF16), True)
        branch_two[...] += dot(active, down[...])
        second_grad[...] += dot_nt(hidden_in, up[...])
        up_bias_grad[...] = column_sum(hidden_in.astype(F32))

    @pl.when((step >= parts) & (step < 2 * parts))
    def _():
        part = step - parts
        own_rows = width // CROPS
        starts = [
            pl.multiple_of((crop * parts + part) * own_rows, own_rows) for crop in range(CROPS)
        ]
        rows = jnp.concatenate([active_t[pl.ds(i, own_rows), :] for i in starts], axis=0)
        made(2 * part, dot(rows, down_in[...]).astype(BF16), False)

    @pl.when(step == 2 * parts)
    def _():
        middle_back_kernel(
            slots,
            info,
            middle,
            branch,
            branch_two,
            second_grad,
            incoming,
            attended,
            out_weight,
            down_bias,
            second_scale,
            gain,
            first_scale,
            out_patches,
            out_specials,
            middle_grad,
            attended_grad,
            out_keep,
            out_send,
            vectors,
        )
        for n in range(count):
            for copy in stores(n):
                copy.wait()


def middle_fused(
    info,
    attended,
    tokens,
    out_weight,
    out_bias,
    first_scale,
    second_gain,
    second_shift,
    second_scale,
    cot_patches,
    cot_specials,
    down_bias,
    up_weight,
    up_bias,
    down_weight,
):
    rows, width = tokens.shape
    slots = cot_patches.shape[0]
    hidden_width = up_weight.shape[1]
    parts = hidden_width // width
    chunks = chunk_list(parts)
    count = 2 * parts
    unit_rows, half = width // CROPS // 2, width // 2
    unit = (2, 2, 2, 2, unit_rows, half)
    shaped = jax.ShapeDtypeStruct
    last = parts - 1
    outs = pl.pallas_call(
        partial(middle_all_kernel, chunks, slots, parts),
        grid=(2 * parts + 1,),
        out_shape=[
            shaped((slots, width), BF16),
            shaped((rows - slots, width), F32),
            shaped((rows, width), F32),
            shaped((rows, width), F32),
            shaped((width, half), BF16),
            shaped((width, half), BF16),
            shaped((8, width), F32),
            shaped((1, width), F32),
            shaped((1, hidden_width), F32),
            shaped((count,) + unit, BF16),
            shaped((count,) + unit, BF16),
        ],
        in_specs=[SMEM]
        + [VMEM] * 11
        + [
            pl.BlockSpec((width, width), lambda i: (0, jnp.minimum(i, last))),
            pl.BlockSpec((1, width), lambda i: (0, jnp.minimum(i, last))),
            pl.BlockSpec((width, width), lambda i: (jnp.minimum(i, last), 0)),
        ],
        out_specs=[VMEM] * 8 + [pl.BlockSpec((1, width), lambda i: (0, jnp.minimum(i, last))), ANY, ANY],
        scratch_shapes=[
            pltpu.VMEM((count,) + unit, BF16),
            pltpu.VMEM((count,) + unit, BF16),
            pltpu.VMEM((rows, width), F32),
            pltpu.VMEM((rows, width), F32),
            pltpu.VMEM((rows, width), BF16),
            pltpu.VMEM((width, rows), BF16),
            pltpu.VMEM((rows, width), F32),
            pltpu.VMEM((rows, width), BF16),
            pltpu.VMEM((rows, half), BF16),
            pltpu.VMEM((rows, half), BF16),
            pltpu.VMEM((rows, width), F32),
            pltpu.VMEM((rows, width), F32),
            pltpu.VMEM((hidden_width, rows), BF16),
            pltpu.SemaphoreType.DMA((2, count)),
        ],
        compiler_params=params(),
        name="middle_all",
    )(
        info,
        attended,
        tokens,
        out_weight,
        out_bias,
        first_scale,
        second_gain,
        second_shift,
        second_scale,
        cot_patches,
        cot_specials,
        down_bias,
        up_weight,
        up_bias,
        down_weight,
    )
    return tuple(outs[:9]) + (outs[9:],)


PLAN = (
    (0, 1, 0), (0, 0, 0), (1, 3, 0), (1, 2, 0), (1, 5, 0), (1, 4, 0),
    (3, 7, 0), (3, 6, 0), (3, 1, 1), (3, 0, 1), (5, 0, 2), (6, 8, 0),
    (6, 3, 1), (6, 2, 1), (6, 0, 3), (7, 5, 1), (7, 4, 1), (8, 2, 2),
    (8, 7, 1), (8, 9, 0), (8, 6, 1), (8, 4, 2), (9, 0, 4), (9, 1, 2),
    (10, 2, 3), (10, 0, 5), (10, 6, 2), (10, 4, 3), (10, 10, 0), (11, 1, 3),
    (11, 8, 1), (12, 3, 2), (12, 6, 3), (13, 1, 4), (14, 5, 2), (14, 11, 0),
    (14, 8, 2), (14, 2, 4), (15, 3, 3), (16, 7, 2), (16, 4, 4), (17, 5, 3),
    (17, 2, 5), (17, 6, 4), (17, 1, 5), (18, 8, 3), (18, 4, 5), (19, 3, 4),
    (19, 6, 5), (19, 7, 3), (19, 1, 6), (20, 9, 1), (20, 5, 4), (22, 7, 4),
    (22, 11, 1), (23, 8, 4), (24, 3, 5), (25, 9, 2), (26, 5, 5), (27, 10, 1),
    (28, 7, 5), (29, 8, 5), (30, 3, 6), (31, 5, 6), (32, 7, 6), (33, 11, 2),
    (34, 9, 3), (35, 10, 2), (36, 9, 4), (37, 11, 3), (38, 9, 5), (39, 10, 3),
    (40, 11, 4), (41, 10, 4), (42, 11, 5), (43, 10, 5),
)


def backward_kernel(
    chunks,
    slots,
    pairs,
    info,
    weights,
    queries,
    keys,
    values,
    attended,
    totals,
    attended_grad,
    mask,
    gain,
    vectors,
    down_bias,
    up_bias,
    out_own,
    kept_in,
    sent_in,
    out_keep,
    out_send,
    firsts_in,
    weight_in,
    tokens_in,
    middle_grad_in,
    grad_patches,
    total_out,
    vector_total,
    specials_out,
    *scratch,
):
    buffers, vector_buffers = scratch[:5], scratch[5:8]
    (
        total,
        got,
        out_got,
        joint_got,
        joint_sent,
        query_sum,
        query_grad,
        key_grad,
        value_grad,
        firsts_t,
        weight,
        tokens,
        middle_grad,
        parts,
        got_parts,
        got_far,
        specials,
        send_sems,
        recv_sems,
        load_sems,
        whole_sems,
    ) = scratch[8:]
    step = pl.program_id(0)
    count = len(chunks)
    columns = total.shape[4]
    rows, width = tokens.shape
    place = Place()
    sender = Sender(place, send_sems, recv_sems)
    sums = ChunkSums(place, sender, buffers, total, count)
    vector_sums = VectorSums(place, sender, vector_buffers, vector_total)
    own = buffers[0]
    passed = kept_in.shape[0]

    def own_loads(n):
        if n < passed:
            return [pltpu.make_async_copy(kept_in.at[n], own.at[n], load_sems.at[n, 0])]
        return [
            pltpu.make_async_copy(
                part_of(out_keep, "out", 0, columns, h), piece(own.at[n], h), load_sems.at[n, i]
            )
            for i, h in enumerate(halves_of(n))
        ]

    def whole_loads():
        pairs_of = ((weight_in, weight), (firsts_in, firsts_t), (tokens_in, tokens), (middle_grad_in, middle_grad))
        return [
            pltpu.make_async_copy(a, b, whole_sems.at[i]) for i, (a, b) in enumerate(pairs_of)
        ]

    early = [n for n, (name, _) in enumerate(chunks) if name != "joint"]
    out_chunk = early[-1]
    late = [n for n, (name, _) in enumerate(chunks) if name == "joint"]

    for n in range(passed):
        sender.add((n, 0), sent_in.at[n], got.at[n], "core")
    for h in halves_of(out_chunk):
        source = part_of(out_send, "out", 0, columns, h)
        sender.add((out_chunk, 0, h), source, piece(out_got, h), "core")
    for n in late:
        sender.add((n, 0), joint_sent.at[n - late[0]], joint_got.at[n - late[0]], "core")
    for index in range(2):
        sender.add(("first", index), parts.at[index], got_parts.at[index], "core")
    sender.add("far", parts.at[2], got_far, "x")
    for name in NEIGHBOURS:
        sender.add(("special", name), specials.at[place.band], specials.at[place.band], name)

    def begin():
        for n in early:
            for copy in own_loads(n):
                copy.start()
        place.greet(PLACES)
        for _, n, stage in PLAN:
            if stage == 0 and n < passed:
                sender.send((n, 0))
        for h in halves_of(out_chunk):
            sender.send((out_chunk, 0, h))

    def early_stage(n, stage):
        if stage == 0:
            for copy in own_loads(n):
                copy.wait()
            if n == out_chunk:
                for h in halves_of(n):
                    sender.arrived((n, 0, h))
                own[n] = own[n] + out_got[...]
            else:
                sender.arrived((n, 0))
                own[n] = own[n] + got[n]
        sums.step(n, stage)

    def late_stage(n, stage):
        if stage == 0:
            sender.arrived((n, 0))
            own[n] = own[n] + joint_got[n - late[0]]
        sums.step(n, stage)

    def stage_of(n, stage):
        (late_stage if n in late else early_stage)(n, stage)

    def exchanges(slot):
        for place_of, n, stage in PLAN:
            if place_of == slot:
                stage_of(n, stage)

    def occupied(slot):
        return any(place_of == slot for place_of, _, _ in PLAN)

    def joint_chunk(part):
        n = late[part]
        picked = joint_columns(firsts_t, *grads, own_pair_first(part, place.band))
        shape = (2, 2, 2, 2, width // CROPS // 2, columns)
        for value, target in zip(picked, (own.at[n], joint_sent.at[part])):
            value = value.reshape(shape)
            for h in halves_of(n):
                if h is None:
                    target[...] = value
                else:
                    target[h] = value[:, :, :, h]
        sender.send((n, 0))

    half_rows = 2 * rows
    per_step = 1

    def between(index):
        for i in range(2 * pairs):
            if occupied(i):

                @pl.when(index == i)
                def _():
                    exchanges(i)

    grads = (query_grad, key_grad, value_grad)
    last = 2 * pairs
    after = last * per_step

    @pl.when(step == 0)
    def _():
        begin()

    @pl.when(step == 1)
    def _():
        for copy in whole_loads():
            copy.start()

    @pl.when(step == pairs)
    def _():
        for copy in whole_loads():
            copy.wait()
        parts[1] = first_part(3, rows, *grads, weight).astype(BF16)
        sender.send(("first", 1))
        parts[2] = first_part(2, rows, *grads, weight).astype(BF16)

    @pl.when(step == pairs + 1)
    def _():
        sender.arrived(("first", 1))
        parts[2] = parts[2] + got_parts[1]
        sender.send("far")

    for part in range(2):

        @pl.when(step == pairs + 2 * part + 2)
        def _():
            joint_chunk(part)

    @pl.when(step < last)
    def _():
        far_half = step < pairs
        pair = jnp.where(far_half, step, jnp.minimum(step - pairs, pairs - 1))
        first_row = pl.multiple_of(jnp.where(far_half, half_rows, 0), half_rows)
        span = pl.ds(first_row, half_rows)
        outs = (key_grad.at[pair, span], value_grad.at[pair, span])
        inputs = (weights, queries, keys, values, attended, totals, attended_grad)
        part = attend_back_pair(*inputs, outs)
        between(step)

        @pl.when(far_half)
        def _():
            query_sum[pair] = part

        @pl.when(step >= pairs)
        def _():
            query_grad[pair] = (query_sum[pair] + part).astype(BF16)

    @pl.when(step == last)
    def _():
        joint_chunk(2)
        exchanges(after)
        parts[0] = first_part(1, rows, *grads, weight).astype(BF16)
        sender.send(("first", 0))
        exchanges(after + 1)
        first_grad = first_part(0, rows, *grads, weight)
        exchanges(after + 2)
        biases = bias_sums(info, slots, rows, query_grad, value_grad)
        exchanges(after + 3)
        sender.arrived(("first", 0))
        sender.arrived("far")
        first_grad = first_grad + got_parts[0].astype(F32) + got_far[...].astype(F32)
        special_grad, rows_of = first_back(
            slots,
            info,
            first_grad,
            tokens,
            middle_grad,
            mask,
            gain,
            grad_patches,
            lambda part: exchanges(after + 4 + part),
        )
        specials[place.band] = jnp.concatenate([out_own[0:4], special_grad[0:4]], axis=0)
        for name in NEIGHBOURS:
            sender.send(("special", name))
        packed = jnp.concatenate([vectors[0:5]] + rows_of + [biases[0:2], down_bias[...]], axis=0)
        pack_vectors(vector_sums.own, packed, up_bias, width // CROPS)
        vector_sums.spread()
        ends = max(entry[0] for entry in PLAN) + 1
        start = after + 4 + rows // ROW_PART
        shared = min(start + 5, ends - 1)
        closed = min(start + 12, ends - 1)
        for slot in range(start, ends):
            exchanges(slot)
            if slot == shared:
                vector_sums.share()
            if slot == closed:
                vector_sums.close()
        for name in NEIGHBOURS:
            sender.arrived(("special", name))
        specials_out[...] = specials[...]
        sender.finish()
        copy = pltpu.make_async_copy(total, total_out, whole_sems.at[4])
        copy.start()
        copy.wait()


def finish_kernel(
    chunks,
    special_count,
    total,
    vector_total,
    specials,
    grad_patches,
    up,
    down,
    out,
    joint,
    up_bias,
    out_specials,
    grad_specials,
    grad_patches_out,
    *vectors,
):
    grad_patches_out[...] = grad_patches[...]
    _, _, _, rows, columns = total.shape
    refs = dict(up=up, down=down, out=out, joint=joint)
    for n, (name, part) in enumerate(chunks):
        for core in range(2):
            for x in range(2):
                row, column = x * rows, core * columns
                if name == "down":
                    row += 2 * rows * part
                else:
                    column += 2 * columns * part
                value = total[n, core, x].astype(F32)
                if name == "joint":
                    for third in range(3):
                        column = third * 2 * columns + (2 * part + core) * PAIR
                        piece_of = value[:, third * PAIR : (third + 1) * PAIR]
                        joint[row : row + rows, column : column + PAIR] = piece_of
                    continue
                refs[name][row : row + rows, column : column + columns] = value
    part = vectors[0].shape[0]
    for i, vector in enumerate(vectors):
        vector[...] = vector_total[i, 0:part]
    up_bias[...] = jnp.concatenate([vector_total[i : i + 1, 0:part] for i in range(11, 15)], axis=1)[0]
    for first, target in ((0, out_specials), (4, grad_specials)):
        picked = [
            specials[s % BANDS, first + s // BANDS : first + s // BANDS + 1]
            for s in range(special_count)
        ]
        target[0] = jnp.concatenate(picked, axis=0).astype(BF16)


def backward_fused(given, slots, special_count):
    g = given
    rows, width = g["tokens"].shape
    hidden_width = g["up_bias_grad"].shape[1]
    every = BANDS * rows
    pairs = width // PAIR
    chunks = chunk_list(hidden_width // width)
    count = len(chunks)
    part = width // CROPS
    unit_rows, columns = part // 2, width // 2
    unit = (2, 2, 2, 2, unit_rows, columns)
    hidden_parts = hidden_width // width
    shaped = jax.ShapeDtypeStruct
    last = 2 * pairs - 1
    far_first = lambda i: 1 - jnp.minimum(i, last) // pairs
    pair_of = lambda i: jnp.minimum(i, last) % pairs
    own_pair = pl.BlockSpec((rows, PAIR), lambda i: (0, pair_of(i)))
    own_heads = pl.BlockSpec((1, rows, PAIR), lambda i: (pair_of(i), 0, 0))
    half_heads = pl.BlockSpec((1, 2 * rows, PAIR), lambda i: (pair_of(i), far_first(i), 0))
    kept = pl.BlockSpec((1, 2 * rows, 2 * rows), lambda i: (pair_of(i), 0, far_first(i)))
    grad_patches, total, vector_total, specials = pl.pallas_call(
        partial(backward_kernel, chunks, slots, pairs),
        grid=(2 * pairs + 1,),
        out_shape=[
            shaped((slots, width), BF16),
            shaped((count, 2, 2, unit_rows, columns), BF16),
            shaped((16, 128), F32),
            shaped((BANDS, 8, width), F32),
        ],
        in_specs=[SMEM, kept, own_heads, half_heads, half_heads, own_pair, own_pair, own_pair]
        + [VMEM] * 6
        + [ANY] * 8,
        out_specs=[VMEM, ANY, VMEM, VMEM],
        scratch_shapes=chunk_scratch(count, unit_rows, columns)
        + vector_scratch()
        + [
            pltpu.VMEM((count, 2, 2, unit_rows, columns), BF16),
            pltpu.VMEM((2 * hidden_parts,) + unit, BF16),
            pltpu.VMEM(unit, BF16),
            pltpu.VMEM((3,) + unit, BF16),
            pltpu.VMEM((3,) + unit, BF16),
            pltpu.VMEM((pairs, rows, PAIR), F32),
            pltpu.VMEM((pairs, rows, PAIR), BF16),
            pltpu.VMEM((pairs, every, PAIR), BF16),
            pltpu.VMEM((pairs, every, PAIR), BF16),
            pltpu.VMEM((width, every), BF16),
            pltpu.VMEM((width, 3 * width), BF16),
            pltpu.VMEM((rows, width), F32),
            pltpu.VMEM((rows, width), F32),
            pltpu.VMEM((3, rows, width), BF16),
            pltpu.VMEM((2, rows, width), BF16),
            pltpu.VMEM((rows, width), BF16),
            pltpu.VMEM((BANDS, 8, width), F32),
            pltpu.SemaphoreType.DMA((10 * count,)),
            pltpu.SemaphoreType.DMA((10 * count,)),
            pltpu.SemaphoreType.DMA((count, 2)),
            pltpu.SemaphoreType.DMA((5,)),
        ],
        compiler_params=pltpu.CompilerParams(
            vmem_limit_bytes=VMEM_LIMIT, collective_id=0, has_side_effects=True
        ),
        name="backward",
    )(
        g["info"],
        g["weights"],
        g["queries"],
        g["keys"],
        g["values"],
        g["attended"],
        g["totals"],
        g["attended_grad"],
        g["mask"],
        g["first_gain"],
        g["vectors"],
        g["down_bias_grad"],
        g["up_bias_grad"],
        g["out_own"],
        *g["mlp_grads"],
        g["out_keep"].reshape(unit),
        g["out_send"].reshape(unit),
        g["firsts_t"],
        g["joint_weight"],
        g["tokens"],
        g["middle_grad"],
    )
    special = shaped((1, special_count, width), BF16)
    results = pl.pallas_call(
        partial(finish_kernel, chunks, special_count),
        out_shape=[
            shaped((part, hidden_width), F32),
            shaped((hidden_width // CROPS, width), F32),
            shaped((part, width), F32),
            shaped((part, 3 * width), F32),
            shaped((hidden_width // CROPS,), F32),
            special,
            special,
            shaped((slots, width), BF16),
        ]
        + [shaped((part,), F32)] * 11,
        in_specs=[VMEM] * 4,
        out_specs=[VMEM] * 19,
        compiler_params=params(),
        name="finish",
    )(total, vector_total, specials, grad_patches)
    up, down, out, joint, up_bias, out_specials, grad_specials, grad_patches = results[:8]
    return grad_patches, up, down, out, joint, results[8:], up_bias, out_specials, grad_specials


def forward_fused(
    info, mask, patches, specials, token, gain, shift, weight, query_bias, value_bias, rows
):
    slots, width = patches.shape
    every, pairs = BANDS * rows, width // PAIR
    shaped = jax.ShapeDtypeStruct
    half_of = lambda i: i // pairs
    pair_of = lambda i: i % pairs
    final_pair = pl.BlockSpec((rows, PAIR), lambda i: (0, jnp.maximum(i - pairs, 0)))
    outs = pl.pallas_call(
        partial(forward_kernel, slots, pairs),
        grid=(2 * pairs,),
        out_shape=[
            shaped((rows, width), F32),
            shaped((pairs, rows, PAIR), BF16),
            shaped((pairs, every, PAIR), BF16),
            shaped((pairs, every, PAIR), BF16),
            shaped((rows, width), F32),
            shaped((rows, width), F32),
            shaped((pairs, 2 * rows, every), BF16),
            shaped((width, every), BF16),
        ],
        in_specs=[SMEM] + [VMEM] * 8 + [ANY],
        out_specs=[
            ANY,
            ANY,
            ANY,
            ANY,
            final_pair,
            final_pair,
            pl.BlockSpec((1, 2 * rows, 2 * rows), lambda i: (pair_of(i), 0, half_of(i))),
            pl.BlockSpec((PAIR, 2 * rows), lambda i: (pair_of(i), half_of(i))),
        ],
        scratch_shapes=[
            pltpu.VMEM((rows, width), F32),
            pltpu.VMEM((BANDS, rows, width), BF16),
            pltpu.VMEM((pairs, rows, PAIR), BF16),
            pltpu.VMEM((pairs, every, PAIR), BF16),
            pltpu.VMEM((pairs, every, PAIR), BF16),
            pltpu.VMEM((every, PAIR), BF16),
            pltpu.VMEM((pairs, rows, PAIR), F32),
            pltpu.VMEM((pairs, rows, PAIR), F32),
            pltpu.VMEM((width, 3 * width), BF16),
            pltpu.SemaphoreType.DMA((3,)),
            pltpu.SemaphoreType.DMA((3,)),
            pltpu.SemaphoreType.DMA((5,)),
        ],
        compiler_params=pltpu.CompilerParams(
            vmem_limit_bytes=VMEM_LIMIT, collective_id=1, has_side_effects=True
        ),
        name="forward",
    )(info, mask, patches, specials, token, gain, shift, query_bias, value_bias, weight)
    return outs


def forward_general(
    info, mask, patches, specials, token, gain, shift, weight, query_bias, value_bias, rows
):
    slots, width = patches.shape
    every, pairs = BANDS * rows, width // PAIR
    shaped = jax.ShapeDtypeStruct
    tokens, first = pl.pallas_call(
        partial(first_kernel, slots),
        out_shape=[shaped((rows, width), F32), shaped((rows, width), BF16)],
        in_specs=[SMEM] + [VMEM] * 6,
        compiler_params=params(),
        name="first",
    )(info, mask, patches, specials, token, gain, shift)
    firsts = gather_blocks(first)
    block = pl.BlockSpec((rows, width), lambda i: (i, 0))
    pair_block = pl.BlockSpec((pairs, rows, PAIR), lambda i: (0, i, 0))
    queries, keys, values = pl.pallas_call(
        partial(project_kernel, slots),
        grid=(BANDS,),
        out_shape=[
            shaped((pairs, rows, PAIR), BF16),
            shaped((pairs, every, PAIR), BF16),
            shaped((pairs, every, PAIR), BF16),
        ],
        in_specs=[SMEM, block, whole((width, 3 * width)), VMEM, VMEM],
        out_specs=[whole((pairs, rows, PAIR)), pair_block, pair_block],
        compiler_params=params(),
        name="project",
    )(info, firsts, weight, query_bias, value_bias)
    own_pair = pl.BlockSpec((rows, PAIR), lambda i: (0, i))
    all_pair = pl.BlockSpec((every, PAIR), lambda i: (0, i))
    own_heads = pl.BlockSpec((1, rows, PAIR), lambda i: (i, 0, 0))
    all_heads = pl.BlockSpec((1, every, PAIR), lambda i: (i, 0, 0))
    attended, totals, weights, firsts_t = pl.pallas_call(
        partial(attend_kernel, slots),
        grid=(pairs,),
        out_shape=[
            shaped((rows, width), F32),
            shaped((rows, width), F32),
            shaped((pairs, 2 * rows, every), BF16),
            shaped((width, every), BF16),
        ],
        in_specs=[SMEM, own_heads, all_heads, all_heads, all_pair],
        out_specs=[
            own_pair,
            own_pair,
            pl.BlockSpec((1, 2 * rows, every), lambda i: (i, 0, 0)),
            pl.BlockSpec((PAIR, every), lambda i: (i, 0)),
        ],
        compiler_params=params(),
        name="attend",
    )(info, queries, keys, values, firsts)
    return tokens, queries, keys, values, attended, totals, weights, firsts_t


def middle_general(
    info,
    attended,
    tokens,
    out_weight,
    out_bias,
    first_scale,
    second_gain,
    second_shift,
    second_scale,
    cot_patches,
    cot_specials,
    down_bias,
    up_weight,
    up_bias,
    down_weight,
):
    rows, width = tokens.shape
    slots = cot_patches.shape[0]
    hidden_width = up_weight.shape[1]
    pad = rows - slots
    shaped = jax.ShapeDtypeStruct
    branch, middle, second, incoming, down_in, down_keep, down_send, down_bias_grad = pl.pallas_call(
        partial(middle_kernel, slots),
        out_shape=[
            shaped((rows, width), F32),
            shaped((rows, width), F32),
            shaped((rows, width), BF16),
            shaped((rows, width), F32),
            shaped((rows, width), BF16),
            shaped((rows, width // 2), BF16),
            shaped((rows, width // 2), BF16),
            shaped((1, width), F32),
        ],
        in_specs=[SMEM] + [VMEM] * 10,
        out_specs=[VMEM] * 8,
        compiler_params=params(),
        name="middle",
    )(
        info,
        attended,
        tokens,
        out_weight,
        out_bias,
        first_scale,
        second_gain,
        second_shift,
        second_scale,
        cot_patches,
        cot_specials,
    )

    steps = hidden_width // width
    half = width // 2
    (
        branch_two,
        second_grad,
        up_keep,
        up_send,
        up_bias_grad,
        down_grad_keep,
        down_grad_send,
    ) = pl.pallas_call(
        mlp_kernel,
        grid=(steps,),
        out_shape=[
            shaped((rows, width), F32),
            shaped((rows, width), F32),
            shaped((width, hidden_width // 2), BF16),
            shaped((width, hidden_width // 2), BF16),
            shaped((1, hidden_width), F32),
            shaped((hidden_width, half), BF16),
            shaped((hidden_width, half), BF16),
        ],
        in_specs=[
            SMEM,
            whole((rows, width)),
            whole((rows, width)),
            whole((rows, half)),
            whole((rows, half)),
            pl.BlockSpec((width, width), lambda i: (0, i)),
            pl.BlockSpec((1, width), lambda i: (0, i)),
            pl.BlockSpec((width, width), lambda i: (i, 0)),
        ],
        out_specs=[
            whole((rows, width)),
            whole((rows, width)),
            pl.BlockSpec((width, half), lambda i: (0, i)),
            pl.BlockSpec((width, half), lambda i: (0, i)),
            pl.BlockSpec((1, width), lambda i: (0, i)),
            pl.BlockSpec((width, half), lambda i: (i, 0)),
            pl.BlockSpec((width, half), lambda i: (i, 0)),
        ],
        compiler_params=params(),
        name="mlp",
    )(info, second, down_in, down_keep, down_send, up_weight, up_bias, down_weight)
    up_got = swap(up_send, "band", 1)
    down_got = swap(down_grad_send, "band", 1)

    out_patches, out_own, middle_grad, attended_grad, out_keep, out_send, vectors = pl.pallas_call(
        partial(middle_back_kernel, slots),
        out_shape=[
            shaped((slots, width), BF16),
            shaped((pad, width), F32),
            shaped((rows, width), F32),
            shaped((rows, width), F32),
            shaped((width, half), BF16),
            shaped((width, half), BF16),
            shaped((8, width), F32),
        ],
        in_specs=[SMEM] + [VMEM] * 11,
        out_specs=[VMEM] * 7,
        compiler_params=params(),
        name="middle_back",
    )(
        info,
        middle,
        branch,
        branch_two,
        second_grad,
        incoming,
        attended,
        out_weight,
        down_bias,
        second_scale,
        second_gain,
        first_scale,
    )

    shared = (out_patches, out_own, middle_grad, attended_grad, out_keep, out_send, vectors)
    halves = dict(up_keep=up_keep, up_got=up_got, down_keep=down_grad_keep, down_got=down_got)
    return shared + (down_bias_grad, up_bias_grad, halves)


def body(
    patches,
    specials,
    patch_mask,
    band_rows,
    mask_token,
    first_gain,
    first_shift,
    joint_weight,
    query_bias,
    value_bias,
    out_weight,
    out_bias,
    first_scale,
    second_gain,
    second_shift,
    up_weight,
    up_bias,
    down_weight,
    down_bias,
    second_scale,
    cot_patches,
    cot_specials,
):
    slots, width = patches.shape[1:]
    special_count = specials.shape[1]
    hidden_width = up_weight.shape[1]
    owned = -(-special_count // BANDS)
    rows = round_up(slots + owned, 16)
    pad = rows - slots
    info = band_rows
    mask = patch_mask
    patches, specials = patches[0], specials[0]
    cot_patches, cot_specials = cot_patches[0], cot_specials[0]
    shaped = jax.ShapeDtypeStruct

    forward = forward_fused if lax.axis_size("crop") == CROPS else forward_general
    tokens, queries, keys, values, attended, totals, weights, firsts_t = forward(
        info,
        mask,
        patches,
        specials,
        mask_token,
        first_gain,
        first_shift,
        joint_weight,
        query_bias,
        value_bias,
        rows,
    )

    middle = middle_fused if lax.axis_size("crop") == CROPS else middle_general
    (
        out_patches,
        out_own,
        middle_grad,
        attended_grad,
        out_keep,
        out_send,
        vectors,
        down_bias_grad,
        up_bias_grad,
        mlp_grads,
    ) = middle(
        info,
        attended,
        tokens,
        out_weight,
        out_bias,
        first_scale,
        second_gain,
        second_shift,
        second_scale,
        cot_patches,
        cot_specials,
        down_bias,
        up_weight,
        up_bias.reshape(1, -1),
        down_weight,
    )
    given = dict(
        info=info,
        weights=weights,
        queries=queries,
        keys=keys,
        values=values,
        attended=attended,
        totals=totals,
        attended_grad=attended_grad,
        mask=mask,
        first_gain=first_gain,
        vectors=vectors,
        down_bias_grad=down_bias_grad,
        up_bias_grad=up_bias_grad,
        out_own=out_own,
        mlp_grads=mlp_grads,
        out_keep=out_keep,
        out_send=out_send,
        firsts_t=firsts_t,
        joint_weight=joint_weight,
        tokens=tokens,
        middle_grad=middle_grad,
    )
    backward = backward_fused if lax.axis_size("crop") == CROPS else backward_general
    (
        grad_patches,
        up,
        down,
        out,
        joint,
        rows_of,
        up_bias_sum,
        out_specials,
        grad_specials,
    ) = backward(given, slots, special_count)
    return (
        out_patches[None],
        out_specials,
        grad_patches[None],
        grad_specials,
        rows_of[5],
        rows_of[6],
        rows_of[7],
        joint,
        rows_of[8],
        rows_of[9],
        out,
        rows_of[4],
        rows_of[3],
        rows_of[1],
        rows_of[2],
        up,
        up_bias_sum,
        down,
        rows_of[10],
        rows_of[0],
    )


def solution(mesh):
    split = P("crop", "band", None)
    special = P("crop", None, None)
    in_specs = (
        (split, special, P("crop", "band")) + (P(),) * 17 + (split, special)
    )
    line, matrix = P("crop"), P("crop", None)
    out_specs = (
        split,
        special,
        split,
        special,
        line,
        line,
        line,
        matrix,
        line,
        line,
        matrix,
        line,
        line,
        line,
        line,
        matrix,
        line,
        matrix,
        line,
        line,
    )
    return jax.shard_map(body, mesh=mesh, in_specs=in_specs, out_specs=out_specs, check_vma=False)
```
